32 devices in a mesh: dp: 4 (over y, x), fsdp: 8 (over z, core).
Axes of the slice: x: 2, y: 2, z: 4, core: 2. Of those that a mesh axis runs over, the one named last changes fastest.
Arguments:
- features: bfloat16 [1152, 49, 2048], P(('dp', 'fsdp')), may hold values from -16 to 16
- grid_size: int32 [1152], P(('dp', 'fsdp')), may hold values from 2 to 7, as said below
- w_reduce: bfloat16 [2, 2048, 512], P(None, 'fsdp'), may hold values from -0.125 to 0.125
- w_spatial: bfloat16 [2, 4608, 512], P(None, 'fsdp'), may hold values from -0.09375 to 0.09375
- w_expand: bfloat16 [2, 512, 2048], P(None, 'fsdp'), may hold values from -0.25 to 0.25
- gain_mid: float32 [2, 2, 512], replicated, may hold values from 0.25 to 1.75
- bias_mid: float32 [2, 2, 512], replicated, may hold values from -2.5 to 2.5
- gain_out: float32 [2, 2048], replicated, may hold values from 0.25 to 1.75
- bias_out: float32 [2, 2048], replicated, may hold values from -2.5 to 2.5
- head_a: bfloat16 [2048, 1000], P('fsdp'), may hold values from -0.5 to 0.5
- head_b: bfloat16 [2048, 365], P('fsdp'), may hold values from -0.5 to 0.5
- head_c: bfloat16 [2048, 40], P('fsdp'), may hold values from -0.5 to 0.5
- label_a: int32 [1152], P(('dp', 'fsdp')), may hold values from 0 to 999
- label_b: int32 [1152], P(('dp', 'fsdp')), may hold values from 0 to 364
- label_c: int32 [1152], P(('dp', 'fsdp')), may hold values from 0 to 39
- drop_bits: int32 [1152, 2048], P(('dp', 'fsdp')), may hold values from 0 to 32767
Outputs:
- trunk_out: bfloat16 [1152, 49, 2048], P(('dp', 'fsdp'))
- grad_features: float32 [1152, 49, 2048], P(('dp', 'fsdp'))
- grad_w_reduce: float32 [2, 2048, 512], P(None, 'fsdp')
- grad_w_spatial: float32 [2, 4608, 512], P(None, 'fsdp')
- grad_w_expand: float32 [2, 512, 2048], P(None, 'fsdp')
- grad_gain_mid: float32 [2, 2, 512], replicated
- grad_bias_mid: float32 [2, 2, 512], replicated
- grad_gain_out: float32 [2, 2048], replicated
- grad_bias_out: float32 [2, 2048], replicated
- grad_head_a: float32 [2048, 1000], P('fsdp')
- grad_head_b: float32 [2048, 365], P('fsdp')
- grad_head_c: float32 [2048, 40], P('fsdp')
The draws below stay inside these ranges and needn't reach their ends.
Inputs may be any that keep to these rules, and one draw needn't show every extreme that they name: `grid_size`: each image's grid side is 7 or 2, the same for the 4 images of an aligned group; both sides occur in every draw.
All inputs are finite; a program needn't handle non-finite values.
Results may differ from the reference program's by a relative error of at most 0.017.
Values may be sent and summed in bfloat16 or wider, within the bound.
No kernel may reach another device: no remote copies, remote signals or barrier semaphores. Data moves between devices by JAX's collectives and lax.ppermute only.
A program may use at most 448 MiB of HBM per device.

```python
import functools
import jax
import jax.numpy as jnp
from jax import lax

C = 2048
M = 512
CLS_A = 1000
CLS_B = 365
CLS_C = 40
SIDE = 7
BLOCKS = 2
GROUP = 4
IMAGES = 1152


def draw_features(key, part):
    key = jax.random.fold_in(key, 5)
    key_values = jax.random.fold_in(key, 1)
    key_scales = jax.random.fold_in(key, 2)
    groups = IMAGES // GROUP
    group_scale = jnp.exp(jax.random.uniform(key_scales, (groups,), jnp.float32, -1.15, 1.15))
    image_scale = jnp.repeat(group_scale, GROUP)
    values = jnp.clip(jax.random.normal(key_values, (IMAGES, SIDE * SIDE, C), jnp.float32), -5.0, 5.0)
    return (values * image_scale[:, None, None]).astype(jnp.bfloat16)


def draw_grid_size(key, part):
    key = jax.random.fold_in(key, 11)
    groups = IMAGES // GROUP
    larger_grid = jax.random.randint(key, (groups,), 0, 2)
    order = jnp.arange(groups, dtype=jnp.int32)
    larger_grid = jnp.where(order == 0, 1, jnp.where(order == 1, 0, larger_grid))
    return jnp.repeat(2 + (SIDE - 2) * larger_grid, GROUP).astype(jnp.int32)


def set_ends(result, own_key, least, high):
    shape = result.shape
    index_at = [jax.random.randint(jax.random.fold_in(own_key, axis), (), 0, shape[axis]) for axis in range(len(shape))]
    result = result.at[tuple(index_at)].set(least)
    longest = shape.index(max(shape))
    index_at[longest] = (index_at[longest] + 1) % shape[longest]
    return result.at[tuple(index_at)].set(high)


def level_of(key, extent, shards, low, largest):
    def one(position, shards_of):
        heights = jax.random.uniform(jax.random.fold_in(jax.random.fold_in(key, 6), position), (shards_of,), jnp.float32, low / len(shards), largest / len(shards))
        return jnp.repeat(jnp.exp(heights), extent[position] // shards_of).reshape((-1,) + (1,) * (len(extent) - position - 1))

    loudness = one(*shards[0])
    for cut in shards[1:]:
        loudness = loudness * one(*cut)
    return loudness


def noise(stream_key, dims, width, most, pieces=(), kind=jnp.bfloat16):
    level = level_of(stream_key, dims, pieces, -0.22, 0.18) if pieces else 1.0
    entries = jax.random.normal(stream_key, dims, jnp.float32) * width * level
    return jnp.minimum(jnp.maximum(entries, -most), most).astype(kind)


def setup_inputs(seed: int = 0) -> dict:
    seeds = jax.random.split(jax.random.key(seed), 17)
    return {
        "features": draw_features(jax.random.fold_in(seeds[16], 71), 0),
        "grid_size": draw_grid_size(jax.random.fold_in(seeds[16], 71), 0),
        "w_reduce": noise(seeds[2], (BLOCKS, C, M), C ** -0.5, 0.125, ((1, 8),)),
        "w_spatial": noise(seeds[3], (BLOCKS, 9 * M, M), (9 * M) ** -0.5, 0.09375, ((1, 8),)),
        "w_expand": noise(seeds[4], (BLOCKS, M, C), M ** -0.5, 0.25, ((1, 8),)),
        "gain_mid": jnp.clip(1.0 + 0.15 * jax.random.normal(seeds[5], (BLOCKS, 2, M), jnp.float32), 0.25, 1.75),
        "bias_mid": noise(seeds[6], (BLOCKS, 2, M), 0.5, 2.5, (), jnp.float32),
        "gain_out": jnp.clip(1.0 + 0.15 * jax.random.normal(seeds[7], (BLOCKS, C), jnp.float32), 0.25, 1.75),
        "bias_out": noise(seeds[8], (BLOCKS, C), 0.5, 2.5, (), jnp.float32),
        "head_a": noise(seeds[9], (C, CLS_A), (C // 16) ** -0.5, 0.5, ((0, 8),)),
        "head_b": noise(seeds[10], (C, CLS_B), (C // 16) ** -0.5, 0.5, ((0, 8),)),
        "head_c": noise(seeds[11], (C, CLS_C), (C // 16) ** -0.5, 0.5, ((0, 8),)),
        "label_a": set_ends(jax.random.randint(seeds[12], (IMAGES,), 0, CLS_A), jax.random.fold_in(seeds[12], 1), 0, CLS_A - 1).astype(jnp.int32),
        "label_b": set_ends(jax.random.randint(seeds[13], (IMAGES,), 0, CLS_B), jax.random.fold_in(seeds[13], 1), 0, CLS_B - 1).astype(jnp.int32),
        "label_c": set_ends(jax.random.randint(seeds[14], (IMAGES,), 0, CLS_C), jax.random.fold_in(seeds[14], 1), 0, CLS_C - 1).astype(jnp.int32),
        "drop_bits": set_ends(jax.random.randint(seeds[15], (IMAGES, C), 0, 32768), jax.random.fold_in(seeds[15], 1), 0, 32767).astype(jnp.int32),
    }


@jax.custom_vjp
def low(v):
    return lax.optimization_barrier(v.astype(jnp.bfloat16)).astype(jnp.float32)

@jax.custom_vjp
def low_back(v):
    return v

def low_keep(v):
    return (low(v), None)

def low_pass(kept, grad):
    return (grad,)

def back_keep(v):
    return (v, None)

def back_low(kept, grad):
    return (low(grad),)
low.defvjp(low_keep, low_pass)
low_back.defvjp(back_keep, back_low)
norm_eps = 1e-05
abs_floor = 0.05
drop_width = 0.1
loss_scale = 256.0

def pixel_masks(grid_size):
    cells = jnp.arange(SIDE * SIDE, dtype=jnp.int32)
    grid_rows = cells // SIDE
    grid_cols = cells % SIDE
    bound = grid_size[:, None]
    inside = (grid_rows[None, :] < bound) & (grid_cols[None, :] < bound)
    return jnp.where(inside, 1.0, 0.0).astype(jnp.float32)

def product(left, right):
    return jnp.dot(left, right, precision=lax.Precision.HIGHEST, preferred_element_type=jnp.float32)

def patches(values):
    images = values.shape[0] // (SIDE * SIDE)
    channels = values.shape[1]
    grid = values.reshape(images, SIDE, SIDE, channels)
    padded = jnp.pad(grid, ((0, 0), (1, 1), (1, 1), (0, 0)))
    taps = [padded[:, row_off:row_off + SIDE, col_off:col_off + SIDE, :] for row_off in range(3) for col_off in range(3)]
    return jnp.concatenate(taps, axis=-1).reshape(images * SIDE * SIDE, 9 * channels)

@jax.checkpoint
def spatial_conv(values, weight):
    return product(patches(values), weight)

def batch_norm(hidden, pixel_rows, live_count, gain, shift):
    center = lax.optimization_barrier(jnp.sum(hidden * pixel_rows, axis=0)) / live_count
    offset = hidden - center
    spread = lax.optimization_barrier(jnp.sum(pixel_rows * offset * offset, axis=0)) / live_count
    return offset * lax.rsqrt(spread + norm_eps) * gain + shift

def bottleneck(inputs, pixel_rows, live_count, w_one, w_two, w_three, gain_pair, bias_pair, gain_last, bias_last):
    hidden_one = low_back(product(inputs, w_one))
    act_one = low(pixel_rows * jax.nn.silu(batch_norm(hidden_one, pixel_rows, live_count, gain_pair[0], bias_pair[0])))
    hidden_two = low_back(spatial_conv(act_one, w_two))
    act_two = low(pixel_rows * jax.nn.silu(batch_norm(hidden_two, pixel_rows, live_count, gain_pair[1], bias_pair[1])))
    hidden_three = low_back(product(act_two, w_three))
    pre_out = batch_norm(hidden_three, pixel_rows, live_count, gain_last, bias_last) + inputs
    return pixel_rows * jax.nn.silu(pre_out)

def trunk(inputs, w_reduce, w_spatial, w_expand, gain_mid, bias_mid, gain_out, bias_out, pixel_rows, live_count):
    current = inputs
    for block_index in range(BLOCKS):
        current = low(bottleneck(current, pixel_rows, live_count, w_reduce[block_index], w_spatial[block_index], w_expand[block_index], gain_mid[block_index], bias_mid[block_index], gain_out[block_index], bias_out[block_index]))
    return current

def task_loss(pooled_raw, weight, labels):
    logits = low_back(product(low(pooled_raw), weight))
    classes = jnp.arange(weight.shape[1], dtype=jnp.int32)
    picked = lax.optimization_barrier(jnp.sum(jnp.where(classes[None, :] == labels[:, None], logits, 0.0), axis=1))
    row_max = lax.optimization_barrier(jnp.max(logits, axis=1, keepdims=True))
    log_total = row_max[:, 0] + jnp.log(lax.optimization_barrier(jnp.sum(jnp.exp(logits - row_max), axis=1)))
    return loss_scale * jnp.sum(log_total - picked)

def grad_drop(task_grads, drop_bits):
    summed = task_grads[0] + task_grads[1] + task_grads[2]
    magnitude = sum([jnp.sqrt(single * single + abs_floor * abs_floor) for single in task_grads])
    purity = 0.5 * (1.0 + summed / magnitude)
    level = (drop_bits.astype(jnp.float32) + 0.5) / 32768.0
    keep_share = jax.nn.sigmoid((purity - level) / drop_width)
    return 0.5 * summed + (keep_share - 0.5) * magnitude

def reference(features, grid_size, w_reduce, w_spatial, w_expand, gain_mid, bias_mid, gain_out, bias_out, head_a, head_b, head_c, label_a, label_b, label_c, drop_bits):
    pixel_mask = pixel_masks(grid_size)
    pixel_area = (grid_size * grid_size).astype(jnp.float32)
    live_count = jnp.sum(pixel_area)
    pixel_rows = pixel_mask.reshape(-1, 1)
    inputs = (features.astype(jnp.float32) * pixel_mask[:, :, None]).reshape(-1, C)
    params = tuple((array.astype(jnp.float32) for array in (w_reduce, w_spatial, w_expand, gain_mid, bias_mid, gain_out, bias_out)))
    trunk_run = functools.partial(trunk, pixel_rows=pixel_rows, live_count=live_count)
    outputs, pull_trunk = jax.vjp(trunk_run, inputs, *params)
    grid_out = outputs.reshape(-1, SIDE * SIDE, C)
    pooled_raw = lax.optimization_barrier(jnp.sum(grid_out * pixel_mask[:, :, None], axis=1)) / pixel_area[:, None]
    task_grads = []
    head_grads = []
    for weight, labels in ((head_a, label_a), (head_b, label_b), (head_c, label_c)):
        task_value = functools.partial(task_loss, labels=labels)
        value_out, pull_head = jax.vjp(task_value, pooled_raw, weight.astype(jnp.float32))
        grad_pooled, grad_weight = pull_head(jnp.ones((), jnp.float32))
        task_grads.append(grad_pooled / pixel_area[:, None])
        head_grads.append(grad_weight / loss_scale)
    merged = grad_drop(task_grads, drop_bits)
    grad_trunk = (pixel_mask[:, :, None] * merged[:, None, :]).reshape(-1, C)
    pulled = pull_trunk(grad_trunk)
    grad_features = pulled[0].reshape(-1, SIDE * SIDE, C) * pixel_mask[:, :, None]
    return (grid_out.astype(jnp.bfloat16), grad_features, pulled[1] / loss_scale, pulled[2] / loss_scale, pulled[3] / loss_scale, pulled[4] / loss_scale, pulled[5] / loss_scale, pulled[6] / loss_scale, pulled[7] / loss_scale, head_grads[0], head_grads[1], head_grads[2])
```

```python
import functools

import jax
import jax.numpy as jnp
from jax import lax
from jax.experimental import pallas as pl
from jax.experimental.pallas import tpu as pltpu
from jax.sharding import PartitionSpec as P

SIDE = 7
TAPS = 3
EPS = 1e-05
FLOOR = 0.05
WIDTH = 0.1
SCALE = 256.0
BF = jnp.bfloat16
F32 = jnp.float32
VMEM_LIMIT = 56 * 1024 * 1024
AXES = ("dp", "fsdp")


def nn(left, right):
    return jnp.dot(left, right, preferred_element_type=F32)


def nt(left, right):
    return lax.dot_general(left, right, (((1,), (1,)), ((), ())), preferred_element_type=F32)


def tn(left, right):
    return lax.dot_general(left, right, (((0,), (0,)), ((), ())), preferred_element_type=F32)


def sigmoid(v):
    return 0.5 * jnp.tanh(0.5 * v) + 0.5


def slope(v):
    s = sigmoid(v)
    return s * (1.0 + v * (1.0 - s))


def rowsum(v):
    return jnp.sum(v, axis=0, keepdims=True)


def params(n_grid):
    return pltpu.CompilerParams(
        dimension_semantics=("arbitrary",) * n_grid, vmem_limit_bytes=VMEM_LIMIT
    )


def whole(shape):
    zeros = (0,) * len(shape)
    return pl.BlockSpec(shape, lambda *g: zeros)


def tile(rows, cols):
    return pl.BlockSpec((rows, cols), lambda j: (j, 0))


def sds(shape, dtype):
    return jax.ShapeDtypeStruct(shape, dtype)


def cost(flops, nbytes, trans=0):
    return pl.CostEstimate(flops=int(flops), bytes_accessed=int(nbytes), transcendentals=int(trans))


def forward_consts(tot, inv, gb):
    mu = tot[0:1, :] * inv
    var = jnp.maximum(tot[1:2, :] * inv - mu * mu, 0.0)
    rstd = lax.rsqrt(var + EPS)
    a = rstd * gb[0:1, :]
    return mu, rstd, a, gb[1:2, :] - mu * a


def backward_consts(mu, rstd, a, btot, inv):
    ex = btot[1:2, :] * rstd * inv
    c1 = -a * rstd * ex
    c0 = -a * btot[0:1, :] * inv - c1 * mu
    return c1, c0


def add_stats(st, first, top, low, cols=slice(None)):
    @pl.when(first)
    def _():
        st[0:1, cols] = top
        st[1:2, cols] = low

    @pl.when(jnp.logical_not(first))
    def _():
        st[0:1, cols] += top
        st[1:2, cols] += low


class Shape:
    def __init__(self, images):
        self.images = images
        self.main = images // 16 * 16
        self.rest = images - self.main
        self.top = SIDE * self.main
        self.low = (SIDE + 1) * self.rest
        self.rows = self.top + self.low
        self.total = SIDE * self.rows
        self.padded = self.main + 16


def prep_kernel(sh, f, mask, x, scr):
    channels = x.shape[1]
    scr[...] = jnp.zeros_like(scr)
    for s in range(SIDE):
        x[s * sh.main : (s + 1) * sh.main, :] = (
            f[s, 0 : sh.main, :].astype(F32) * mask[s * sh.main : (s + 1) * sh.main, :]
        ).astype(BF)
        scr[s * sh.rest : (s + 1) * sh.rest, :] = f[s, sh.main : sh.images, :].astype(F32)
    x[sh.top : sh.rows, :] = jnp.where(mask[sh.top : sh.rows, :] > 0.0, scr[...], 0.0).astype(BF)


def prep(sh, features, mask):
    channels = features.shape[2]
    return pl.pallas_call(
        functools.partial(prep_kernel, sh),
        grid=(SIDE,),
        in_specs=[
            pl.BlockSpec((SIDE, sh.images, channels), lambda j: (j, 0, 0)),
            tile(sh.rows, 1),
        ],
        out_specs=tile(sh.rows, channels),
        out_shape=sds((sh.total, channels), BF),
        scratch_shapes=[pltpu.VMEM((sh.low, channels), F32)],
        compiler_params=params(1),
        name="prep",
    )(features, mask)


def reduce_kernel(x, w, h, st):
    acc = nn(x[...], w[...])
    h[...] = acc
    add_stats(st, pl.program_id(0) == 0, rowsum(acc), rowsum(acc * acc))


def reduce_conv(sh, x, w):
    c, m = w.shape
    return pl.pallas_call(
        reduce_kernel,
        grid=(SIDE,),
        in_specs=[tile(sh.rows, c), whole((c, m))],
        out_specs=[tile(sh.rows, m), whole((2, m))],
        out_shape=[sds((sh.total, m), F32), sds((2, m), F32)],
        compiler_params=params(1),
        cost_estimate=cost(2 * sh.total * c * m, 2 * sh.total * c + 4 * sh.total * m),
        name="reduce_conv",
    )(x, w)


def shifted(sh, v, scr):
    m = v.shape[1]
    gap = jnp.zeros((sh.main, m), F32)
    scr[8 : 8 + sh.low, :] = v[sh.top :, :]
    before = jnp.concatenate([gap, v[: sh.top - sh.main, :], scr[8 - sh.rest : 8 - sh.rest + sh.low, :]], axis=0)
    after = jnp.concatenate([v[sh.main : sh.top, :], gap, scr[8 + sh.rest : 8 + sh.rest + sh.low, :]], axis=0)
    return before, v, after


def put_shifted(sh, v, scr, pat, row):
    m = v.shape[1]
    at = pl.ds(pl.multiple_of(row * sh.rows, sh.rows), sh.rows)
    for k, part in enumerate(shifted(sh, v, scr)):
        pat[at, k * m : (k + 1) * m] = part.astype(BF)


def spatial_kernel(sh, inv, h1, tot, gb, mask, mask_out, w, act, h2, st, pat, scr):
    j = pl.program_id(0)
    m = h1.shape[1]

    @pl.when(j == 0)
    def _():
        pat[...] = jnp.zeros_like(pat)
        scr[...] = jnp.zeros_like(scr)

    mu, rstd, a, b = forward_consts(tot, inv[0, 0], gb)
    acc = None
    for k in range(2):
        at = pl.ds(pl.multiple_of((j + k) * sh.rows, sh.rows), sh.rows)
        part = nn(pat[at, :], w[k * TAPS * m : (k + 1) * TAPS * m, :])
        acc = part if acc is None else acc + part
    live = jnp.where(j < SIDE, mask[...], 0.0)
    v = h1[...] * a + b
    y = live * (v * sigmoid(v))

    @pl.when(j < SIDE)
    def _():
        act[...] = y.astype(BF)

    put_shifted(sh, y, scr, pat, j + 2)
    at = pl.ds(pl.multiple_of((j + 2) * sh.rows, sh.rows), sh.rows)
    acc = acc + nn(pat[at, :], w[2 * TAPS * m :, :])
    h2[...] = acc
    got = jnp.where(j > 0, mask_out[...], 0.0) * acc
    add_stats(st, j == 0, rowsum(got), rowsum(got * acc))


def spatial_conv(sh, h1, tot, inv, gb, mask, w):
    m = h1.shape[1]
    into = lambda j: (jnp.minimum(j, SIDE - 1), 0)
    outof = lambda j: (jnp.maximum(j - 1, 0), 0)
    return pl.pallas_call(
        functools.partial(spatial_kernel, sh),
        grid=(SIDE + 1,),
        in_specs=[
            pl.BlockSpec(memory_space=pltpu.SMEM),
            pl.BlockSpec((sh.rows, m), into),
            whole((2, m)),
            whole((2, m)),
            pl.BlockSpec((sh.rows, 1), into),
            pl.BlockSpec((sh.rows, 1), outof),
            whole(w.shape),
        ],
        out_specs=[
            pl.BlockSpec((sh.rows, m), into),
            pl.BlockSpec((sh.rows, m), outof),
            whole((2, m)),
        ],
        out_shape=[sds((sh.total, m), BF), sds((sh.total, m), F32), sds((2, m), F32)],
        scratch_shapes=[
            pltpu.VMEM(((SIDE + 3) * sh.rows, TAPS * m), BF),
            pltpu.VMEM((sh.low + 16, m), F32),
        ],
        compiler_params=params(1),
        cost_estimate=cost(2 * sh.total * w.size, 2 * w.size + 10 * sh.total * m),
        name="spatial_conv",
    )(inv, h1, tot, gb, mask, mask, w)


def expand_kernel(inv, h2, tot, gb, mask, w, act, h3, st):
    first = pl.program_id(0) == 0
    mu, rstd, a, b = forward_consts(tot, inv[0, 0], gb)
    v = h2[...] * a + b
    y = (mask[...] * (v * sigmoid(v))).astype(BF)
    act[...] = y
    step = 512
    for c in range(0, w.shape[1], step):
        cols = slice(c, c + step)
        acc = nn(y, w[:, cols])
        h3[:, cols] = acc.astype(BF)
        add_stats(st, first, rowsum(acc), rowsum(acc * acc), cols)


def expand_conv(sh, h2, tot, inv, gb, mask, w):
    m, c = w.shape
    return pl.pallas_call(
        expand_kernel,
        grid=(SIDE,),
        in_specs=[
            pl.BlockSpec(memory_space=pltpu.SMEM),
            tile(sh.rows, m),
            whole((2, m)),
            whole((2, m)),
            tile(sh.rows, 1),
            whole((m, c)),
        ],
        out_specs=[tile(sh.rows, m), tile(sh.rows, c), whole((2, c))],
        out_shape=[sds((sh.total, m), BF), sds((sh.total, c), BF), sds((2, c), F32)],
        compiler_params=params(1),
        cost_estimate=cost(2 * sh.total * c * m, 2 * sh.total * c + 6 * sh.total * m),
        name="expand_conv",
    )(inv, h2, tot, gb, mask, w)


def join_kernel(inv, h3, x, tot, gb, mask, w, y, h1, st):
    mu, rstd, a, b = forward_consts(tot, inv[0, 0], gb)
    step = 512
    acc = None
    for c in range(0, x.shape[1], step):
        cols = slice(c, c + step)
        v = h3[:, cols].astype(F32) * a[:, cols] + b[:, cols] + x[:, cols].astype(F32)
        out = (mask[...] * (v * sigmoid(v))).astype(BF)
        y[:, cols] = out
        part = nn(out, w[cols, :])
        acc = part if acc is None else acc + part
    h1[...] = acc
    add_stats(st, pl.program_id(0) == 0, rowsum(acc), rowsum(acc * acc))


def join(sh, h3, x, tot, inv, gb, mask, w):
    c, m = w.shape
    return pl.pallas_call(
        join_kernel,
        grid=(SIDE,),
        in_specs=[
            pl.BlockSpec(memory_space=pltpu.SMEM),
            tile(sh.rows, c),
            tile(sh.rows, c),
            whole((2, c)),
            whole((2, c)),
            tile(sh.rows, 1),
            whole((c, m)),
        ],
        out_specs=[tile(sh.rows, c), tile(sh.rows, m), whole((2, m))],
        out_shape=[sds((sh.total, c), BF), sds((sh.total, m), F32), sds((2, m), F32)],
        compiler_params=params(1),
        cost_estimate=cost(2 * sh.total * c * m, 6 * sh.total * c + 4 * sh.total * m),
        name="join",
    )(inv, h3, x, tot, gb, mask, w)


def last_kernel(sh, inv, h3, x, tot, gb, mask, area, pick, trunk, pooled, sums, scr):
    j = pl.program_id(0)
    mu, rstd, a, b = forward_consts(tot, inv[0, 0], gb)
    step = 512
    for c in range(0, x.shape[1], step):
        cols = slice(c, c + step)
        v = h3[:, cols].astype(F32) * a[:, cols] + b[:, cols] + x[:, cols].astype(F32)
        out = mask[...] * (v * sigmoid(v))
        low = out.astype(BF)
        scr[:, cols] = out[sh.top :, :]
        for s in range(SIDE):
            trunk[s, 0 : sh.main, cols] = low[s * sh.main : (s + 1) * sh.main, :]
            trunk[s, sh.main : sh.images, cols] = scr[s * sh.rest : (s + 1) * sh.rest, cols].astype(BF)
        part = nn(pick[...], low)

        @pl.when(j == 0)
        def _():
            sums[:, cols] = part

        @pl.when(j > 0)
        def _():
            sums[:, cols] += part

    @pl.when(j == SIDE - 1)
    def _():
        pooled[...] = (sums[...] / area[...]).astype(BF)


def last_join(sh, h3, x, tot, inv, gb, mask, area, pick):
    c = x.shape[1]
    return pl.pallas_call(
        functools.partial(last_kernel, sh),
        grid=(SIDE,),
        in_specs=[
            pl.BlockSpec(memory_space=pltpu.SMEM),
            tile(sh.rows, c),
            tile(sh.rows, c),
            whole((2, c)),
            whole((2, c)),
            tile(sh.rows, 1),
            whole((sh.padded, 1)),
            whole((sh.padded, sh.rows)),
        ],
        out_specs=[
            pl.BlockSpec((SIDE, sh.images, c), lambda j: (j, 0, 0)),
            whole((sh.padded, c)),
        ],
        out_shape=[sds((SIDE * SIDE, sh.images, c), BF), sds((sh.padded, c), BF)],
        scratch_shapes=[pltpu.VMEM((sh.padded, c), F32), pltpu.VMEM((sh.low, c), F32)],
        compiler_params=params(1),
        cost_estimate=cost(2 * sh.padded * sh.total * c, 6 * sh.total * c),
        name="last_join",
    )(inv, h3, x, tot, gb, mask, area, pick)


def heads_kernel(sizes, offsets, pooled, labels, area, bits, w, merged, out):
    rows = pooled.shape[0]
    out[...] = jnp.zeros_like(out)
    summed = None
    at = 0
    for t, (classes, place) in enumerate(zip(sizes, offsets)):
        span = -(-classes // 16) * 16
        wt = w[at : at + span, :]
        at += span
        logits = nt(pooled[...], wt)
        index = lax.broadcasted_iota(jnp.int32, (rows, span), 1)
        inside = index < classes
        logits = jnp.where(inside, logits, -1e30)
        top = jnp.max(logits, axis=1, keepdims=True)
        ex = jnp.where(inside, jnp.exp(logits - top), 0.0)
        probs = ex / jnp.sum(ex, axis=1, keepdims=True)
        targets = jnp.where(index == labels[:, t : t + 1], 1.0, 0.0)
        grad = (SCALE * (probs - targets)).astype(BF)
        out[:, place : place + span] = grad
        single = nn(grad, wt) / area[...]
        size = jnp.sqrt(single * single + FLOOR * FLOOR)
        summed = single if summed is None else summed + single
        magnitude = size if t == 0 else magnitude + size
    purity = 0.5 * (1.0 + summed / magnitude)
    level = (bits[...].astype(F32) + 0.5) / 32768.0
    keep = sigmoid((purity - level) / WIDTH)
    merged[...] = 0.5 * summed + (keep - 0.5) * magnitude


def heads(pooled, labels, area, bits, w, sizes, offsets, span):
    rows, c = pooled.shape
    return pl.pallas_call(
        functools.partial(heads_kernel, sizes, offsets),
        out_shape=[sds((rows, c), F32), sds((rows, span), BF)],
        compiler_params=pltpu.CompilerParams(vmem_limit_bytes=VMEM_LIMIT),
        cost_estimate=cost(4 * rows * c * span, 2 * w.size),
        name="heads",
    )(pooled, labels, area, bits, w)


def top_grad_kernel(sh, inv, merged, h3, x, tot, gb, mask, e3, st, scr):
    j = pl.program_id(0)
    mu, rstd, a, b = forward_consts(tot, inv[0, 0], gb)

    @pl.when(j == 0)
    def _():
        for s in range(SIDE + 1):
            scr[s * sh.rest : (s + 1) * sh.rest, :] = merged[sh.main : sh.images, :]

    step = 256
    for c in range(0, x.shape[1], step):
        cols = slice(c, c + step)
        h = h3[:, cols].astype(F32)
        v = h * a[:, cols] + b[:, cols] + x[:, cols].astype(F32)
        up = jnp.concatenate([merged[0 : sh.main, cols]] * SIDE + [scr[:, cols]], axis=0)
        e = mask[...] * up * slope(v)
        e3[:, cols] = e.astype(BF)
        add_stats(st, j == 0, rowsum(e), rowsum(e * (h - mu[:, cols])), cols)


def top_grad(sh, merged, h3, x, tot, inv, gb, mask):
    c = x.shape[1]
    return pl.pallas_call(
        functools.partial(top_grad_kernel, sh),
        grid=(SIDE,),
        in_specs=[
            pl.BlockSpec(memory_space=pltpu.SMEM),
            whole(merged.shape),
            tile(sh.rows, c),
            tile(sh.rows, c),
            whole((2, c)),
            whole((2, c)),
            tile(sh.rows, 1),
        ],
        out_specs=[tile(sh.rows, c), whole((2, c))],
        out_shape=[sds((sh.total, c), BF), sds((2, c), F32)],
        scratch_shapes=[pltpu.VMEM((sh.low, c), F32)],
        compiler_params=params(1),
        cost_estimate=cost(20 * sh.total * c, 6 * sh.total * c),
        name="top_grad",
    )(inv, merged, h3, x, tot, gb, mask)


def expand_back_kernel(inv, e3, h3, tot3, gb3, btot3, mask, w, h2, tot2, gb2, g3, e2, st):
    mu, rstd, a, b = forward_consts(tot3, inv[0, 0], gb3)
    c1, c0 = backward_consts(mu, rstd, a, btot3, inv[0, 0])
    step = 512
    acc = None
    for c in range(0, e3.shape[1], step):
        cols = slice(c, c + step)
        g = a[:, cols] * e3[:, cols].astype(F32) + c1[:, cols] * h3[:, cols].astype(F32) + c0[:, cols]
        g = (mask[...] * g).astype(BF)
        g3[:, cols] = g
        part = nt(g, w[:, cols])
        acc = part if acc is None else acc + part
    mu, rstd, a, b = forward_consts(tot2, inv[0, 0], gb2)
    h = h2[...]
    e = mask[...] * acc * slope(h * a + b)
    e2[...] = e
    add_stats(st, pl.program_id(0) == 0, rowsum(e), rowsum(e * (h - mu)))


def expand_back(sh, e3, h3, tot3, gb3, btot3, inv, mask, w, h2, tot2, gb2):
    m, c = w.shape
    return pl.pallas_call(
        expand_back_kernel,
        grid=(SIDE,),
        in_specs=[
            pl.BlockSpec(memory_space=pltpu.SMEM),
            tile(sh.rows, c),
            tile(sh.rows, c),
            whole((2, c)),
            whole((2, c)),
            whole((2, c)),
            tile(sh.rows, 1),
            whole((m, c)),
            tile(sh.rows, m),
            whole((2, m)),
            whole((2, m)),
        ],
        out_specs=[tile(sh.rows, c), tile(sh.rows, m), whole((2, m))],
        out_shape=[sds((sh.total, c), BF), sds((sh.total, m), F32), sds((2, m), F32)],
        compiler_params=params(1),
        cost_estimate=cost(2 * sh.total * c * m, 6 * sh.total * c + 8 * sh.total * m),
        name="expand_back",
    )(inv, e3, h3, tot3, gb3, btot3, mask, w, h2, tot2, gb2)


def spatial_back_kernel(
    sh, inv, e2, h2, tot2, gb2, btot2, mask, mask_out, w, h1, tot1, gb1, g2, e1, st, pat, scr
):
    j = pl.program_id(0)
    m = e2.shape[1]

    @pl.when(j == 0)
    def _():
        pat[...] = jnp.zeros_like(pat)
        scr[...] = jnp.zeros_like(scr)

    def taps(k):
        at = pl.ds(pl.multiple_of((j + k) * sh.rows, sh.rows), sh.rows)
        total = None
        for l in range(TAPS):
            tap = TAPS * (2 - k) + (2 - l)
            part = nt(pat[at, l * m : (l + 1) * m], w[tap * m : (tap + 1) * m, :])
            total = part if total is None else total + part
        return total

    acc = taps(0) + taps(1)
    mu, rstd, a, b = forward_consts(tot2, inv[0, 0], gb2)
    c1, c0 = backward_consts(mu, rstd, a, btot2, inv[0, 0])
    live = jnp.where(j < SIDE, mask[...], 0.0)
    g = live * (a * e2[...] + c1 * h2[...] + c0)

    @pl.when(j < SIDE)
    def _():
        g2[...] = g.astype(BF)

    put_shifted(sh, g, scr, pat, j + 2)
    acc = acc + taps(2)
    mu, rstd, a, b = forward_consts(tot1, inv[0, 0], gb1)
    h = h1[...]
    e = jnp.where(j > 0, mask_out[...], 0.0) * acc * slope(h * a + b)
    e1[...] = e
    add_stats(st, j == 0, rowsum(e), rowsum(e * (h - mu)))


def spatial_back(sh, e2, h2, tot2, gb2, btot2, inv, mask, w, h1, tot1, gb1):
    m = e2.shape[1]
    into = lambda j: (jnp.minimum(j, SIDE - 1), 0)
    outof = lambda j: (jnp.maximum(j - 1, 0), 0)
    return pl.pallas_call(
        functools.partial(spatial_back_kernel, sh),
        grid=(SIDE + 1,),
        in_specs=[
            pl.BlockSpec(memory_space=pltpu.SMEM),
            pl.BlockSpec((sh.rows, m), into),
            pl.BlockSpec((sh.rows, m), into),
            whole((2, m)),
            whole((2, m)),
            whole((2, m)),
            pl.BlockSpec((sh.rows, 1), into),
            pl.BlockSpec((sh.rows, 1), outof),
            whole(w.shape),
            pl.BlockSpec((sh.rows, m), outof),
            whole((2, m)),
            whole((2, m)),
        ],
        out_specs=[
            pl.BlockSpec((sh.rows, m), into),
            pl.BlockSpec((sh.rows, m), outof),
            whole((2, m)),
        ],
        out_shape=[sds((sh.total, m), BF), sds((sh.total, m), F32), sds((2, m), F32)],
        scratch_shapes=[
            pltpu.VMEM(((SIDE + 3) * sh.rows, TAPS * m), BF),
            pltpu.VMEM((sh.low + 16, m), F32),
        ],
        compiler_params=params(1),
        cost_estimate=cost(2 * sh.total * w.size, 2 * w.size + 18 * sh.total * m),
        name="spatial_back",
    )(inv, e2, h2, tot2, gb2, btot2, mask, mask, w, h1, tot1, gb1)


def reduce_back_kernel(
    inv, e1, h1, tot1, gb1, btot1, mask, w, e3, h3, x, tot3, gb3, g1, down, st
):
    mu, rstd, a, b = forward_consts(tot1, inv[0, 0], gb1)
    c1, c0 = backward_consts(mu, rstd, a, btot1, inv[0, 0])
    g = (mask[...] * (a * e1[...] + c1 * h1[...] + c0)).astype(BF)
    g1[...] = g
    mu, rstd, a, b = forward_consts(tot3, inv[0, 0], gb3)
    first = pl.program_id(0) == 0
    step = 256
    for c in range(0, x.shape[1], step):
        cols = slice(c, c + step)
        up = nt(g, w[cols, :]) + e3[:, cols].astype(F32)
        h = h3[:, cols].astype(F32)
        v = h * a[:, cols] + b[:, cols] + x[:, cols].astype(F32)
        e = mask[...] * up * slope(v)
        down[:, cols] = e.astype(BF)
        add_stats(st, first, rowsum(e), rowsum(e * (h - mu[:, cols])), cols)


def reduce_back(sh, e1, h1, tot1, gb1, btot1, inv, mask, w, e3, h3, x, tot3, gb3):
    c, m = w.shape
    return pl.pallas_call(
        reduce_back_kernel,
        grid=(SIDE,),
        in_specs=[
            pl.BlockSpec(memory_space=pltpu.SMEM),
            tile(sh.rows, m),
            tile(sh.rows, m),
            whole((2, m)),
            whole((2, m)),
            whole((2, m)),
            tile(sh.rows, 1),
            whole((c, m)),
            tile(sh.rows, c),
            tile(sh.rows, c),
            tile(sh.rows, c),
            whole((2, c)),
            whole((2, c)),
        ],
        out_specs=[tile(sh.rows, m), tile(sh.rows, c), whole((2, c))],
        out_shape=[sds((sh.total, m), BF), sds((sh.total, c), BF), sds((2, c), F32)],
        compiler_params=params(1),
        cost_estimate=cost(2 * sh.total * c * m, 8 * sh.total * c + 10 * sh.total * m),
        name="reduce_back",
    )(inv, e1, h1, tot1, gb1, btot1, mask, w, e3, h3, x, tot3, gb3)


def features_back_kernel(sh, inv, e1, h1, tot1, gb1, btot1, mask, w, e3, g1, out, scr):
    mu, rstd, a, b = forward_consts(tot1, inv[0, 0], gb1)
    c1, c0 = backward_consts(mu, rstd, a, btot1, inv[0, 0])
    g = (mask[...] * (a * e1[...] + c1 * h1[...] + c0)).astype(BF)
    g1[...] = g
    step = 512
    for c in range(0, w.shape[0], step):
        cols = slice(c, c + step)
        up = mask[...] * (nt(g, w[cols, :]) + e3[:, cols].astype(F32))
        scr[:, cols] = up[sh.top :, :]
        for s in range(SIDE):
            out[s, 0 : sh.main, cols] = up[s * sh.main : (s + 1) * sh.main, :]
            out[s, sh.main : sh.images, cols] = scr[s * sh.rest : (s + 1) * sh.rest, cols]


def features_back(sh, e1, h1, tot1, gb1, btot1, inv, mask, w, e3):
    c, m = w.shape
    return pl.pallas_call(
        functools.partial(features_back_kernel, sh),
        grid=(SIDE,),
        in_specs=[
            pl.BlockSpec(memory_space=pltpu.SMEM),
            tile(sh.rows, m),
            tile(sh.rows, m),
            whole((2, m)),
            whole((2, m)),
            whole((2, m)),
            tile(sh.rows, 1),
            whole((c, m)),
            tile(sh.rows, c),
        ],
        out_specs=[tile(sh.rows, m), pl.BlockSpec((SIDE, sh.images, c), lambda j: (j, 0, 0))],
        out_shape=[sds((sh.total, m), BF), sds((SIDE * SIDE, sh.images, c), F32)],
        scratch_shapes=[pltpu.VMEM((sh.low, c), F32)],
        compiler_params=params(1),
        cost_estimate=cost(2 * sh.total * c * m, 6 * sh.total * c + 10 * sh.total * m),
        name="features_back",
    )(inv, e1, h1, tot1, gb1, btot1, mask, w, e3)


def wgrad_kernel(left, right, out):
    out[...] = tn(left[...], right[...]).astype(BF)


def wgrad(left, right, step):
    rows, a = left.shape
    b = right.shape[1]
    by_left = a >= b
    if by_left:
        specs = [pl.BlockSpec((rows, step), lambda j: (0, j)), whole((rows, b))]
        out_spec = pl.BlockSpec((step, b), lambda j: (j, 0))
    else:
        specs = [whole((rows, a)), pl.BlockSpec((rows, step), lambda j: (0, j))]
        out_spec = pl.BlockSpec((a, step), lambda j: (0, j))
    return pl.pallas_call(
        wgrad_kernel,
        grid=(max(a, b) // step,),
        in_specs=specs,
        out_specs=out_spec,
        out_shape=sds((a, b), BF),
        compiler_params=params(1),
        cost_estimate=cost(2 * rows * a * b, 2 * (rows * (a + b) + a * b)),
        name="wgrad",
    )(left, right)


def spatial_wgrad_kernel(sh, act, g, out, pat, scr):
    j = pl.program_id(0)
    m = act.shape[1]

    @pl.when(j == 0)
    def _():
        scr[...] = jnp.zeros_like(scr)
        pat[0 : sh.rows, :] = jnp.zeros((sh.rows, TAPS * m), BF)
        pat[(SIDE + 1) * sh.rows :, :] = jnp.zeros((sh.rows, TAPS * m), BF)
        for r in range(SIDE):
            put_shifted(sh, act[r * sh.rows : (r + 1) * sh.rows, :].astype(F32), scr, pat, r + 1)

    for k in range(TAPS):

        @pl.when(j == k)
        def _(k=k):
            rows = slice(k * sh.rows, (k + SIDE) * sh.rows)
            for l in range(TAPS):
                out[l * m : (l + 1) * m, :] = tn(pat[rows, l * m : (l + 1) * m], g[...]).astype(BF)


def spatial_wgrad(sh, act, g):
    m = act.shape[1]
    return pl.pallas_call(
        functools.partial(spatial_wgrad_kernel, sh),
        grid=(TAPS,),
        in_specs=[whole(act.shape), whole(g.shape)],
        out_specs=pl.BlockSpec((TAPS * m, m), lambda j: (j, 0)),
        out_shape=sds((TAPS * TAPS * m, m), BF),
        scratch_shapes=[
            pltpu.VMEM(((SIDE + 2) * sh.rows, TAPS * m), BF),
            pltpu.VMEM((sh.low + 16, m), F32),
        ],
        compiler_params=params(1),
        cost_estimate=cost(18 * sh.total * m * m, 4 * sh.total * m + 18 * m * m),
        name="spatial_wgrad",
    )(act, g)


def total_of(v, devices):
    flat = v.reshape(8, -1)
    spread = jnp.broadcast_to(flat[None], (devices,) + flat.shape)
    got = lax.all_to_all(spread, AXES, 0, 0, tiled=True)
    return jnp.sum(got, axis=0).reshape(v.shape)


def on_device(
    devices,
    owners,
    features,
    grid_size,
    w_reduce,
    w_spatial,
    w_expand,
    gain_mid,
    bias_mid,
    gain_out,
    bias_out,
    head_a,
    head_b,
    head_c,
    label_a,
    label_b,
    label_c,
    drop_bits,
):
    images, _, channels = features.shape
    inner = w_reduce.shape[2]
    blocks = w_reduce.shape[0]
    sh = Shape(images)

    gather = functools.partial(lax.all_gather, axis_name="fsdp", axis=0, tiled=True)
    weights = [
        (gather(w_reduce[b]), gather(w_spatial[b]), gather(w_expand[b])) for b in range(blocks)
    ]
    sizes = [head.shape[1] for head in (head_a, head_b, head_c)]
    spans = [-(-size // 16) * 16 for size in sizes]
    lanes = [-(-size // 128) * 128 for size in sizes]
    offsets = [0, lanes[0], lanes[0] + lanes[1]]
    head_t = jnp.concatenate(
        [
            jnp.pad(head.T, ((0, span - size), (0, 0)))
            for head, size, span in zip((head_a, head_b, head_c), sizes, spans)
        ],
        axis=0,
    )
    head_all = lax.all_gather(head_t, "fsdp", axis=1, tiled=True)

    steps = jnp.arange(SIDE + 1, dtype=jnp.int32)
    bound = grid_size
    row_ok = steps[:SIDE, None, None] < bound[None, None, :]
    col_ok = steps[None, :, None] < bound[None, None, :]
    alive = (row_ok & col_ok).astype(F32)
    mask = jnp.concatenate(
        [
            alive[:, :SIDE, : sh.main].reshape(SIDE, sh.top),
            alive[:, :, sh.main :].reshape(SIDE, sh.low),
        ],
        axis=1,
    ).reshape(sh.total, 1)
    pixel_area = (grid_size * grid_size).astype(F32)
    area = jnp.pad(pixel_area, (0, sh.padded - images), constant_values=1.0)[:, None]
    row = jnp.arange(sh.rows, dtype=jnp.int32)
    owner = jnp.where(row < sh.top, row % sh.main, sh.main + (row - sh.top) % sh.rest)
    pick = (owner[None, :] == jnp.arange(sh.padded, dtype=jnp.int32)[:, None]).astype(BF)
    labels = jnp.pad(jnp.stack([label_a, label_b, label_c], axis=1), ((0, sh.padded - images), (0, 0)))
    bits = jnp.pad(drop_bits, ((0, sh.padded - images), (0, 0)))
    gb_mid = jnp.stack([gain_mid, bias_mid], axis=2)
    gb_out = jnp.stack([gain_out, bias_out], axis=1)

    x = prep(sh, jnp.transpose(features, (1, 0, 2)), mask)
    saved = []
    h1, part = reduce_conv(sh, x, weights[0][0])
    count = jnp.broadcast_to(jnp.sum(pixel_area), (2, inner))
    both = total_of(jnp.concatenate([part, count], axis=0), devices)
    tot1, live_count = both[:2], both[2, 0]
    inv = (1.0 / live_count).reshape(1, 1)
    for b in range(blocks):
        w1, w2, w3 = weights[b]
        act1, h2, part = spatial_conv(sh, h1, tot1, inv, gb_mid[b, 0], mask, w2)
        tot2 = total_of(part, devices)
        act2, h3, part = expand_conv(sh, h2, tot2, inv, gb_mid[b, 1], mask, w3)
        tot3 = total_of(part, devices)
        saved.append((x, h1, tot1, act1, h2, tot2, act2, h3, tot3))
        if b + 1 < blocks:
            x, h1, part = join(sh, h3, x, tot3, inv, gb_out[b], mask, weights[b + 1][0])
            tot1 = total_of(part, devices)
    trunk, pooled = last_join(sh, h3, x, tot3, inv, gb_out[-1], mask, area, pick)
    merged, grad_logits = heads(
        pooled, labels, area, bits, head_all, sizes, offsets, sum(lanes)
    )

    mine = lax.all_to_all(
        pooled.reshape(sh.padded, owners, channels // owners).transpose(1, 0, 2),
        "fsdp",
        0,
        0,
        tiled=True,
    ).reshape(owners * sh.padded, channels // owners)
    all_logits = gather(grad_logits)
    head_grad = tn(all_logits, mine).astype(BF)

    e3, part = top_grad(sh, merged, h3, x, tot3, inv, gb_out[-1], mask)
    btot3 = total_of(part, devices)
    scatter = functools.partial(lax.psum_scatter, axis_name="fsdp", scatter_dimension=0, tiled=True)
    reduce_grads, spatial_grads, expand_grads = [], [], []
    sums_mid, sums_out = [], []
    for b in reversed(range(blocks)):
        w1, w2, w3 = weights[b]
        x, h1, tot1, act1, h2, tot2, act2, h3, tot3 = saved[b]
        g3, e2, part = expand_back(
            sh, e3, h3, tot3, gb_out[b], btot3, inv, mask, w3, h2, tot2, gb_mid[b, 1]
        )
        btot2 = total_of(part, devices)
        expand_grads.insert(0, scatter(wgrad(act2, g3, inner)))
        g2, e1, part = spatial_back(
            sh, e2, h2, tot2, gb_mid[b, 1], btot2, inv, mask, w2, h1, tot1, gb_mid[b, 0]
        )
        btot1 = total_of(part, devices)
        spatial_grads.insert(0, scatter(spatial_wgrad(sh, act1, g2)))
        sums_out.insert(0, (btot3, tot3))
        sums_mid.insert(0, ((btot1, tot1), (btot2, tot2)))
        if b > 0:
            xp, _, _, _, _, _, _, h3p, tot3p = saved[b - 1]
            g1, e3, part = reduce_back(
                sh, e1, h1, tot1, gb_mid[b, 0], btot1, inv, mask, w1, e3, h3p, xp, tot3p, gb_out[b - 1]
            )
            btot3 = total_of(part, devices)
        else:
            g1, grad_features = features_back(
                sh, e1, h1, tot1, gb_mid[b, 0], btot1, inv, mask, w1, e3
            )
        reduce_grads.insert(0, scatter(wgrad(x, g1, inner)))

    reduced = lax.psum(
        (jnp.stack(reduce_grads), jnp.stack(spatial_grads), jnp.stack(expand_grads), head_grad), "dp"
    )
    finals = [v.astype(F32) / SCALE for v in reduced]
    at = [(place, size) for place, size in zip(offsets, sizes)]

    def gains(pair):
        btot, tot = pair
        mu = tot[0] / live_count
        var = jnp.maximum(tot[1] / live_count - mu * mu, 0.0)
        return btot[1] * lax.rsqrt(var + EPS) / SCALE

    return (
        jnp.transpose(trunk, (1, 0, 2)),
        jnp.transpose(grad_features, (1, 0, 2)),
        finals[0],
        finals[1],
        finals[2],
        jnp.stack([jnp.stack([gains(p) for p in pairs]) for pairs in sums_mid]),
        jnp.stack([jnp.stack([p[0][0] / SCALE for p in pairs]) for pairs in sums_mid]),
        jnp.stack([gains(p) for p in sums_out]),
        jnp.stack([p[0][0] / SCALE for p in sums_out]),
    ) + tuple(finals[3][place : place + size].T for place, size in at)


def solution(mesh):
    split = P(AXES)
    rows = P(None, "fsdp", None)
    head = P("fsdp", None)
    in_specs = (
        P(AXES, None, None), split, rows, rows, rows, P(), P(), P(), P(),
        head, head, head, split, split, split, P(AXES, None),
    )
    out_specs = (
        P(AXES, None, None), P(AXES, None, None), rows, rows, rows, P(), P(), P(), P(), head, head, head,
    )
    body = functools.partial(on_device, mesh.size, mesh.shape["fsdp"])
    return jax.shard_map(body, mesh=mesh, in_specs=in_specs, out_specs=out_specs, check_vma=False)
```

```python
import functools

import jax
import jax.numpy as jnp
from jax import lax
from jax.experimental import pallas as pl
from jax.experimental.pallas import tpu as pltpu
from jax.sharding import PartitionSpec as P

SIDE = 7
TAPS = 3
EPS = 1e-05
FLOOR = 0.05
WIDTH = 0.1
SCALE = 256.0
BF = jnp.bfloat16
F32 = jnp.float32
VMEM_LIMIT = 56 * 1024 * 1024
AXES = ("dp", "fsdp")


def nn(left, right):
    return jnp.dot(left, right, preferred_element_type=F32)


def nt(left, right):
    return lax.dot_general(left, right, (((1,), (1,)), ((), ())), preferred_element_type=F32)


def tn(left, right):
    return lax.dot_general(left, right, (((0,), (0,)), ((), ())), preferred_element_type=F32)


def sigmoid(v):
    return 0.5 * jnp.tanh(0.5 * v) + 0.5


def silu_half(u):
    return u * jnp.tanh(u) + u


def slope_twice(u):
    t = jnp.tanh(u)
    return (1.0 + t) * (1.0 + u * (1.0 - t))


def rowsum(v):
    return jnp.sum(v, axis=0, keepdims=True)


def params(n_grid):
    return pltpu.CompilerParams(
        dimension_semantics=("arbitrary",) * n_grid, vmem_limit_bytes=VMEM_LIMIT
    )


def whole(shape):
    zeros = (0,) * len(shape)
    return pl.BlockSpec(shape, lambda *g: zeros)


def tile(rows, cols):
    return pl.BlockSpec((rows, cols), lambda j: (j, 0))


def sds(shape, dtype):
    return jax.ShapeDtypeStruct(shape, dtype)


def cost(flops, nbytes, trans=0):
    return pl.CostEstimate(flops=int(flops), bytes_accessed=int(nbytes), transcendentals=int(trans))


def forward_consts(tot, inv, gb):
    mu = tot[0:1, :] * inv
    var = jnp.maximum(tot[1:2, :] * inv - mu * mu, 0.0)
    rstd = lax.rsqrt(var + EPS)
    a = rstd * gb[0:1, :]
    return mu, rstd, a, gb[1:2, :] - mu * a


def backward_consts(mu, rstd, a, btot, inv):
    ex = (btot[1:2, :] - mu * btot[0:1, :]) * rstd * inv
    c1 = -a * rstd * ex
    c0 = -a * btot[0:1, :] * inv - c1 * mu
    return c1, c0


def clear_at_first(*refs):
    @pl.when(pl.program_id(0) == 0)
    def _():
        for ref in refs:
            ref[...] = jnp.zeros_like(ref)


def add_stats(st, top, low, cols=slice(None)):
    st[0:1, cols] += top
    st[1:2, cols] += low


class Shape:
    def __init__(self, images):
        self.images = images
        self.main = images // 16 * 16
        self.rest = images - self.main
        self.top = SIDE * self.main
        self.low = (SIDE + 1) * self.rest
        self.rows = self.top + self.low
        self.total = SIDE * self.rows
        self.padded = self.main + 16


def prep_kernel(sh, f, mask, x, scr):
    channels = x.shape[1]
    scr[...] = jnp.zeros_like(scr)
    for s in range(SIDE):
        x[s * sh.main : (s + 1) * sh.main, :] = (
            f[s, 0 : sh.main, :].astype(F32) * mask[s * sh.main : (s + 1) * sh.main, :]
        ).astype(BF)
        scr[s * sh.rest : (s + 1) * sh.rest, :] = f[s, sh.main : sh.images, :].astype(F32)
    x[sh.top : sh.rows, :] = jnp.where(mask[sh.top : sh.rows, :] > 0.0, scr[...], 0.0).astype(BF)


def prep(sh, features, mask):
    channels = features.shape[2]
    return pl.pallas_call(
        functools.partial(prep_kernel, sh),
        grid=(SIDE,),
        in_specs=[
            pl.BlockSpec((SIDE, sh.images, channels), lambda j: (j, 0, 0)),
            tile(sh.rows, 1),
        ],
        out_specs=tile(sh.rows, channels),
        out_shape=sds((sh.total, channels), BF),
        scratch_shapes=[pltpu.VMEM((sh.low, channels), F32)],
        compiler_params=params(1),
        name="prep",
    )(features, mask)


def reduce_kernel(x, w, h, st):
    clear_at_first(st)
    acc = nn(x[...], w[...])
    h[...] = acc
    add_stats(st, rowsum(acc), rowsum(acc * acc))


def reduce_conv(sh, x, w):
    c, m = w.shape
    return pl.pallas_call(
        reduce_kernel,
        grid=(SIDE,),
        in_specs=[tile(sh.rows, c), whole((c, m))],
        out_specs=[tile(sh.rows, m), whole((2, m))],
        out_shape=[sds((sh.total, m), F32), sds((2, m), F32)],
        compiler_params=params(1),
        cost_estimate=cost(2 * sh.total * c * m, 2 * sh.total * c + 4 * sh.total * m),
        name="reduce_conv",
    )(x, w)


def shifted(sh, v, scr):
    m = v.shape[1]
    gap = jnp.zeros((sh.main, m), F32)
    scr[8 : 8 + sh.low, :] = v[sh.top :, :]
    before = jnp.concatenate([gap, v[: sh.top - sh.main, :], scr[8 - sh.rest : 8 - sh.rest + sh.low, :]], axis=0)
    after = jnp.concatenate([v[sh.main : sh.top, :], gap, scr[8 + sh.rest : 8 + sh.rest + sh.low, :]], axis=0)
    return before, v, after


def put_shifted(sh, v, scr, pat, row):
    m = v.shape[1]
    at = pl.ds(pl.multiple_of(row * sh.rows, sh.rows), sh.rows)
    for k, part in enumerate(shifted(sh, v, scr)):
        pat[at, k * m : (k + 1) * m] = part.astype(BF)


def spatial_kernel(sh, inv, h1, tot, gb, mask, mask_out, w, act, h2, st, pat, scr):
    j = pl.program_id(0)
    m = h1.shape[1]

    clear_at_first(pat, scr, st)
    mu, rstd, a, b = forward_consts(tot, inv[0, 0], gb)
    acc = None
    for k in range(2):
        at = pl.ds(pl.multiple_of((j + k) * sh.rows, sh.rows), sh.rows)
        part = nn(pat[at, :], w[k * TAPS * m : (k + 1) * TAPS * m, :])
        acc = part if acc is None else acc + part
    y = mask[...] * silu_half(h1[...] * (0.5 * a) + 0.5 * b)
    act[...] = y.astype(BF)
    put_shifted(sh, jnp.where(j < SIDE, y, 0.0), scr, pat, j + 2)
    at = pl.ds(pl.multiple_of((j + 2) * sh.rows, sh.rows), sh.rows)
    acc = acc + nn(pat[at, :], w[2 * TAPS * m :, :])
    h2[...] = acc
    got = jnp.where(j > 0, mask_out[...], 0.0) * acc
    add_stats(st, rowsum(got), rowsum(got * acc))


def spatial_conv(sh, h1, tot, inv, gb, mask, w):
    m = h1.shape[1]
    into = lambda j: (jnp.minimum(j, SIDE - 1), 0)
    outof = lambda j: (jnp.maximum(j - 1, 0), 0)
    return pl.pallas_call(
        functools.partial(spatial_kernel, sh),
        grid=(SIDE + 1,),
        in_specs=[
            pl.BlockSpec(memory_space=pltpu.SMEM),
            pl.BlockSpec((sh.rows, m), into),
            whole((2, m)),
            whole((2, m)),
            pl.BlockSpec((sh.rows, 1), into),
            pl.BlockSpec((sh.rows, 1), outof),
            whole(w.shape),
        ],
        out_specs=[
            pl.BlockSpec((sh.rows, m), into),
            pl.BlockSpec((sh.rows, m), outof),
            whole((2, m)),
        ],
        out_shape=[sds((sh.total, m), BF), sds((sh.total, m), F32), sds((2, m), F32)],
        scratch_shapes=[
            pltpu.VMEM(((SIDE + 3) * sh.rows, TAPS * m), BF),
            pltpu.VMEM((sh.low + 16, m), F32),
        ],
        compiler_params=params(1),
        cost_estimate=cost(2 * sh.total * w.size, 2 * w.size + 10 * sh.total * m),
        name="spatial_conv",
    )(inv, h1, tot, gb, mask, mask, w)


def expand_kernel(inv, h2, tot, gb, mask, w, act, h3, st):
    clear_at_first(st)
    mu, rstd, a, b = forward_consts(tot, inv[0, 0], gb)
    y = (mask[...] * silu_half(h2[...] * (0.5 * a) + 0.5 * b)).astype(BF)
    act[...] = y
    step = 512
    for c in range(0, w.shape[1], step):
        cols = slice(c, c + step)
        acc = nn(y, w[:, cols])
        h3[:, cols] = acc.astype(BF)
        add_stats(st, rowsum(acc), rowsum(acc * acc), cols)


def expand_conv(sh, h2, tot, inv, gb, mask, w):
    m, c = w.shape
    return pl.pallas_call(
        expand_kernel,
        grid=(SIDE,),
        in_specs=[
            pl.BlockSpec(memory_space=pltpu.SMEM),
            tile(sh.rows, m),
            whole((2, m)),
            whole((2, m)),
            tile(sh.rows, 1),
            whole((m, c)),
        ],
        out_specs=[tile(sh.rows, m), tile(sh.rows, c), whole((2, c))],
        out_shape=[sds((sh.total, m), BF), sds((sh.total, c), BF), sds((2, c), F32)],
        compiler_params=params(1),
        cost_estimate=cost(2 * sh.total * c * m, 2 * sh.total * c + 6 * sh.total * m),
        name="expand_conv",
    )(inv, h2, tot, gb, mask, w)


def join_kernel(inv, h3, x, tot, gb, mask, w, y, h1, st):
    clear_at_first(st)
    mu, rstd, a, b = forward_consts(tot, inv[0, 0], gb)
    step = 512
    acc = None
    for c in range(0, x.shape[1], step):
        cols = slice(c, c + step)
        v = h3[:, cols].astype(F32) * a[:, cols] + b[:, cols] + x[:, cols].astype(F32)
        out = (mask[...] * silu_half(0.5 * v)).astype(BF)
        y[:, cols] = out
        part = nn(out, w[cols, :])
        acc = part if acc is None else acc + part
    h1[...] = acc
    add_stats(st, rowsum(acc), rowsum(acc * acc))


def join(sh, h3, x, tot, inv, gb, mask, w):
    c, m = w.shape
    return pl.pallas_call(
        join_kernel,
        grid=(SIDE,),
        in_specs=[
            pl.BlockSpec(memory_space=pltpu.SMEM),
            tile(sh.rows, c),
            tile(sh.rows, c),
            whole((2, c)),
            whole((2, c)),
            tile(sh.rows, 1),
            whole((c, m)),
        ],
        out_specs=[tile(sh.rows, c), tile(sh.rows, m), whole((2, m))],
        out_shape=[sds((sh.total, c), BF), sds((sh.total, m), F32), sds((2, m), F32)],
        compiler_params=params(1),
        cost_estimate=cost(2 * sh.total * c * m, 6 * sh.total * c + 4 * sh.total * m),
        name="join",
    )(inv, h3, x, tot, gb, mask, w)


def last_kernel(sh, inv, h3, x, tot, gb, mask, area, pick, trunk, pooled, sums, scr):
    j = pl.program_id(0)
    clear_at_first(sums)
    mu, rstd, a, b = forward_consts(tot, inv[0, 0], gb)
    step = 512
    for c in range(0, x.shape[1], step):
        cols = slice(c, c + step)
        v = h3[:, cols].astype(F32) * a[:, cols] + b[:, cols] + x[:, cols].astype(F32)
        out = mask[...] * silu_half(0.5 * v)
        low = out.astype(BF)
        scr[:, cols] = out[sh.top :, :]
        for s in range(SIDE):
            trunk[s, 0 : sh.main, cols] = low[s * sh.main : (s + 1) * sh.main, :]
            trunk[s, sh.main : sh.images, cols] = scr[s * sh.rest : (s + 1) * sh.rest, cols].astype(BF)
        sums[:, cols] += nn(pick[...], low)

    @pl.when(j == SIDE - 1)
    def _():
        pooled[...] = (sums[...] / area[...]).astype(BF)


def last_join(sh, h3, x, tot, inv, gb, mask, area, pick):
    c = x.shape[1]
    return pl.pallas_call(
        functools.partial(last_kernel, sh),
        grid=(SIDE,),
        in_specs=[
            pl.BlockSpec(memory_space=pltpu.SMEM),
            tile(sh.rows, c),
            tile(sh.rows, c),
            whole((2, c)),
            whole((2, c)),
            tile(sh.rows, 1),
            whole((sh.padded, 1)),
            whole((sh.padded, sh.rows)),
        ],
        out_specs=[
            pl.BlockSpec((SIDE, sh.images, c), lambda j: (j, 0, 0)),
            whole((sh.padded, c)),
        ],
        out_shape=[sds((SIDE * SIDE, sh.images, c), BF), sds((sh.padded, c), BF)],
        scratch_shapes=[pltpu.VMEM((sh.padded, c), F32), pltpu.VMEM((sh.low, c), F32)],
        compiler_params=params(1),
        cost_estimate=cost(2 * sh.padded * sh.total * c, 6 * sh.total * c),
        name="last_join",
    )(inv, h3, x, tot, gb, mask, area, pick)


def heads_kernel(sizes, offsets, pooled, labels, area, bits, w, merged, out):
    rows = pooled.shape[0]
    out[...] = jnp.zeros_like(out)
    summed = None
    at = 0
    for t, (classes, place) in enumerate(zip(sizes, offsets)):
        span = -(-classes // 16) * 16
        wt = w[at : at + span, :]
        at += span
        logits = nt(pooled[...], wt)
        index = lax.broadcasted_iota(jnp.int32, (rows, span), 1)
        inside = index < classes
        logits = jnp.where(inside, logits, -1e30)
        top = jnp.max(logits, axis=1, keepdims=True)
        ex = jnp.where(inside, jnp.exp(logits - top), 0.0)
        probs = ex / jnp.sum(ex, axis=1, keepdims=True)
        targets = jnp.where(index == labels[:, t : t + 1], 1.0, 0.0)
        grad = (SCALE * (probs - targets)).astype(BF)
        out[:, place : place + span] = grad
        single = nn(grad, wt) / area[...]
        size = jnp.sqrt(single * single + FLOOR * FLOOR)
        summed = single if summed is None else summed + single
        magnitude = size if t == 0 else magnitude + size
    purity = 0.5 * (1.0 + summed / magnitude)
    level = (bits[...].astype(F32) + 0.5) / 32768.0
    keep = sigmoid((purity - level) / WIDTH)
    merged[...] = 0.5 * summed + (keep - 0.5) * magnitude


def heads(pooled, labels, area, bits, w, sizes, offsets, span):
    rows, c = pooled.shape
    return pl.pallas_call(
        functools.partial(heads_kernel, sizes, offsets),
        out_shape=[sds((rows, c), F32), sds((rows, span), BF)],
        compiler_params=pltpu.CompilerParams(vmem_limit_bytes=VMEM_LIMIT),
        cost_estimate=cost(4 * rows * c * span, 2 * w.size),
        name="heads",
    )(pooled, labels, area, bits, w)


def top_grad_kernel(sh, inv, merged, h3, x, tot, gb, mask, e3, st, scr):
    j = pl.program_id(0)
    clear_at_first(st)

    @pl.when(j == 0)
    def _():
        for s in range(SIDE + 1):
            scr[s * sh.rest : (s + 1) * sh.rest, :] = merged[sh.main : sh.images, :]

    half = 0.5 * mask[...]
    mu, rstd, a, b = forward_consts(tot, inv[0, 0], gb)
    step = 256
    for c in range(0, x.shape[1], step):
        cols = slice(c, c + step)
        h = h3[:, cols].astype(F32)
        v = h * a[:, cols] + b[:, cols] + x[:, cols].astype(F32)
        up = jnp.concatenate([merged[0 : sh.main, cols]] * SIDE + [scr[:, cols]], axis=0)
        e = half * up * slope_twice(0.5 * v)
        e3[:, cols] = e.astype(BF)
        add_stats(st, rowsum(e), rowsum(e * h), cols)


def top_grad(sh, merged, h3, x, tot, inv, gb, mask):
    c = x.shape[1]
    return pl.pallas_call(
        functools.partial(top_grad_kernel, sh),
        grid=(SIDE,),
        in_specs=[
            pl.BlockSpec(memory_space=pltpu.SMEM),
            whole(merged.shape),
            tile(sh.rows, c),
            tile(sh.rows, c),
            whole((2, c)),
            whole((2, c)),
            tile(sh.rows, 1),
        ],
        out_specs=[tile(sh.rows, c), whole((2, c))],
        out_shape=[sds((sh.total, c), BF), sds((2, c), F32)],
        scratch_shapes=[pltpu.VMEM((sh.low, c), F32)],
        compiler_params=params(1),
        cost_estimate=cost(20 * sh.total * c, 6 * sh.total * c),
        name="top_grad",
    )(inv, merged, h3, x, tot, gb, mask)


def expand_back_kernel(inv, e3, h3, tot3, gb3, btot3, mask, w, h2, tot2, gb2, g3, e2, st):
    clear_at_first(st)
    mu, rstd, a, b = forward_consts(tot3, inv[0, 0], gb3)
    c1, c0 = backward_consts(mu, rstd, a, btot3, inv[0, 0])
    step = 512
    acc = None
    for c in range(0, e3.shape[1], step):
        cols = slice(c, c + step)
        g = a[:, cols] * e3[:, cols].astype(F32) + c1[:, cols] * h3[:, cols].astype(F32) + c0[:, cols]
        g = (mask[...] * g).astype(BF)
        g3[:, cols] = g
        part = nt(g, w[:, cols])
        acc = part if acc is None else acc + part
    mu, rstd, a, b = forward_consts(tot2, inv[0, 0], gb2)
    h = h2[...]
    e = acc * (0.5 * slope_twice(h * (0.5 * a) + 0.5 * b))
    e2[...] = e
    add_stats(st, rowsum(e), rowsum(e * h))


def expand_back(sh, e3, h3, tot3, gb3, btot3, inv, mask, w, h2, tot2, gb2):
    m, c = w.shape
    return pl.pallas_call(
        expand_back_kernel,
        grid=(SIDE,),
        in_specs=[
            pl.BlockSpec(memory_space=pltpu.SMEM),
            tile(sh.rows, c),
            tile(sh.rows, c),
            whole((2, c)),
            whole((2, c)),
            whole((2, c)),
            tile(sh.rows, 1),
            whole((m, c)),
            tile(sh.rows, m),
            whole((2, m)),
            whole((2, m)),
        ],
        out_specs=[tile(sh.rows, c), tile(sh.rows, m), whole((2, m))],
        out_shape=[sds((sh.total, c), BF), sds((sh.total, m), F32), sds((2, m), F32)],
        compiler_params=params(1),
        cost_estimate=cost(2 * sh.total * c * m, 6 * sh.total * c + 8 * sh.total * m),
        name="expand_back",
    )(inv, e3, h3, tot3, gb3, btot3, mask, w, h2, tot2, gb2)


def spatial_back_kernel(
    sh, inv, e2, h2, tot2, gb2, btot2, mask, mask_out, w, h1, tot1, gb1, g2, e1, st, pat, scr
):
    j = pl.program_id(0)
    m = e2.shape[1]

    clear_at_first(pat, scr, st)

    def taps(k):
        at = pl.ds(pl.multiple_of((j + k) * sh.rows, sh.rows), sh.rows)
        total = None
        for l in range(TAPS):
            tap = TAPS * (2 - k) + (2 - l)
            part = nt(pat[at, l * m : (l + 1) * m], w[tap * m : (tap + 1) * m, :])
            total = part if total is None else total + part
        return total

    acc = taps(0) + taps(1)
    mu, rstd, a, b = forward_consts(tot2, inv[0, 0], gb2)
    c1, c0 = backward_consts(mu, rstd, a, btot2, inv[0, 0])
    g = mask[...] * (a * e2[...] + c1 * h2[...] + c0)
    g2[...] = g.astype(BF)
    put_shifted(sh, jnp.where(j < SIDE, g, 0.0), scr, pat, j + 2)
    acc = acc + taps(2)
    mu, rstd, a, b = forward_consts(tot1, inv[0, 0], gb1)
    h = h1[...]
    e = jnp.where(j > 0, 0.5 * mask_out[...], 0.0) * acc * slope_twice(h * (0.5 * a) + 0.5 * b)
    e1[...] = e
    add_stats(st, rowsum(e), rowsum(e * h))


def spatial_back(sh, e2, h2, tot2, gb2, btot2, inv, mask, w, h1, tot1, gb1):
    m = e2.shape[1]
    into = lambda j: (jnp.minimum(j, SIDE - 1), 0)
    outof = lambda j: (jnp.maximum(j - 1, 0), 0)
    return pl.pallas_call(
        functools.partial(spatial_back_kernel, sh),
        grid=(SIDE + 1,),
        in_specs=[
            pl.BlockSpec(memory_space=pltpu.SMEM),
            pl.BlockSpec((sh.rows, m), into),
            pl.BlockSpec((sh.rows, m), into),
            whole((2, m)),
            whole((2, m)),
            whole((2, m)),
            pl.BlockSpec((sh.rows, 1), into),
            pl.BlockSpec((sh.rows, 1), outof),
            whole(w.shape),
            pl.BlockSpec((sh.rows, m), outof),
            whole((2, m)),
            whole((2, m)),
        ],
        out_specs=[
            pl.BlockSpec((sh.rows, m), into),
            pl.BlockSpec((sh.rows, m), outof),
            whole((2, m)),
        ],
        out_shape=[sds((sh.total, m), BF), sds((sh.total, m), F32), sds((2, m), F32)],
        scratch_shapes=[
            pltpu.VMEM(((SIDE + 3) * sh.rows, TAPS * m), BF),
            pltpu.VMEM((sh.low + 16, m), F32),
        ],
        compiler_params=params(1),
        cost_estimate=cost(2 * sh.total * w.size, 2 * w.size + 18 * sh.total * m),
        name="spatial_back",
    )(inv, e2, h2, tot2, gb2, btot2, mask, mask, w, h1, tot1, gb1)


def reduce_back_kernel(
    inv, e1, h1, tot1, gb1, btot1, mask, w, e3, h3, x, tot3, gb3, g1, down, st
):
    clear_at_first(st)
    mu, rstd, a, b = forward_consts(tot1, inv[0, 0], gb1)
    c1, c0 = backward_consts(mu, rstd, a, btot1, inv[0, 0])
    g = (mask[...] * (a * e1[...] + c1 * h1[...] + c0)).astype(BF)
    g1[...] = g
    mu, rstd, a, b = forward_consts(tot3, inv[0, 0], gb3)
    step = 256
    for c in range(0, x.shape[1], step):
        cols = slice(c, c + step)
        up = nt(g, w[cols, :]) + e3[:, cols].astype(F32)
        h = h3[:, cols].astype(F32)
        v = h * a[:, cols] + b[:, cols] + x[:, cols].astype(F32)
        e = up * (0.5 * slope_twice(0.5 * v))
        down[:, cols] = e.astype(BF)
        add_stats(st, rowsum(e), rowsum(e * h), cols)


def reduce_back(sh, e1, h1, tot1, gb1, btot1, inv, mask, w, e3, h3, x, tot3, gb3):
    c, m = w.shape
    return pl.pallas_call(
        reduce_back_kernel,
        grid=(SIDE,),
        in_specs=[
            pl.BlockSpec(memory_space=pltpu.SMEM),
            tile(sh.rows, m),
            tile(sh.rows, m),
            whole((2, m)),
            whole((2, m)),
            whole((2, m)),
            tile(sh.rows, 1),
            whole((c, m)),
            tile(sh.rows, c),
            tile(sh.rows, c),
            tile(sh.rows, c),
            whole((2, c)),
            whole((2, c)),
        ],
        out_specs=[tile(sh.rows, m), tile(sh.rows, c), whole((2, c))],
        out_shape=[sds((sh.total, m), BF), sds((sh.total, c), BF), sds((2, c), F32)],
        compiler_params=params(1),
        cost_estimate=cost(2 * sh.total * c * m, 8 * sh.total * c + 10 * sh.total * m),
        name="reduce_back",
    )(inv, e1, h1, tot1, gb1, btot1, mask, w, e3, h3, x, tot3, gb3)


def features_back_kernel(sh, inv, e1, h1, tot1, gb1, btot1, mask, w, e3, out, scr):
    mu, rstd, a, b = forward_consts(tot1, inv[0, 0], gb1)
    c1, c0 = backward_consts(mu, rstd, a, btot1, inv[0, 0])
    g = (mask[...] * (a * e1[...] + c1 * h1[...] + c0)).astype(BF)
    step = 512
    for c in range(0, w.shape[0], step):
        cols = slice(c, c + step)
        up = nt(g, w[cols, :]) + e3[:, cols].astype(F32)
        scr[:, cols] = up[sh.top :, :]
        for s in range(SIDE):
            out[s, 0 : sh.main, cols] = up[s * sh.main : (s + 1) * sh.main, :]
            out[s, sh.main : sh.images, cols] = scr[s * sh.rest : (s + 1) * sh.rest, cols]


def features_back(sh, e1, h1, tot1, gb1, btot1, inv, mask, w, e3):
    c, m = w.shape
    return pl.pallas_call(
        functools.partial(features_back_kernel, sh),
        grid=(SIDE,),
        in_specs=[
            pl.BlockSpec(memory_space=pltpu.SMEM),
            tile(sh.rows, m),
            tile(sh.rows, m),
            whole((2, m)),
            whole((2, m)),
            whole((2, m)),
            tile(sh.rows, 1),
            whole((c, m)),
            tile(sh.rows, c),
        ],
        out_specs=pl.BlockSpec((SIDE, sh.images, c), lambda j: (j, 0, 0)),
        out_shape=sds((SIDE * SIDE, sh.images, c), F32),
        scratch_shapes=[pltpu.VMEM((sh.low, c), F32)],
        compiler_params=params(1),
        cost_estimate=cost(2 * sh.total * c * m, 6 * sh.total * c + 10 * sh.total * m),
        name="features_back",
    )(inv, e1, h1, tot1, gb1, btot1, mask, w, e3)


def wgrad_kernel(left, right, out):
    out[...] = tn(left[...], right[...]).astype(BF)


def wgrad(left, right, step):
    rows, a = left.shape
    b = right.shape[1]
    by_left = a >= b
    if by_left:
        specs = [pl.BlockSpec((rows, step), lambda j: (0, j)), whole((rows, b))]
        out_spec = pl.BlockSpec((step, b), lambda j: (j, 0))
    else:
        specs = [whole((rows, a)), pl.BlockSpec((rows, step), lambda j: (0, j))]
        out_spec = pl.BlockSpec((a, step), lambda j: (0, j))
    return pl.pallas_call(
        wgrad_kernel,
        grid=(max(a, b) // step,),
        in_specs=specs,
        out_specs=out_spec,
        out_shape=sds((a, b), BF),
        compiler_params=params(1),
        cost_estimate=cost(2 * rows * a * b, 2 * (rows * (a + b) + a * b)),
        name="wgrad",
    )(left, right)


def reduce_wgrad_kernel(inv, e1, h1, tot1, gb1, btot1, mask, x, out, acc):
    clear_at_first(acc)
    mu, rstd, a, b = forward_consts(tot1, inv[0, 0], gb1)
    c1, c0 = backward_consts(mu, rstd, a, btot1, inv[0, 0])
    g = (mask[...] * (a * e1[...] + c1 * h1[...] + c0)).astype(BF)
    step = 512
    for c in range(0, x.shape[1], step):
        acc[c : c + step, :] += tn(x[:, c : c + step], g)

    @pl.when(pl.program_id(0) == SIDE - 1)
    def _():
        out[...] = acc[...].astype(BF)


def reduce_wgrad(sh, e1, h1, tot1, gb1, btot1, inv, mask, x):
    c, m = x.shape[1], e1.shape[1]
    return pl.pallas_call(
        reduce_wgrad_kernel,
        grid=(SIDE,),
        in_specs=[
            pl.BlockSpec(memory_space=pltpu.SMEM),
            tile(sh.rows, m),
            tile(sh.rows, m),
            whole((2, m)),
            whole((2, m)),
            whole((2, m)),
            tile(sh.rows, 1),
            tile(sh.rows, c),
        ],
        out_specs=whole((c, m)),
        out_shape=sds((c, m), BF),
        scratch_shapes=[pltpu.VMEM((c, m), F32)],
        compiler_params=params(1),
        cost_estimate=cost(2 * sh.total * c * m, 2 * sh.total * c + 8 * sh.total * m),
        name="reduce_wgrad",
    )(inv, e1, h1, tot1, gb1, btot1, mask, x)


def spatial_wgrad_kernel(sh, act, g, out, pat, scr):
    j = pl.program_id(0)
    m = act.shape[1]

    @pl.when(j == 0)
    def _():
        scr[...] = jnp.zeros_like(scr)
        pat[0 : sh.rows, :] = jnp.zeros((sh.rows, TAPS * m), BF)
        pat[(SIDE + 1) * sh.rows :, :] = jnp.zeros((sh.rows, TAPS * m), BF)
        for r in range(SIDE):
            put_shifted(sh, act[r * sh.rows : (r + 1) * sh.rows, :].astype(F32), scr, pat, r + 1)

    for k in range(TAPS):

        @pl.when(j == k)
        def _(k=k):
            rows = slice(k * sh.rows, (k + SIDE) * sh.rows)
            for l in range(TAPS):
                out[l * m : (l + 1) * m, :] = tn(pat[rows, l * m : (l + 1) * m], g[...]).astype(BF)


def spatial_wgrad(sh, act, g):
    m = act.shape[1]
    return pl.pallas_call(
        functools.partial(spatial_wgrad_kernel, sh),
        grid=(TAPS,),
        in_specs=[whole(act.shape), whole(g.shape)],
        out_specs=pl.BlockSpec((TAPS * m, m), lambda j: (j, 0)),
        out_shape=sds((TAPS * TAPS * m, m), BF),
        scratch_shapes=[
            pltpu.VMEM(((SIDE + 2) * sh.rows, TAPS * m), BF),
            pltpu.VMEM((sh.low + 16, m), F32),
        ],
        compiler_params=params(1),
        cost_estimate=cost(18 * sh.total * m * m, 4 * sh.total * m + 18 * m * m),
        name="spatial_wgrad",
    )(act, g)


def assemble_kernel(place, own, mate, out, sem):
    dps, chips, rows, width = own.shape
    copies = []
    for e, src in enumerate((own, mate)):
        for j in range(dps):
            for k in range(chips):
                owner = place[0, 1] ^ (2 * k + e)
                row = pl.multiple_of(owner * rows, rows)
                col = pl.multiple_of((place[0, 0] ^ j) * width, width)
                copies.append(
                    pltpu.make_async_copy(
                        src.at[j, k],
                        out.at[pl.ds(row, rows), pl.ds(col, width)],
                        sem.at[len(copies)],
                    )
                )
    for copy in copies:
        copy.start()
    for copy in copies:
        copy.wait()


def assemble(place, own, mate):
    dps, chips, rows, width = own.shape
    anywhere = pl.BlockSpec(memory_space=pl.ANY)
    return pl.pallas_call(
        assemble_kernel,
        in_specs=[pl.BlockSpec(memory_space=pltpu.SMEM), anywhere, anywhere],
        out_specs=pl.BlockSpec(memory_space=pltpu.VMEM),
        out_shape=sds((2 * chips * rows, dps * width), BF),
        scratch_shapes=[pltpu.SemaphoreType.DMA((2 * dps * chips,))],
        compiler_params=pltpu.CompilerParams(vmem_limit_bytes=VMEM_LIMIT),
        cost_estimate=cost(0, 8 * own.size),
        name="assemble",
    )(place, own, mate)


def flips(v, axis, size, unit):
    return [v] + [
        lax.ppermute(v, axis, [(i, i ^ (unit * k)) for i in range(size)]) for k in range(1, size // unit)
    ]


def others(v, axis, size, unit):
    turns = size // unit
    ways = [
        [(i, (i // unit + d) % turns * unit + i % unit) for i in range(size)]
        for d in range(1, turns)
    ]
    return sum([lax.ppermute(v, axis, way) for way in ways], v)


def total_of(v, sizes):
    dp, fsdp = sizes
    flat = v.reshape(8, -1)
    if flat.size > 2048:
        flat = flat + lax.ppermute(flat, "fsdp", [(i, i ^ 1) for i in range(fsdp)])
        flat = others(flat, "fsdp", fsdp, 2)
        return others(flat, "dp", dp, 1).reshape(v.shape)
    devices = dp * fsdp
    spread = jnp.broadcast_to(flat[None], (devices,) + flat.shape)
    got = lax.all_to_all(spread, AXES, 0, 0, tiled=True)
    return jnp.sum(got, axis=0).reshape(v.shape)


def copies_sum(arrays, dp):
    flat = [v.reshape(-1, 512) for v in arrays]
    flat = jnp.concatenate(flat, axis=0) if len(flat) > 1 else flat[0]
    cut = flat.shape[0] // 32 * 16
    halves = [flat[:cut], flat[cut:]]
    bits = [1 << k for k in range(dp.bit_length() - 1)]
    for turn in range(len(bits)):
        for h in range(2):
            bit = (bits, bits[::-1])[h][turn]
            got = lax.ppermute(halves[h], "dp", [(i, i ^ bit) for i in range(dp)])
            halves[h] = (halves[h].astype(F32) + got.astype(F32)).astype(BF)
    return halves


def copies_out(halves, arrays):
    flat = jnp.concatenate(halves, axis=0).astype(F32) / SCALE
    out, at = [], 0
    for v in arrays:
        rows = v.size // 512
        out.append(flat[at : at + rows].reshape(v.shape))
        at += rows
    return out


def on_device(
    dp,
    owners,
    features,
    grid_size,
    w_reduce,
    w_spatial,
    w_expand,
    gain_mid,
    bias_mid,
    gain_out,
    bias_out,
    head_a,
    head_b,
    head_c,
    label_a,
    label_b,
    label_c,
    drop_bits,
):
    images, _, channels = features.shape
    inner = w_reduce.shape[2]
    blocks = w_reduce.shape[0]
    sh = Shape(images)

    gather = functools.partial(lax.all_gather, axis_name="fsdp", axis=0, tiled=True)
    weights = [
        (
            gather(w_reduce[b]),
            None if b == 0 and owners == 8 and dp == 4 else gather(w_spatial[b]),
            gather(w_expand[b]),
        )
        for b in range(blocks)
    ]
    sizes = [head.shape[1] for head in (head_a, head_b, head_c)]
    spans = [-(-size // 16) * 16 for size in sizes]
    lanes = [-(-size // 128) * 128 for size in sizes]
    offsets = [0, lanes[0], lanes[0] + lanes[1]]
    head_t = jnp.concatenate(
        [
            jnp.pad(head.T, ((0, span - size), (0, 0)))
            for head, size, span in zip((head_a, head_b, head_c), sizes, spans)
        ],
        axis=0,
    )
    head_all = lax.all_gather(head_t, "fsdp", axis=1, tiled=True)

    steps = jnp.arange(SIDE + 1, dtype=jnp.int32)
    bound = grid_size
    row_ok = steps[:SIDE, None, None] < bound[None, None, :]
    col_ok = steps[None, :, None] < bound[None, None, :]
    alive = (row_ok & col_ok).astype(F32)
    mask = jnp.concatenate(
        [
            alive[:, :SIDE, : sh.main].reshape(SIDE, sh.top),
            alive[:, :, sh.main :].reshape(SIDE, sh.low),
        ],
        axis=1,
    ).reshape(sh.total, 1)
    pixel_area = (grid_size * grid_size).astype(F32)
    area = jnp.pad(pixel_area, (0, sh.padded - images), constant_values=1.0)[:, None]
    row = jnp.arange(sh.rows, dtype=jnp.int32)
    owner = jnp.where(row < sh.top, row % sh.main, sh.main + (row - sh.top) % sh.rest)
    pick = (owner[None, :] == jnp.arange(sh.padded, dtype=jnp.int32)[:, None]).astype(BF)
    labels = jnp.pad(jnp.stack([label_a, label_b, label_c], axis=1), ((0, sh.padded - images), (0, 0)))
    bits = jnp.pad(drop_bits, ((0, sh.padded - images), (0, 0)))
    gb_mid = jnp.stack([gain_mid, bias_mid], axis=2)
    gb_out = jnp.stack([gain_out, bias_out], axis=1)

    x = prep(sh, jnp.transpose(features, (1, 0, 2)), mask)
    saved = []

    def in_order(*values):
        return lax.optimization_barrier(values)

    place = jnp.stack([lax.axis_index("dp"), lax.axis_index("fsdp")]).astype(jnp.int32).reshape(1, 2)
    short = owners == 8 and dp == 4
    w1 = weights[0][0]
    if short:
        width = inner // dp
        quarter = lax.dynamic_slice_in_dim(w_spatial[0], place[0, 0] * width, width, 1)
        x, *column = in_order(x, *flips(quarter, "fsdp", owners, 2))
        column = jnp.stack(column)
        own = jnp.stack(flips(column, "dp", dp, 1))
        w1, own = in_order(w1, own)
        mate = lax.ppermute(own, "fsdp", [(i, i ^ 1) for i in range(owners)])
    h1, part = reduce_conv(sh, x, w1)
    if short:
        part, mate = in_order(part, mate)
    count = jnp.broadcast_to(jnp.sum(pixel_area), (2, inner))
    both = total_of(jnp.concatenate([part, count], axis=0), (dp, owners))
    if short:
        both, first_spatial = in_order(both, assemble(place, own, mate))
        weights[0] = (weights[0][0], first_spatial, weights[0][2])
    tot1, live_count = both[:2], both[2, 0]
    inv = (1.0 / live_count).reshape(1, 1)
    for b in range(blocks):
        w1, w2, w3 = weights[b]
        act1, h2, part = spatial_conv(sh, h1, tot1, inv, gb_mid[b, 0], mask, w2)
        tot2 = total_of(part, (dp, owners))
        act2, h3, part = expand_conv(sh, h2, tot2, inv, gb_mid[b, 1], mask, w3)
        tot3 = total_of(part, (dp, owners))
        saved.append((x, h1, tot1, act1, h2, tot2, act2, h3, tot3))
        if b + 1 < blocks:
            x, h1, part = join(sh, h3, x, tot3, inv, gb_out[b], mask, weights[b + 1][0])
            tot1 = total_of(part, (dp, owners))
    trunk, pooled = last_join(sh, h3, x, tot3, inv, gb_out[-1], mask, area, pick)
    merged, grad_logits = heads(
        pooled, labels, area, bits, head_all, sizes, offsets, sum(lanes)
    )

    mine = lax.all_to_all(
        pooled.reshape(sh.padded, owners, channels // owners).transpose(1, 0, 2),
        "fsdp",
        0,
        0,
        tiled=True,
    ).reshape(owners * sh.padded, channels // owners)
    all_logits = gather(grad_logits)
    head_grad = tn(all_logits, mine).astype(BF)

    def in_order(*values):
        return lax.optimization_barrier(values)

    e3, part = top_grad(sh, merged, h3, x, tot3, inv, gb_out[-1], mask)
    btot3 = total_of(part, (dp, owners))
    scatter = functools.partial(lax.psum_scatter, axis_name="fsdp", scatter_dimension=0, tiled=True)
    shards = {}
    sums_mid, sums_out = [], []
    for b in reversed(range(blocks)):
        w1, w2, w3 = weights[b]
        x, h1, tot1, act1, h2, tot2, act2, h3, tot3 = saved[b]
        g3, e2, part = expand_back(
            sh, e3, h3, tot3, gb_out[b], btot3, inv, mask, w3, h2, tot2, gb_mid[b, 1]
        )
        grad = wgrad(act2, g3, inner)
        btot2 = total_of(part, (dp, owners))
        btot2, grad = in_order(btot2, grad)
        shards["expand", b] = scatter(grad)
        g2, e1, part = spatial_back(
            sh, e2, h2, tot2, gb_mid[b, 1], btot2, inv, mask, w2, h1, tot1, gb_mid[b, 0]
        )
        grad = spatial_wgrad(sh, act1, g2)
        if b + 1 < blocks:
            early = [head_grad] + [shards[k, b + 1] for k in ("reduce", "spatial", "expand")]
            part, *early = in_order(part, *early)
            early_halves = copies_sum(early, dp)
        btot1 = total_of(part, (dp, owners))
        btot1, grad = in_order(btot1, grad)
        shards["spatial", b] = scatter(grad)
        sums_out.insert(0, (btot3, tot3))
        sums_mid.insert(0, ((btot1, tot1), (btot2, tot2)))
        if b > 0:
            xp, _, _, _, _, _, _, h3p, tot3p = saved[b - 1]
            g1, e3, part = reduce_back(
                sh, e1, h1, tot1, gb_mid[b, 0], btot1, inv, mask, w1, e3, h3p, xp, tot3p, gb_out[b - 1]
            )
            grad = wgrad(x, g1, inner)
            btot3 = total_of(part, (dp, owners))
            btot3, grad = in_order(btot3, grad)
            shards["reduce", b] = scatter(grad)
        else:
            grad = reduce_wgrad(sh, e1, h1, tot1, gb_mid[b, 0], btot1, inv, mask, x)
            e3, grad = in_order(e3, grad)
            shards["reduce", b] = scatter(grad)
            grad_features = features_back(
                sh, e1, h1, tot1, gb_mid[b, 0], btot1, inv, mask, w1, e3
            )
            (
                grad_features,
                shards["expand", b],
                shards["spatial", b],
                shards["reduce", b],
            ) = in_order(
                grad_features, shards["expand", b], shards["spatial", b], shards["reduce", b]
            )

    groups = [early, [shards["expand", 0], shards["spatial", 0]], [shards["reduce", 0]]]
    halves = [early_halves, copies_sum(groups[1], dp), copies_sum(groups[2], dp)]
    sums = [copies_out(h, g) for h, g in zip(halves, groups)]
    head_grad, reduce_one, spatial_one, expand_one = sums[0]
    (expand_zero, spatial_zero), (reduce_zero,) = sums[1:]
    at = [(place, size) for place, size in zip(offsets, sizes)]

    def gains(pair):
        btot, tot = pair
        mu = tot[0] / live_count
        var = jnp.maximum(tot[1] / live_count - mu * mu, 0.0)
        return (btot[1] - mu * btot[0]) * lax.rsqrt(var + EPS) / SCALE

    return (
        jnp.transpose(trunk, (1, 0, 2)),
        jnp.transpose(grad_features, (1, 0, 2)),
        jnp.stack([reduce_zero, reduce_one]),
        jnp.stack([spatial_zero, spatial_one]),
        jnp.stack([expand_zero, expand_one]),
        jnp.stack([jnp.stack([gains(p) for p in pairs]) for pairs in sums_mid]),
        jnp.stack([jnp.stack([p[0][0] / SCALE for p in pairs]) for pairs in sums_mid]),
        jnp.stack([gains(p) for p in sums_out]),
        jnp.stack([p[0][0] / SCALE for p in sums_out]),
    ) + tuple(head_grad[place : place + size].T for place, size in at)


def solution(mesh):
    split = P(AXES)
    rows = P(None, "fsdp", None)
    head = P("fsdp", None)
    in_specs = (
        P(AXES, None, None), split, rows, rows, rows, P(), P(), P(), P(),
        head, head, head, split, split, split, P(AXES, None),
    )
    out_specs = (
        P(AXES, None, None), P(AXES, None, None), rows, rows, rows, P(), P(), P(), P(), head, head, head,
    )
    body = functools.partial(on_device, mesh.shape["dp"], mesh.shape["fsdp"])
    return jax.shard_map(body, mesh=mesh, in_specs=in_specs, out_specs=out_specs, check_vma=False)
```

```python
import functools

import jax
import jax.numpy as jnp
from jax import lax
from jax.experimental import pallas as pl
from jax.experimental.pallas import tpu as pltpu
from jax.sharding import PartitionSpec as P

SIDE = 7
TAPS = 3
EPS = 1e-05
FLOOR = 0.05
WIDTH = 0.1
SCALE = 256.0
BF = jnp.bfloat16
F32 = jnp.float32
VMEM_LIMIT = 56 * 1024 * 1024
AXES = ("dp", "fsdp")


def nn(left, right):
    return jnp.dot(left, right, preferred_element_type=F32)


def nt(left, right):
    return lax.dot_general(left, right, (((1,), (1,)), ((), ())), preferred_element_type=F32)


def tn(left, right):
    return lax.dot_general(left, right, (((0,), (0,)), ((), ())), preferred_element_type=F32)


def sigmoid(v):
    return 0.5 * jnp.tanh(0.5 * v) + 0.5


def silu_half(u):
    return u * jnp.tanh(u) + u


def slope_twice(u):
    t = jnp.tanh(u)
    return (1.0 + t) * (1.0 + u * (1.0 - t))


def rowsum(v):
    return jnp.sum(v, axis=0, keepdims=True)


def params(n_grid):
    return pltpu.CompilerParams(
        dimension_semantics=("arbitrary",) * n_grid, vmem_limit_bytes=VMEM_LIMIT
    )


def whole(shape):
    zeros = (0,) * len(shape)
    return pl.BlockSpec(shape, lambda *g: zeros)


def tile(rows, cols):
    return pl.BlockSpec((rows, cols), lambda j: (j, 0))


def sds(shape, dtype):
    return jax.ShapeDtypeStruct(shape, dtype)


def cost(flops, nbytes, trans=0):
    return pl.CostEstimate(flops=int(flops), bytes_accessed=int(nbytes), transcendentals=int(trans))


def forward_consts(tot, inv, gb):
    mu = tot[0:1, :] * inv
    var = jnp.maximum(tot[1:2, :] * inv - mu * mu, 0.0)
    rstd = lax.rsqrt(var + EPS)
    a = rstd * gb[0:1, :]
    return mu, rstd, a, gb[1:2, :] - mu * a


def backward_consts(mu, rstd, a, btot, inv):
    ex = (btot[1:2, :] - mu * btot[0:1, :]) * rstd * inv
    c1 = -a * rstd * ex
    c0 = -a * btot[0:1, :] * inv - c1 * mu
    return c1, c0


def clear_at_first(*refs):
    @pl.when(pl.program_id(0) == 0)
    def _():
        for ref in refs:
            ref[...] = jnp.zeros_like(ref)


def add_stats(st, top, low, cols=slice(None)):
    st[0:1, cols] += top
    st[1:2, cols] += low


class Shape:
    def __init__(self, images):
        self.images = images
        self.main = images // 16 * 16
        self.rest = images - self.main
        self.top = SIDE * self.main
        self.low = (SIDE + 1) * self.rest
        self.rows = self.top + self.low
        self.total = SIDE * self.rows
        self.padded = self.main + 16


def prep_kernel(sh, f, mask, x, scr):
    channels = x.shape[1]
    scr[...] = jnp.zeros_like(scr)
    for s in range(SIDE):
        x[s * sh.main : (s + 1) * sh.main, :] = (
            f[s, 0 : sh.main, :].astype(F32) * mask[s * sh.main : (s + 1) * sh.main, :]
        ).astype(BF)
        scr[s * sh.rest : (s + 1) * sh.rest, :] = f[s, sh.main : sh.images, :].astype(F32)
    x[sh.top : sh.rows, :] = jnp.where(mask[sh.top : sh.rows, :] > 0.0, scr[...], 0.0).astype(BF)


def prep(sh, features, mask):
    channels = features.shape[2]
    return pl.pallas_call(
        functools.partial(prep_kernel, sh),
        grid=(SIDE,),
        in_specs=[
            pl.BlockSpec((SIDE, sh.images, channels), lambda j: (j, 0, 0)),
            tile(sh.rows, 1),
        ],
        out_specs=tile(sh.rows, channels),
        out_shape=sds((sh.total, channels), BF),
        scratch_shapes=[pltpu.VMEM((sh.low, channels), F32)],
        compiler_params=params(1),
        name="prep",
    )(features, mask)


def reduce_kernel(x, w, h, st):
    clear_at_first(st)
    acc = nn(x[...], w[...])
    h[...] = acc
    add_stats(st, rowsum(acc), rowsum(acc * acc))


def reduce_conv(sh, x, w):
    c, m = w.shape
    return pl.pallas_call(
        reduce_kernel,
        grid=(SIDE,),
        in_specs=[tile(sh.rows, c), whole((c, m))],
        out_specs=[tile(sh.rows, m), whole((2, m))],
        out_shape=[sds((sh.total, m), F32), sds((2, m), F32)],
        compiler_params=params(1),
        cost_estimate=cost(2 * sh.total * c * m, 2 * sh.total * c + 4 * sh.total * m),
        name="reduce_conv",
    )(x, w)


def shifted(sh, v, scr):
    m = v.shape[1]
    gap = jnp.zeros((sh.main, m), F32)
    scr[8 : 8 + sh.low, :] = v[sh.top :, :]
    before = jnp.concatenate([gap, v[: sh.top - sh.main, :], scr[8 - sh.rest : 8 - sh.rest + sh.low, :]], axis=0)
    after = jnp.concatenate([v[sh.main : sh.top, :], gap, scr[8 + sh.rest : 8 + sh.rest + sh.low, :]], axis=0)
    return before, v, after


def put_shifted(sh, v, scr, pat, row):
    m = v.shape[1]
    at = pl.ds(pl.multiple_of(row * sh.rows, sh.rows), sh.rows)
    for k, part in enumerate(shifted(sh, v, scr)):
        pat[at, k * m : (k + 1) * m] = part.astype(BF)


def spatial_kernel(sh, inv, h1, tot, gb, mask, mask_out, w, act, h2, st, pat, scr):
    j = pl.program_id(0)
    m = h1.shape[1]

    clear_at_first(pat, scr, st)
    mu, rstd, a, b = forward_consts(tot, inv[0, 0], gb)
    acc = None
    for k in range(2):
        at = pl.ds(pl.multiple_of((j + k) * sh.rows, sh.rows), sh.rows)
        part = nn(pat[at, :], w[k * TAPS * m : (k + 1) * TAPS * m, :])
        acc = part if acc is None else acc + part
    y = mask[...] * silu_half(h1[...] * (0.5 * a) + 0.5 * b)
    act[...] = y.astype(BF)
    put_shifted(sh, jnp.where(j < SIDE, y, 0.0), scr, pat, j + 2)
    at = pl.ds(pl.multiple_of((j + 2) * sh.rows, sh.rows), sh.rows)
    acc = acc + nn(pat[at, :], w[2 * TAPS * m :, :])
    h2[...] = acc
    got = jnp.where(j > 0, mask_out[...], 0.0) * acc
    add_stats(st, rowsum(got), rowsum(got * acc))


def spatial_conv(sh, h1, tot, inv, gb, mask, w):
    m = h1.shape[1]
    into = lambda j: (jnp.minimum(j, SIDE - 1), 0)
    outof = lambda j: (jnp.maximum(j - 1, 0), 0)
    return pl.pallas_call(
        functools.partial(spatial_kernel, sh),
        grid=(SIDE + 1,),
        in_specs=[
            pl.BlockSpec(memory_space=pltpu.SMEM),
            pl.BlockSpec((sh.rows, m), into),
            whole((2, m)),
            whole((2, m)),
            pl.BlockSpec((sh.rows, 1), into),
            pl.BlockSpec((sh.rows, 1), outof),
            whole(w.shape),
        ],
        out_specs=[
            pl.BlockSpec((sh.rows, m), into),
            pl.BlockSpec((sh.rows, m), outof),
            whole((2, m)),
        ],
        out_shape=[sds((sh.total, m), BF), sds((sh.total, m), F32), sds((2, m), F32)],
        scratch_shapes=[
            pltpu.VMEM(((SIDE + 3) * sh.rows, TAPS * m), BF),
            pltpu.VMEM((sh.low + 16, m), F32),
        ],
        compiler_params=params(1),
        cost_estimate=cost(2 * sh.total * w.size, 2 * w.size + 10 * sh.total * m),
        name="spatial_conv",
    )(inv, h1, tot, gb, mask, mask, w)


def expand_kernel(inv, h2, tot, gb, mask, w, act, h3, st):
    clear_at_first(st)
    mu, rstd, a, b = forward_consts(tot, inv[0, 0], gb)
    y = (mask[...] * silu_half(h2[...] * (0.5 * a) + 0.5 * b)).astype(BF)
    act[...] = y
    step = 512
    for c in range(0, w.shape[1], step):
        cols = slice(c, c + step)
        acc = nn(y, w[:, cols])
        h3[:, cols] = acc.astype(BF)
        add_stats(st, rowsum(acc), rowsum(acc * acc), cols)


def expand_conv(sh, h2, tot, inv, gb, mask, w):
    m, c = w.shape
    return pl.pallas_call(
        expand_kernel,
        grid=(SIDE,),
        in_specs=[
            pl.BlockSpec(memory_space=pltpu.SMEM),
            tile(sh.rows, m),
            whole((2, m)),
            whole((2, m)),
            tile(sh.rows, 1),
            whole((m, c)),
        ],
        out_specs=[tile(sh.rows, m), tile(sh.rows, c), whole((2, c))],
        out_shape=[sds((sh.total, m), BF), sds((sh.total, c), BF), sds((2, c), F32)],
        compiler_params=params(1),
        cost_estimate=cost(2 * sh.total * c * m, 2 * sh.total * c + 6 * sh.total * m),
        name="expand_conv",
    )(inv, h2, tot, gb, mask, w)


def join_kernel(inv, h3, x, tot, gb, mask, w, y, h1, st):
    clear_at_first(st)
    mu, rstd, a, b = forward_consts(tot, inv[0, 0], gb)
    step = 512
    acc = None
    for c in range(0, x.shape[1], step):
        cols = slice(c, c + step)
        v = h3[:, cols].astype(F32) * a[:, cols] + b[:, cols] + x[:, cols].astype(F32)
        out = (mask[...] * silu_half(0.5 * v)).astype(BF)
        y[:, cols] = out
        part = nn(out, w[cols, :])
        acc = part if acc is None else acc + part
    h1[...] = acc
    add_stats(st, rowsum(acc), rowsum(acc * acc))


def join(sh, h3, x, tot, inv, gb, mask, w):
    c, m = w.shape
    return pl.pallas_call(
        join_kernel,
        grid=(SIDE,),
        in_specs=[
            pl.BlockSpec(memory_space=pltpu.SMEM),
            tile(sh.rows, c),
            tile(sh.rows, c),
            whole((2, c)),
            whole((2, c)),
            tile(sh.rows, 1),
            whole((c, m)),
        ],
        out_specs=[tile(sh.rows, c), tile(sh.rows, m), whole((2, m))],
        out_shape=[sds((sh.total, c), BF), sds((sh.total, m), F32), sds((2, m), F32)],
        compiler_params=params(1),
        cost_estimate=cost(2 * sh.total * c * m, 6 * sh.total * c + 4 * sh.total * m),
        name="join",
    )(inv, h3, x, tot, gb, mask, w)


def last_kernel(sh, inv, h3, x, tot, gb, mask, area, pick, trunk, pooled, sums, scr):
    j = pl.program_id(0)
    clear_at_first(sums)
    mu, rstd, a, b = forward_consts(tot, inv[0, 0], gb)
    step = 512
    for c in range(0, x.shape[1], step):
        cols = slice(c, c + step)
        v = h3[:, cols].astype(F32) * a[:, cols] + b[:, cols] + x[:, cols].astype(F32)
        out = mask[...] * silu_half(0.5 * v)
        low = out.astype(BF)
        scr[:, cols] = out[sh.top :, :]
        for s in range(SIDE):
            trunk[s, 0 : sh.main, cols] = low[s * sh.main : (s + 1) * sh.main, :]
            trunk[s, sh.main : sh.images, cols] = scr[s * sh.rest : (s + 1) * sh.rest, cols].astype(BF)
        sums[:, cols] += nn(pick[...], low)

    @pl.when(j == SIDE - 1)
    def _():
        pooled[...] = (sums[...] / area[...]).astype(BF)


def last_join(sh, h3, x, tot, inv, gb, mask, area, pick):
    c = x.shape[1]
    return pl.pallas_call(
        functools.partial(last_kernel, sh),
        grid=(SIDE,),
        in_specs=[
            pl.BlockSpec(memory_space=pltpu.SMEM),
            tile(sh.rows, c),
            tile(sh.rows, c),
            whole((2, c)),
            whole((2, c)),
            tile(sh.rows, 1),
            whole((sh.padded, 1)),
            whole((sh.padded, sh.rows)),
        ],
        out_specs=[
            pl.BlockSpec((SIDE, sh.images, c), lambda j: (j, 0, 0)),
            whole((sh.padded, c)),
        ],
        out_shape=[sds((SIDE * SIDE, sh.images, c), BF), sds((sh.padded, c), BF)],
        scratch_shapes=[pltpu.VMEM((sh.padded, c), F32), pltpu.VMEM((sh.low, c), F32)],
        compiler_params=params(1),
        cost_estimate=cost(2 * sh.padded * sh.total * c, 6 * sh.total * c),
        name="last_join",
    )(inv, h3, x, tot, gb, mask, area, pick)


def heads_kernel(sizes, offsets, pooled, labels, area, bits, w, merged, out):
    rows = pooled.shape[0]
    out[...] = jnp.zeros_like(out)
    summed = None
    at = 0
    for t, (classes, place) in enumerate(zip(sizes, offsets)):
        span = -(-classes // 16) * 16
        wt = w[at : at + span, :]
        at += span
        logits = nt(pooled[...], wt)
        index = lax.broadcasted_iota(jnp.int32, (rows, span), 1)
        inside = index < classes
        logits = jnp.where(inside, logits, -1e30)
        top = jnp.max(logits, axis=1, keepdims=True)
        ex = jnp.where(inside, jnp.exp(logits - top), 0.0)
        probs = ex / jnp.sum(ex, axis=1, keepdims=True)
        targets = jnp.where(index == labels[:, t : t + 1], 1.0, 0.0)
        grad = (SCALE * (probs - targets)).astype(BF)
        out[:, place : place + span] = grad
        single = nn(grad, wt) / area[...]
        size = jnp.sqrt(single * single + FLOOR * FLOOR)
        summed = single if summed is None else summed + single
        magnitude = size if t == 0 else magnitude + size
    purity = 0.5 * (1.0 + summed / magnitude)
    level = (bits[...].astype(F32) + 0.5) / 32768.0
    keep = sigmoid((purity - level) / WIDTH)
    merged[...] = 0.5 * summed + (keep - 0.5) * magnitude


def heads(pooled, labels, area, bits, w, sizes, offsets, span):
    rows, c = pooled.shape
    return pl.pallas_call(
        functools.partial(heads_kernel, sizes, offsets),
        out_shape=[sds((rows, c), F32), sds((rows, span), BF)],
        compiler_params=pltpu.CompilerParams(vmem_limit_bytes=VMEM_LIMIT),
        cost_estimate=cost(4 * rows * c * span, 2 * w.size),
        name="heads",
    )(pooled, labels, area, bits, w)


def top_grad_kernel(sh, inv, merged, h3, x, tot, gb, mask, e3, st, scr):
    j = pl.program_id(0)
    clear_at_first(st)

    @pl.when(j == 0)
    def _():
        for s in range(SIDE + 1):
            scr[s * sh.rest : (s + 1) * sh.rest, :] = merged[sh.main : sh.images, :]

    half = 0.5 * mask[...]
    mu, rstd, a, b = forward_consts(tot, inv[0, 0], gb)
    step = 256
    for c in range(0, x.shape[1], step):
        cols = slice(c, c + step)
        h = h3[:, cols].astype(F32)
        v = h * a[:, cols] + b[:, cols] + x[:, cols].astype(F32)
        up = jnp.concatenate([merged[0 : sh.main, cols]] * SIDE + [scr[:, cols]], axis=0)
        e = half * up * slope_twice(0.5 * v)
        e3[:, cols] = e.astype(BF)
        add_stats(st, rowsum(e), rowsum(e * h), cols)


def top_grad(sh, merged, h3, x, tot, inv, gb, mask):
    c = x.shape[1]
    return pl.pallas_call(
        functools.partial(top_grad_kernel, sh),
        grid=(SIDE,),
        in_specs=[
            pl.BlockSpec(memory_space=pltpu.SMEM),
            whole(merged.shape),
            tile(sh.rows, c),
            tile(sh.rows, c),
            whole((2, c)),
            whole((2, c)),
            tile(sh.rows, 1),
        ],
        out_specs=[tile(sh.rows, c), whole((2, c))],
        out_shape=[sds((sh.total, c), BF), sds((2, c), F32)],
        scratch_shapes=[pltpu.VMEM((sh.low, c), F32)],
        compiler_params=params(1),
        cost_estimate=cost(20 * sh.total * c, 6 * sh.total * c),
        name="top_grad",
    )(inv, merged, h3, x, tot, gb, mask)


def expand_back_kernel(inv, e3, h3, tot3, gb3, btot3, mask, w, h2, tot2, gb2, g3, e2, st):
    clear_at_first(st)
    mu, rstd, a, b = forward_consts(tot3, inv[0, 0], gb3)
    c1, c0 = backward_consts(mu, rstd, a, btot3, inv[0, 0])
    step = 512
    acc = None
    for c in range(0, e3.shape[1], step):
        cols = slice(c, c + step)
        g = a[:, cols] * e3[:, cols].astype(F32) + c1[:, cols] * h3[:, cols].astype(F32) + c0[:, cols]
        g = (mask[...] * g).astype(BF)
        g3[:, cols] = g
        part = nt(g, w[:, cols])
        acc = part if acc is None else acc + part
    mu, rstd, a, b = forward_consts(tot2, inv[0, 0], gb2)
    h = h2[...]
    e = acc * (0.5 * slope_twice(h * (0.5 * a) + 0.5 * b))
    e2[...] = e
    add_stats(st, rowsum(e), rowsum(e * h))


def expand_back(sh, e3, h3, tot3, gb3, btot3, inv, mask, w, h2, tot2, gb2):
    m, c = w.shape
    return pl.pallas_call(
        expand_back_kernel,
        grid=(SIDE,),
        in_specs=[
            pl.BlockSpec(memory_space=pltpu.SMEM),
            tile(sh.rows, c),
            tile(sh.rows, c),
            whole((2, c)),
            whole((2, c)),
            whole((2, c)),
            tile(sh.rows, 1),
            whole((m, c)),
            tile(sh.rows, m),
            whole((2, m)),
            whole((2, m)),
        ],
        out_specs=[tile(sh.rows, c), tile(sh.rows, m), whole((2, m))],
        out_shape=[sds((sh.total, c), BF), sds((sh.total, m), F32), sds((2, m), F32)],
        compiler_params=params(1),
        cost_estimate=cost(2 * sh.total * c * m, 6 * sh.total * c + 8 * sh.total * m),
        name="expand_back",
    )(inv, e3, h3, tot3, gb3, btot3, mask, w, h2, tot2, gb2)


def spatial_back_kernel(
    sh, inv, e2, h2, tot2, gb2, btot2, mask, mask_out, w, h1, tot1, gb1, g2, e1, st, pat, scr
):
    j = pl.program_id(0)
    m = e2.shape[1]

    clear_at_first(pat, scr, st)

    def taps(k):
        at = pl.ds(pl.multiple_of((j + k) * sh.rows, sh.rows), sh.rows)
        total = None
        for l in range(TAPS):
            tap = TAPS * (2 - k) + (2 - l)
            part = nt(pat[at, l * m : (l + 1) * m], w[tap * m : (tap + 1) * m, :])
            total = part if total is None else total + part
        return total

    acc = taps(0) + taps(1)
    mu, rstd, a, b = forward_consts(tot2, inv[0, 0], gb2)
    c1, c0 = backward_consts(mu, rstd, a, btot2, inv[0, 0])
    g = mask[...] * (a * e2[...] + c1 * h2[...] + c0)
    g2[...] = g.astype(BF)
    put_shifted(sh, jnp.where(j < SIDE, g, 0.0), scr, pat, j + 2)
    acc = acc + taps(2)
    mu, rstd, a, b = forward_consts(tot1, inv[0, 0], gb1)
    h = h1[...]
    e = jnp.where(j > 0, 0.5 * mask_out[...], 0.0) * acc * slope_twice(h * (0.5 * a) + 0.5 * b)
    e1[...] = e
    add_stats(st, rowsum(e), rowsum(e * h))


def spatial_back(sh, e2, h2, tot2, gb2, btot2, inv, mask, w, h1, tot1, gb1):
    m = e2.shape[1]
    into = lambda j: (jnp.minimum(j, SIDE - 1), 0)
    outof = lambda j: (jnp.maximum(j - 1, 0), 0)
    return pl.pallas_call(
        functools.partial(spatial_back_kernel, sh),
        grid=(SIDE + 1,),
        in_specs=[
            pl.BlockSpec(memory_space=pltpu.SMEM),
            pl.BlockSpec((sh.rows, m), into),
            pl.BlockSpec((sh.rows, m), into),
            whole((2, m)),
            whole((2, m)),
            whole((2, m)),
            pl.BlockSpec((sh.rows, 1), into),
            pl.BlockSpec((sh.rows, 1), outof),
            whole(w.shape),
            pl.BlockSpec((sh.rows, m), outof),
            whole((2, m)),
            whole((2, m)),
        ],
        out_specs=[
            pl.BlockSpec((sh.rows, m), into),
            pl.BlockSpec((sh.rows, m), outof),
            whole((2, m)),
        ],
        out_shape=[sds((sh.total, m), BF), sds((sh.total, m), F32), sds((2, m), F32)],
        scratch_shapes=[
            pltpu.VMEM(((SIDE + 3) * sh.rows, TAPS * m), BF),
            pltpu.VMEM((sh.low + 16, m), F32),
        ],
        compiler_params=params(1),
        cost_estimate=cost(2 * sh.total * w.size, 2 * w.size + 18 * sh.total * m),
        name="spatial_back",
    )(inv, e2, h2, tot2, gb2, btot2, mask, mask, w, h1, tot1, gb1)


def reduce_back_kernel(
    inv, e1, h1, tot1, gb1, btot1, mask, w, e3, h3, x, tot3, gb3, g1, down, st
):
    clear_at_first(st)
    mu, rstd, a, b = forward_consts(tot1, inv[0, 0], gb1)
    c1, c0 = backward_consts(mu, rstd, a, btot1, inv[0, 0])
    g = (mask[...] * (a * e1[...] + c1 * h1[...] + c0)).astype(BF)
    g1[...] = g
    mu, rstd, a, b = forward_consts(tot3, inv[0, 0], gb3)
    step = 256
    for c in range(0, x.shape[1], step):
        cols = slice(c, c + step)
        up = nt(g, w[cols, :]) + e3[:, cols].astype(F32)
        h = h3[:, cols].astype(F32)
        v = h * a[:, cols] + b[:, cols] + x[:, cols].astype(F32)
        e = up * (0.5 * slope_twice(0.5 * v))
        down[:, cols] = e.astype(BF)
        add_stats(st, rowsum(e), rowsum(e * h), cols)


def reduce_back(sh, e1, h1, tot1, gb1, btot1, inv, mask, w, e3, h3, x, tot3, gb3):
    c, m = w.shape
    return pl.pallas_call(
        reduce_back_kernel,
        grid=(SIDE,),
        in_specs=[
            pl.BlockSpec(memory_space=pltpu.SMEM),
            tile(sh.rows, m),
            tile(sh.rows, m),
            whole((2, m)),
            whole((2, m)),
            whole((2, m)),
            tile(sh.rows, 1),
            whole((c, m)),
            tile(sh.rows, c),
            tile(sh.rows, c),
            tile(sh.rows, c),
            whole((2, c)),
            whole((2, c)),
        ],
        out_specs=[tile(sh.rows, m), tile(sh.rows, c), whole((2, c))],
        out_shape=[sds((sh.total, m), BF), sds((sh.total, c), BF), sds((2, c), F32)],
        compiler_params=params(1),
        cost_estimate=cost(2 * sh.total * c * m, 8 * sh.total * c + 10 * sh.total * m),
        name="reduce_back",
    )(inv, e1, h1, tot1, gb1, btot1, mask, w, e3, h3, x, tot3, gb3)


def features_back_kernel(sh, inv, e1, h1, tot1, gb1, btot1, mask, w, e3, out, scr):
    mu, rstd, a, b = forward_consts(tot1, inv[0, 0], gb1)
    c1, c0 = backward_consts(mu, rstd, a, btot1, inv[0, 0])
    g = (mask[...] * (a * e1[...] + c1 * h1[...] + c0)).astype(BF)
    step = 512
    for c in range(0, w.shape[0], step):
        cols = slice(c, c + step)
        up = nt(g, w[cols, :]) + e3[:, cols].astype(F32)
        scr[:, cols] = up[sh.top :, :]
        for s in range(SIDE):
            out[s, 0 : sh.main, cols] = up[s * sh.main : (s + 1) * sh.main, :]
            out[s, sh.main : sh.images, cols] = scr[s * sh.rest : (s + 1) * sh.rest, cols]


def features_back(sh, e1, h1, tot1, gb1, btot1, inv, mask, w, e3):
    c, m = w.shape
    return pl.pallas_call(
        functools.partial(features_back_kernel, sh),
        grid=(SIDE,),
        in_specs=[
            pl.BlockSpec(memory_space=pltpu.SMEM),
            tile(sh.rows, m),
            tile(sh.rows, m),
            whole((2, m)),
            whole((2, m)),
            whole((2, m)),
            tile(sh.rows, 1),
            whole((c, m)),
            tile(sh.rows, c),
        ],
        out_specs=pl.BlockSpec((SIDE, sh.images, c), lambda j: (j, 0, 0)),
        out_shape=sds((SIDE * SIDE, sh.images, c), F32),
        scratch_shapes=[pltpu.VMEM((sh.low, c), F32)],
        compiler_params=params(1),
        cost_estimate=cost(2 * sh.total * c * m, 6 * sh.total * c + 10 * sh.total * m),
        name="features_back",
    )(inv, e1, h1, tot1, gb1, btot1, mask, w, e3)


def wgrad_kernel(left, right, out):
    out[...] = tn(left[...], right[...]).astype(BF)


def wgrad(left, right, step):
    rows, a = left.shape
    b = right.shape[1]
    by_left = a >= b
    if by_left:
        specs = [pl.BlockSpec((rows, step), lambda j: (0, j)), whole((rows, b))]
        out_spec = pl.BlockSpec((step, b), lambda j: (j, 0))
    else:
        specs = [whole((rows, a)), pl.BlockSpec((rows, step), lambda j: (0, j))]
        out_spec = pl.BlockSpec((a, step), lambda j: (0, j))
    return pl.pallas_call(
        wgrad_kernel,
        grid=(max(a, b) // step,),
        in_specs=specs,
        out_specs=out_spec,
        out_shape=sds((a, b), BF),
        compiler_params=params(1),
        cost_estimate=cost(2 * rows * a * b, 2 * (rows * (a + b) + a * b)),
        name="wgrad",
    )(left, right)


def reduce_wgrad_kernel(inv, e1, h1, tot1, gb1, btot1, mask, x, out, acc):
    clear_at_first(acc)
    mu, rstd, a, b = forward_consts(tot1, inv[0, 0], gb1)
    c1, c0 = backward_consts(mu, rstd, a, btot1, inv[0, 0])
    g = (mask[...] * (a * e1[...] + c1 * h1[...] + c0)).astype(BF)
    step = 512
    for c in range(0, x.shape[1], step):
        acc[c : c + step, :] += tn(x[:, c : c + step], g)

    @pl.when(pl.program_id(0) == SIDE - 1)
    def _():
        out[...] = acc[...].astype(BF)


def reduce_wgrad(sh, e1, h1, tot1, gb1, btot1, inv, mask, x):
    c, m = x.shape[1], e1.shape[1]
    return pl.pallas_call(
        reduce_wgrad_kernel,
        grid=(SIDE,),
        in_specs=[
            pl.BlockSpec(memory_space=pltpu.SMEM),
            tile(sh.rows, m),
            tile(sh.rows, m),
            whole((2, m)),
            whole((2, m)),
            whole((2, m)),
            tile(sh.rows, 1),
            tile(sh.rows, c),
        ],
        out_specs=whole((c, m)),
        out_shape=sds((c, m), BF),
        scratch_shapes=[pltpu.VMEM((c, m), F32)],
        compiler_params=params(1),
        cost_estimate=cost(2 * sh.total * c * m, 2 * sh.total * c + 8 * sh.total * m),
        name="reduce_wgrad",
    )(inv, e1, h1, tot1, gb1, btot1, mask, x)


def put_owned(place, val, outs, first):
    dps, chips, rows, width = outs[0].shape
    last, at = first + val.shape[0], first
    while at < last:
        chip, start = at // (2 * rows), at % (2 * rows)
        stop = min(2 * rows, start + last - at)
        for side in range(2):
            low, high = max(start, side * rows), min(stop, (side + 1) * rows)
            if low >= high:
                continue
            source = pl.ds(at - first + low - start, high - low)
            for q in range(dps):
                piece = val[source, q * width : (q + 1) * width]
                for e, out in enumerate(outs):

                    @pl.when((place[0, 1] & 1) == (side ^ e))
                    def _(piece=piece, out=out, low=low, high=high, q=q):
                        out[q ^ place[0, 0], chip ^ (place[0, 1] >> 1), low - side * rows : high - side * rows, :] = piece
        at += stop - start


def spatial_wgrad_kernel(sh, owned, place, act, g, *rest):
    *outs, pat, scr, val = rest
    j = pl.program_id(0)
    m = act.shape[1]

    @pl.when(j == 0)
    def _():
        scr[...] = jnp.zeros_like(scr)
        pat[0 : sh.rows, :] = jnp.zeros((sh.rows, TAPS * m), BF)
        pat[(SIDE + 1) * sh.rows :, :] = jnp.zeros((sh.rows, TAPS * m), BF)
        for r in range(SIDE):
            put_shifted(sh, act[r * sh.rows : (r + 1) * sh.rows, :].astype(F32), scr, pat, r + 1)

    for k in range(TAPS):

        @pl.when(j == k)
        def _(k=k):
            rows = slice(k * sh.rows, (k + SIDE) * sh.rows)
            for l in range(TAPS):
                into = val if owned else outs[0]
                into[l * m : (l + 1) * m, :] = tn(pat[rows, l * m : (l + 1) * m], g[...]).astype(BF)
            if owned:
                put_owned(place, val, outs, k * TAPS * m)


def spatial_wgrad(sh, act, g, place, owners, dp, owned):
    m = act.shape[1]
    rows = TAPS * TAPS * m
    owned_shape = (dp, owners // 2, rows // owners, m // dp)
    return pl.pallas_call(
        functools.partial(spatial_wgrad_kernel, sh, owned),
        grid=(TAPS,),
        in_specs=[pl.BlockSpec(memory_space=pltpu.SMEM), whole(act.shape), whole(g.shape)],
        out_specs=[whole(owned_shape)] * 2 if owned else [pl.BlockSpec((TAPS * m, m), lambda j: (j, 0))],
        out_shape=[sds(owned_shape, BF)] * 2 if owned else [sds((rows, m), BF)],
        scratch_shapes=[
            pltpu.VMEM(((SIDE + 2) * sh.rows, TAPS * m), BF),
            pltpu.VMEM((sh.low + 16, m), F32),
            pltpu.VMEM((TAPS * m, m), BF),
        ],
        compiler_params=params(1),
        cost_estimate=cost(18 * sh.total * m * m, 4 * sh.total * m + 18 * m * m),
        name="spatial_wgrad",
    )(place, act, g)


def assemble_kernel(place, own, mate, out, sem):
    dps, chips, rows, width = own.shape
    copies = []
    for e, src in enumerate((own, mate)):
        for j in range(dps):
            for k in range(chips):
                owner = place[0, 1] ^ (2 * k + e)
                row = pl.multiple_of(owner * rows, rows)
                col = pl.multiple_of((place[0, 0] ^ j) * width, width)
                copies.append(
                    pltpu.make_async_copy(
                        src.at[j, k],
                        out.at[pl.ds(row, rows), pl.ds(col, width)],
                        sem.at[len(copies)],
                    )
                )
    for copy in copies:
        copy.start()
    for copy in copies:
        copy.wait()


def assemble(place, own, mate):
    dps, chips, rows, width = own.shape
    anywhere = pl.BlockSpec(memory_space=pl.ANY)
    return pl.pallas_call(
        assemble_kernel,
        in_specs=[pl.BlockSpec(memory_space=pltpu.SMEM), anywhere, anywhere],
        out_specs=pl.BlockSpec(memory_space=pltpu.VMEM),
        out_shape=sds((2 * chips * rows, dps * width), BF),
        scratch_shapes=[pltpu.SemaphoreType.DMA((2 * dps * chips,))],
        compiler_params=pltpu.CompilerParams(vmem_limit_bytes=VMEM_LIMIT),
        cost_estimate=cost(0, 8 * own.size),
        name="assemble",
    )(place, own, mate)


def flips(v, axis, size, unit):
    return [v] + [
        lax.ppermute(v, axis, [(i, i ^ (unit * k)) for i in range(size)]) for k in range(1, size // unit)
    ]


def others(v, axis, size, unit):
    turns = size // unit
    ways = [
        [(i, (i // unit + d) % turns * unit + i % unit) for i in range(size)]
        for d in range(1, turns)
    ]
    return sum([lax.ppermute(v, axis, way) for way in ways], v)


def total_of(v, sizes):
    dp, fsdp = sizes
    flat = v.reshape(8, -1)
    if flat.size > 2048:
        flat = flat + lax.ppermute(flat, "fsdp", [(i, i ^ 1) for i in range(fsdp)])
        flat = others(flat, "fsdp", fsdp, 2)
        return others(flat, "dp", dp, 1).reshape(v.shape)
    devices = dp * fsdp
    spread = jnp.broadcast_to(flat[None], (devices,) + flat.shape)
    got = lax.all_to_all(spread, AXES, 0, 0, tiled=True)
    return jnp.sum(got, axis=0).reshape(v.shape)


def added(*terms):
    return sum([v.astype(F32) for v in terms[1:]], terms[0].astype(F32)).astype(BF)


def copies_halves(arrays):
    flat = [v.reshape(-1, 512) for v in arrays]
    flat = jnp.concatenate(flat, axis=0) if len(flat) > 1 else flat[0]
    cut = flat.shape[0] // 32 * 16
    return [flat[:cut], flat[cut:]]


def copies_swap(halves, dp, turn):
    bits = [1 << k for k in range(dp.bit_length() - 1)]
    return [
        lax.ppermute(half, "dp", [(i, i ^ (bits, bits[::-1])[h][turn]) for i in range(dp)])
        for h, half in enumerate(halves)
    ]


def copies_add(halves, got):
    return [added(half, other) for half, other in zip(halves, got)]


def copies_sum(halves, dp, first=0):
    for turn in range(first, dp.bit_length() - 1):
        halves = copies_add(halves, copies_swap(halves, dp, turn))
    return halves


def swap_core(parts, owners):
    return lax.ppermute(parts[1], "fsdp", [(i, i ^ 1) for i in range(owners)])


def swap_rest(blocks, axis, size, unit):
    return [
        lax.ppermute(blocks[k], axis, [(i, i ^ (unit * k)) for i in range(size)])
        for k in range(1, len(blocks))
    ]


def copies_out(halves, arrays):
    flat = jnp.concatenate(halves, axis=0).astype(F32) / SCALE
    out, at = [], 0
    for v in arrays:
        rows = v.size // 512
        out.append(flat[at : at + rows].reshape(v.shape))
        at += rows
    return out


def on_device(
    dp,
    owners,
    features,
    grid_size,
    w_reduce,
    w_spatial,
    w_expand,
    gain_mid,
    bias_mid,
    gain_out,
    bias_out,
    head_a,
    head_b,
    head_c,
    label_a,
    label_b,
    label_c,
    drop_bits,
):
    images, _, channels = features.shape
    inner = w_reduce.shape[2]
    blocks = w_reduce.shape[0]
    sh = Shape(images)

    gather = functools.partial(lax.all_gather, axis_name="fsdp", axis=0, tiled=True)
    weights = [
        (
            gather(w_reduce[b]),
            None if b == 0 and owners == 8 and dp == 4 else gather(w_spatial[b]),
            gather(w_expand[b]),
        )
        for b in range(blocks)
    ]
    sizes = [head.shape[1] for head in (head_a, head_b, head_c)]
    spans = [-(-size // 16) * 16 for size in sizes]
    lanes = [-(-size // 128) * 128 for size in sizes]
    offsets = [0, lanes[0], lanes[0] + lanes[1]]
    head_t = jnp.concatenate(
        [
            jnp.pad(head.T, ((0, span - size), (0, 0)))
            for head, size, span in zip((head_a, head_b, head_c), sizes, spans)
        ],
        axis=0,
    )
    head_all = lax.all_gather(head_t, "fsdp", axis=1, tiled=True)

    steps = jnp.arange(SIDE + 1, dtype=jnp.int32)
    bound = grid_size
    row_ok = steps[:SIDE, None, None] < bound[None, None, :]
    col_ok = steps[None, :, None] < bound[None, None, :]
    alive = (row_ok & col_ok).astype(F32)
    mask = jnp.concatenate(
        [
            alive[:, :SIDE, : sh.main].reshape(SIDE, sh.top),
            alive[:, :, sh.main :].reshape(SIDE, sh.low),
        ],
        axis=1,
    ).reshape(sh.total, 1)
    pixel_area = (grid_size * grid_size).astype(F32)
    area = jnp.pad(pixel_area, (0, sh.padded - images), constant_values=1.0)[:, None]
    row = jnp.arange(sh.rows, dtype=jnp.int32)
    owner = jnp.where(row < sh.top, row % sh.main, sh.main + (row - sh.top) % sh.rest)
    pick = (owner[None, :] == jnp.arange(sh.padded, dtype=jnp.int32)[:, None]).astype(BF)
    labels = jnp.pad(jnp.stack([label_a, label_b, label_c], axis=1), ((0, sh.padded - images), (0, 0)))
    bits = jnp.pad(drop_bits, ((0, sh.padded - images), (0, 0)))
    gb_mid = jnp.stack([gain_mid, bias_mid], axis=2)
    gb_out = jnp.stack([gain_out, bias_out], axis=1)

    x = prep(sh, jnp.transpose(features, (1, 0, 2)), mask)
    saved = []

    def in_order(*values):
        return lax.optimization_barrier(values)

    place = jnp.stack([lax.axis_index("dp"), lax.axis_index("fsdp")]).astype(jnp.int32).reshape(1, 2)
    short = owners == 8 and dp == 4
    w1 = weights[0][0]
    if short:
        width = inner // dp
        quarter = lax.dynamic_slice_in_dim(w_spatial[0], place[0, 0] * width, width, 1)
        x, *column = in_order(x, *flips(quarter, "fsdp", owners, 2))
        column = jnp.stack(column)
        own = jnp.stack(flips(column, "dp", dp, 1))
        w1, own = in_order(w1, own)
        mate = lax.ppermute(own, "fsdp", [(i, i ^ 1) for i in range(owners)])
    h1, part = reduce_conv(sh, x, w1)
    if short:
        part, mate = in_order(part, mate)
    count = jnp.broadcast_to(jnp.sum(pixel_area), (2, inner))
    both = total_of(jnp.concatenate([part, count], axis=0), (dp, owners))
    if short:
        both, first_spatial = in_order(both, assemble(place, own, mate))
        weights[0] = (weights[0][0], first_spatial, weights[0][2])
    tot1, live_count = both[:2], both[2, 0]
    inv = (1.0 / live_count).reshape(1, 1)
    for b in range(blocks):
        w1, w2, w3 = weights[b]
        act1, h2, part = spatial_conv(sh, h1, tot1, inv, gb_mid[b, 0], mask, w2)
        tot2 = total_of(part, (dp, owners))
        act2, h3, part = expand_conv(sh, h2, tot2, inv, gb_mid[b, 1], mask, w3)
        tot3 = total_of(part, (dp, owners))
        saved.append((x, h1, tot1, act1, h2, tot2, act2, h3, tot3))
        if b + 1 < blocks:
            x, h1, part = join(sh, h3, x, tot3, inv, gb_out[b], mask, weights[b + 1][0])
            tot1 = total_of(part, (dp, owners))
    trunk, pooled = last_join(sh, h3, x, tot3, inv, gb_out[-1], mask, area, pick)
    merged, grad_logits = heads(
        pooled, labels, area, bits, head_all, sizes, offsets, sum(lanes)
    )

    mine = lax.all_to_all(
        pooled.reshape(sh.padded, owners, channels // owners).transpose(1, 0, 2),
        "fsdp",
        0,
        0,
        tiled=True,
    ).reshape(owners * sh.padded, channels // owners)
    all_logits = gather(grad_logits)

    def in_order(*values):
        return lax.optimization_barrier(values)

    e3, part = top_grad(sh, merged, h3, x, tot3, inv, gb_out[-1], mask)
    part, mine = in_order(part, mine)
    btot3 = total_of(part, (dp, owners))
    scatter = functools.partial(lax.psum_scatter, axis_name="fsdp", scatter_dimension=0, tiled=True)
    shards, swaps = {}, {}
    sums_mid, sums_out = [], []
    for b in reversed(range(blocks)):
        w1, w2, w3 = weights[b]
        x, h1, tot1, act1, h2, tot2, act2, h3, tot3 = saved[b]
        g3, e2, part = expand_back(
            sh, e3, h3, tot3, gb_out[b], btot3, inv, mask, w3, h2, tot2, gb_mid[b, 1]
        )
        grad = wgrad(act2, g3, inner)
        if short and b + 1 < blocks:
            terms = swaps[b + 1]
            part, *got = in_order(part, *swap_rest(terms, "dp", dp, 1))
            total = added(terms[0], *got)
            swaps[b + 1] = [total[k] for k in range(owners // 2)]
        btot2 = total_of(part, (dp, owners))
        btot2, grad = in_order(btot2, grad)
        shards["expand", b] = scatter(grad)
        if b + 1 == blocks:
            head_grad = tn(all_logits, mine).astype(BF)
        g2, e1, part = spatial_back(
            sh, e2, h2, tot2, gb_mid[b, 1], btot2, inv, mask, w2, h1, tot1, gb_mid[b, 0]
        )
        grad = spatial_wgrad(sh, act1, g2, place, owners, dp, short)
        if short and b + 1 < blocks:
            part, *got = in_order(part, *swap_rest(swaps[b + 1], "fsdp", owners, 2))
            shards["spatial", b + 1] = added(swaps[b + 1][0], *got)
        if b == 0:
            early = [head_grad] + [shards["reduce", k] for k in range(1, blocks)]
            early += [shards["expand", k] for k in range(1, blocks)]
            halves = copies_halves(early)
            part, *swapped = in_order(part, *copies_swap(halves, dp, 0))
            halves = copies_add(halves, swapped)
            swapped = copies_swap(halves, dp, 1)
        btot1 = total_of(part, (dp, owners))
        btot1, *grad = in_order(btot1, *grad)
        if short:
            other = swap_core(grad, owners)
        else:
            shards["spatial", b] = scatter(grad[0])
        sums_out.insert(0, (btot3, tot3))
        sums_mid.insert(0, ((btot1, tot1), (btot2, tot2)))
        if b > 0:
            xp, _, _, _, _, _, _, h3p, tot3p = saved[b - 1]
            g1, e3, part = reduce_back(
                sh, e1, h1, tot1, gb_mid[b, 0], btot1, inv, mask, w1, e3, h3p, xp, tot3p, gb_out[b - 1]
            )
            if short:
                part, other = in_order(part, other)
                swaps[b] = [added(grad[0][j], other[j]) for j in range(dp)]
            grad = wgrad(x, g1, inner)
            btot3 = total_of(part, (dp, owners))
            btot3, grad = in_order(btot3, grad)
            shards["reduce", b] = scatter(grad)
        else:
            spatial = grad
            grad = reduce_wgrad(sh, e1, h1, tot1, gb_mid[b, 0], btot1, inv, mask, x)
            grad, *swapped = in_order(grad, *swapped)
            halves = copies_add(halves, swapped)
            if short:
                grad, other = in_order(grad, other)
                swaps[b] = [added(spatial[0][j], other[j]) for j in range(dp)]
                e3, grad, *swaps[b] = in_order(e3, grad, *swaps[b])
                got = swap_rest(swaps[b], "dp", dp, 1)
            else:
                e3, grad = in_order(e3, grad)
                got = [shards["spatial", k] for k in range(blocks)]
            shards["reduce", b] = scatter(grad)
            grad_features = features_back(
                sh, e1, h1, tot1, gb_mid[b, 0], btot1, inv, mask, w1, e3
            )
            grad_features, shards["reduce", b], shards["expand", b], *got = in_order(
                grad_features, shards["reduce", b], shards["expand", b], *got
            )

    if short:
        total = added(swaps[0][0], *got)
        total = [total[k] for k in range(owners // 2)]
        shards["spatial", 0] = added(total[0], *swap_rest(total, "fsdp", owners, 2))
        flat = jnp.stack([shards["spatial", b] for b in range(blocks)])
        flat = jnp.broadcast_to(flat[None], (dp,) + flat.shape)
        flat = lax.all_to_all(flat, "dp", 0, 0, tiled=True)
        spatial = jnp.transpose(flat, (1, 2, 0, 3)).reshape(w_spatial.shape).astype(F32) / SCALE
    sums = copies_out(halves, early)
    late = [shards["reduce", 0], shards["expand", 0]] + ([] if short else got)
    lates = copies_out(copies_sum(copies_halves(late), dp), late)
    head_grad = sums[0]
    reduce_all = jnp.stack([lates[0]] + sums[1:blocks])
    expand_all = jnp.stack([lates[1]] + sums[blocks:])
    if not short:
        spatial = jnp.stack(lates[2:])
    at = [(place, size) for place, size in zip(offsets, sizes)]

    def gains(pair):
        btot, tot = pair
        mu = tot[0] / live_count
        var = jnp.maximum(tot[1] / live_count - mu * mu, 0.0)
        return (btot[1] - mu * btot[0]) * lax.rsqrt(var + EPS) / SCALE

    return (
        jnp.transpose(trunk, (1, 0, 2)),
        jnp.transpose(grad_features, (1, 0, 2)),
        reduce_all,
        spatial,
        expand_all,
        jnp.stack([jnp.stack([gains(p) for p in pairs]) for pairs in sums_mid]),
        jnp.stack([jnp.stack([p[0][0] / SCALE for p in pairs]) for pairs in sums_mid]),
        jnp.stack([gains(p) for p in sums_out]),
        jnp.stack([p[0][0] / SCALE for p in sums_out]),
    ) + tuple(head_grad[place : place + size].T for place, size in at)


def solution(mesh):
    split = P(AXES)
    rows = P(None, "fsdp", None)
    head = P("fsdp", None)
    in_specs = (
        P(AXES, None, None), split, rows, rows, rows, P(), P(), P(), P(),
        head, head, head, split, split, split, P(AXES, None),
    )
    out_specs = (
        P(AXES, None, None), P(AXES, None, None), rows, rows, rows, P(), P(), P(), P(), head, head, head,
    )
    body = functools.partial(on_device, mesh.shape["dp"], mesh.shape["fsdp"])
    return jax.shard_map(body, mesh=mesh, in_specs=in_specs, out_specs=out_specs, check_vma=False)
```

```python
import functools

import jax
import jax.numpy as jnp
from jax import lax
from jax.experimental import pallas as pl
from jax.experimental.pallas import tpu as pltpu
from jax.sharding import PartitionSpec as P

SIDE = 7
TAPS = 3
EPS = 1e-05
FLOOR = 0.05
WIDTH = 0.1
SCALE = 256.0
BF = jnp.bfloat16
F32 = jnp.float32
VMEM_LIMIT = 56 * 1024 * 1024
AXES = ("dp", "fsdp")


def nn(left, right):
    return jnp.dot(left, right, preferred_element_type=F32)


def nt(left, right):
    return lax.dot_general(left, right, (((1,), (1,)), ((), ())), preferred_element_type=F32)


def tn(left, right):
    return lax.dot_general(left, right, (((0,), (0,)), ((), ())), preferred_element_type=F32)


def sigmoid(v):
    return 0.5 * jnp.tanh(0.5 * v) + 0.5


def silu_half(u):
    return u * jnp.tanh(u) + u


def slope_twice(u):
    t = jnp.tanh(u)
    return (1.0 + t) * (1.0 + u * (1.0 - t))


def rowsum(v):
    return jnp.sum(v, axis=0, keepdims=True)


def params(n_grid):
    return pltpu.CompilerParams(
        dimension_semantics=("arbitrary",) * n_grid, vmem_limit_bytes=VMEM_LIMIT
    )


def whole(shape):
    zeros = (0,) * len(shape)
    return pl.BlockSpec(shape, lambda *g: zeros)


def tile(rows, cols):
    return pl.BlockSpec((rows, cols), lambda j: (j, 0))


def sds(shape, dtype):
    return jax.ShapeDtypeStruct(shape, dtype)


def cost(flops, nbytes, trans=0):
    return pl.CostEstimate(flops=int(flops), bytes_accessed=int(nbytes), transcendentals=int(trans))


def forward_consts(tot, inv, gb):
    mu = tot[0:1, :] * inv
    var = jnp.maximum(tot[1:2, :] * inv - mu * mu, 0.0)
    rstd = lax.rsqrt(var + EPS)
    a = rstd * gb[0:1, :]
    return mu, rstd, a, gb[1:2, :] - mu * a


def backward_consts(mu, rstd, a, btot, inv):
    ex = (btot[1:2, :] - mu * btot[0:1, :]) * rstd * inv
    c1 = -a * rstd * ex
    c0 = -a * btot[0:1, :] * inv - c1 * mu
    return c1, c0


def clear_at_first(*refs):
    @pl.when(pl.program_id(0) == 0)
    def _():
        for ref in refs:
            ref[...] = jnp.zeros_like(ref)


def add_stats(st, top, low, cols=slice(None)):
    st[0:1, cols] += top
    st[1:2, cols] += low


class Shape:
    def __init__(self, images):
        self.images = images
        self.main = images // 16 * 16
        self.rest = images - self.main
        self.top = SIDE * self.main
        self.low = (SIDE + 1) * self.rest
        self.rows = self.top + self.low
        self.total = SIDE * self.rows
        self.step = self.total // 4
        self.half = self.total // 2
        self.padded = self.main + 16


def prep_kernel(sh, f, mask, x, scr):
    channels = x.shape[1]
    scr[...] = jnp.zeros_like(scr)
    for s in range(SIDE):
        x[s * sh.main : (s + 1) * sh.main, :] = (
            f[s, 0 : sh.main, :].astype(F32) * mask[s * sh.main : (s + 1) * sh.main, :]
        ).astype(BF)
        scr[s * sh.rest : (s + 1) * sh.rest, :] = f[s, sh.main : sh.images, :].astype(F32)
    x[sh.top : sh.rows, :] = jnp.where(mask[sh.top : sh.rows, :] > 0.0, scr[...], 0.0).astype(BF)


def prep(sh, features, mask):
    channels = features.shape[2]
    return pl.pallas_call(
        functools.partial(prep_kernel, sh),
        grid=(SIDE,),
        in_specs=[
            pl.BlockSpec((SIDE, sh.images, channels), lambda j: (j, 0, 0)),
            tile(sh.rows, 1),
        ],
        out_specs=tile(sh.rows, channels),
        out_shape=sds((sh.total, channels), BF),
        scratch_shapes=[pltpu.VMEM((sh.low, channels), F32)],
        compiler_params=params(1),
        name="prep",
    )(features, mask)


def reduce_kernel(x, w, h, st):
    clear_at_first(st)
    acc = nn(x[...], w[...])
    h[...] = acc
    add_stats(st, rowsum(acc), rowsum(acc * acc))


def reduce_conv(sh, x, w):
    c, m = w.shape
    return pl.pallas_call(
        reduce_kernel,
        grid=(sh.total // sh.step,),
        in_specs=[tile(sh.step, c), whole((c, m))],
        out_specs=[tile(sh.step, m), whole((2, m))],
        out_shape=[sds((sh.total, m), F32), sds((2, m), F32)],
        compiler_params=params(1),
        cost_estimate=cost(2 * sh.total * c * m, 2 * sh.total * c + 4 * sh.total * m),
        name="reduce_conv",
    )(x, w)


def shifted(sh, v, scr):
    m = v.shape[1]
    gap = jnp.zeros((sh.main, m), F32)
    scr[8 : 8 + sh.low, :] = v[sh.top :, :]
    before = jnp.concatenate([gap, v[: sh.top - sh.main, :], scr[8 - sh.rest : 8 - sh.rest + sh.low, :]], axis=0)
    after = jnp.concatenate([v[sh.main : sh.top, :], gap, scr[8 + sh.rest : 8 + sh.rest + sh.low, :]], axis=0)
    return before, v, after


def put_shifted(sh, v, scr, pat, row):
    m = v.shape[1]
    at = pl.ds(pl.multiple_of(row * sh.rows, sh.rows), sh.rows)
    for k, part in enumerate(shifted(sh, v, scr)):
        pat[at, k * m : (k + 1) * m] = part.astype(BF)


def spatial_kernel(sh, inv, h1, tot, gb, mask, mask_out, w, act, h2, st, pat, scr):
    j = pl.program_id(0)
    m = h1.shape[1]

    clear_at_first(pat, scr, st)
    mu, rstd, a, b = forward_consts(tot, inv[0, 0], gb)
    acc = None
    for k in range(2):
        at = pl.ds(pl.multiple_of((j + k) * sh.rows, sh.rows), sh.rows)
        part = nn(pat[at, :], w[k * TAPS * m : (k + 1) * TAPS * m, :])
        acc = part if acc is None else acc + part
    y = mask[...] * silu_half(h1[...] * (0.5 * a) + 0.5 * b)
    act[...] = y.astype(BF)
    put_shifted(sh, jnp.where(j < SIDE, y, 0.0), scr, pat, j + 2)
    at = pl.ds(pl.multiple_of((j + 2) * sh.rows, sh.rows), sh.rows)
    acc = acc + nn(pat[at, :], w[2 * TAPS * m :, :])
    h2[...] = acc
    got = jnp.where(j > 0, mask_out[...], 0.0) * acc
    add_stats(st, rowsum(got), rowsum(got * acc))


def spatial_conv(sh, h1, tot, inv, gb, mask, w):
    m = h1.shape[1]
    into = lambda j: (jnp.minimum(j, SIDE - 1), 0)
    outof = lambda j: (jnp.maximum(j - 1, 0), 0)
    return pl.pallas_call(
        functools.partial(spatial_kernel, sh),
        grid=(SIDE + 1,),
        in_specs=[
            pl.BlockSpec(memory_space=pltpu.SMEM),
            pl.BlockSpec((sh.rows, m), into),
            whole((2, m)),
            whole((2, m)),
            pl.BlockSpec((sh.rows, 1), into),
            pl.BlockSpec((sh.rows, 1), outof),
            whole(w.shape),
        ],
        out_specs=[
            pl.BlockSpec((sh.rows, m), into),
            pl.BlockSpec((sh.rows, m), outof),
            whole((2, m)),
        ],
        out_shape=[sds((sh.total, m), BF), sds((sh.total, m), F32), sds((2, m), F32)],
        scratch_shapes=[
            pltpu.VMEM(((SIDE + 3) * sh.rows, TAPS * m), BF),
            pltpu.VMEM((sh.low + 16, m), F32),
        ],
        compiler_params=params(1),
        cost_estimate=cost(2 * sh.total * w.size, 2 * w.size + 10 * sh.total * m),
        name="spatial_conv",
    )(inv, h1, tot, gb, mask, mask, w)


def expand_kernel(inv, h2, tot, gb, mask, w, act, h3, st):
    clear_at_first(st)
    mu, rstd, a, b = forward_consts(tot, inv[0, 0], gb)
    y = (mask[...] * silu_half(h2[...] * (0.5 * a) + 0.5 * b)).astype(BF)
    act[...] = y
    step = 512
    for c in range(0, w.shape[1], step):
        cols = slice(c, c + step)
        acc = nn(y, w[:, cols])
        h3[:, cols] = acc.astype(BF)
        add_stats(st, rowsum(acc), rowsum(acc * acc), cols)


def expand_conv(sh, h2, tot, inv, gb, mask, w):
    m, c = w.shape
    return pl.pallas_call(
        expand_kernel,
        grid=(sh.total // sh.step,),
        in_specs=[
            pl.BlockSpec(memory_space=pltpu.SMEM),
            tile(sh.step, m),
            whole((2, m)),
            whole((2, m)),
            tile(sh.step, 1),
            whole((m, c)),
        ],
        out_specs=[tile(sh.step, m), tile(sh.step, c), whole((2, c))],
        out_shape=[sds((sh.total, m), BF), sds((sh.total, c), BF), sds((2, c), F32)],
        compiler_params=params(1),
        cost_estimate=cost(2 * sh.total * c * m, 2 * sh.total * c + 6 * sh.total * m),
        name="expand_conv",
    )(inv, h2, tot, gb, mask, w)


def join_kernel(inv, h3, x, tot, gb, mask, w, y, h1, st):
    clear_at_first(st)
    mu, rstd, a, b = forward_consts(tot, inv[0, 0], gb)
    step = 512
    acc = None
    for c in range(0, x.shape[1], step):
        cols = slice(c, c + step)
        v = h3[:, cols].astype(F32) * a[:, cols] + b[:, cols] + x[:, cols].astype(F32)
        out = (mask[...] * silu_half(0.5 * v)).astype(BF)
        y[:, cols] = out
        part = nn(out, w[cols, :])
        acc = part if acc is None else acc + part
    h1[...] = acc
    add_stats(st, rowsum(acc), rowsum(acc * acc))


def join(sh, h3, x, tot, inv, gb, mask, w):
    c, m = w.shape
    return pl.pallas_call(
        join_kernel,
        grid=(sh.total // sh.step,),
        in_specs=[
            pl.BlockSpec(memory_space=pltpu.SMEM),
            tile(sh.step, c),
            tile(sh.step, c),
            whole((2, c)),
            whole((2, c)),
            tile(sh.step, 1),
            whole((c, m)),
        ],
        out_specs=[tile(sh.step, c), tile(sh.step, m), whole((2, m))],
        out_shape=[sds((sh.total, c), BF), sds((sh.total, m), F32), sds((2, m), F32)],
        compiler_params=params(1),
        cost_estimate=cost(2 * sh.total * c * m, 6 * sh.total * c + 4 * sh.total * m),
        name="join",
    )(inv, h3, x, tot, gb, mask, w)


def last_kernel(sh, inv, h3, x, tot, gb, mask, area, pick, trunk, pooled, sums, scr):
    j = pl.program_id(0)
    clear_at_first(sums)
    mu, rstd, a, b = forward_consts(tot, inv[0, 0], gb)
    step = 512
    for c in range(0, x.shape[1], step):
        cols = slice(c, c + step)
        v = h3[:, cols].astype(F32) * a[:, cols] + b[:, cols] + x[:, cols].astype(F32)
        out = mask[...] * silu_half(0.5 * v)
        low = out.astype(BF)
        scr[:, cols] = out[sh.top :, :]
        for s in range(SIDE):
            trunk[s, 0 : sh.main, cols] = low[s * sh.main : (s + 1) * sh.main, :]
            trunk[s, sh.main : sh.images, cols] = scr[s * sh.rest : (s + 1) * sh.rest, cols].astype(BF)
        sums[:, cols] += nn(pick[...], low)

    @pl.when(j == SIDE - 1)
    def _():
        pooled[...] = (sums[...] / area[...]).astype(BF)


def last_join(sh, h3, x, tot, inv, gb, mask, area, pick):
    c = x.shape[1]
    return pl.pallas_call(
        functools.partial(last_kernel, sh),
        grid=(SIDE,),
        in_specs=[
            pl.BlockSpec(memory_space=pltpu.SMEM),
            tile(sh.rows, c),
            tile(sh.rows, c),
            whole((2, c)),
            whole((2, c)),
            tile(sh.rows, 1),
            whole((sh.padded, 1)),
            whole((sh.padded, sh.rows)),
        ],
        out_specs=[
            pl.BlockSpec((SIDE, sh.images, c), lambda j: (j, 0, 0)),
            whole((sh.padded, c)),
        ],
        out_shape=[sds((SIDE * SIDE, sh.images, c), BF), sds((sh.padded, c), BF)],
        scratch_shapes=[pltpu.VMEM((sh.padded, c), F32), pltpu.VMEM((sh.low, c), F32)],
        compiler_params=params(1),
        cost_estimate=cost(2 * sh.padded * sh.total * c, 6 * sh.total * c),
        name="last_join",
    )(inv, h3, x, tot, gb, mask, area, pick)


def heads_kernel(sizes, offsets, pooled, labels, area, bits, w, merged, out):
    rows = pooled.shape[0]
    out[...] = jnp.zeros_like(out)
    summed = None
    at = 0
    for t, (classes, place) in enumerate(zip(sizes, offsets)):
        span = -(-classes // 16) * 16
        wt = w[at : at + span, :]
        at += span
        logits = nt(pooled[...], wt)
        index = lax.broadcasted_iota(jnp.int32, (rows, span), 1)
        inside = index < classes
        logits = jnp.where(inside, logits, -1e30)
        top = jnp.max(logits, axis=1, keepdims=True)
        ex = jnp.where(inside, jnp.exp(logits - top), 0.0)
        probs = ex / jnp.sum(ex, axis=1, keepdims=True)
        targets = jnp.where(index == labels[:, t : t + 1], 1.0, 0.0)
        grad = (SCALE * (probs - targets)).astype(BF)
        out[:, place : place + span] = grad
        single = nn(grad, wt) / area[...]
        size = jnp.sqrt(single * single + FLOOR * FLOOR)
        summed = single if summed is None else summed + single
        magnitude = size if t == 0 else magnitude + size
    purity = 0.5 * (1.0 + summed / magnitude)
    level = (bits[...].astype(F32) + 0.5) / 32768.0
    keep = sigmoid((purity - level) / WIDTH)
    merged[...] = 0.5 * summed + (keep - 0.5) * magnitude


def heads(pooled, labels, area, bits, w, sizes, offsets, span):
    rows, c = pooled.shape
    return pl.pallas_call(
        functools.partial(heads_kernel, sizes, offsets),
        out_shape=[sds((rows, c), F32), sds((rows, span), BF)],
        compiler_params=pltpu.CompilerParams(vmem_limit_bytes=VMEM_LIMIT),
        cost_estimate=cost(4 * rows * c * span, 2 * w.size),
        name="heads",
    )(pooled, labels, area, bits, w)


def top_grad_kernel(sh, inv, merged, h3, x, tot, gb, mask, e3, st, scr):
    j = pl.program_id(0)
    clear_at_first(st)

    @pl.when(j == 0)
    def _():
        for s in range(SIDE + 1):
            scr[s * sh.rest : (s + 1) * sh.rest, :] = merged[sh.main : sh.images, :]

    half = 0.5 * mask[...]
    mu, rstd, a, b = forward_consts(tot, inv[0, 0], gb)
    step = 256
    for c in range(0, x.shape[1], step):
        cols = slice(c, c + step)
        h = h3[:, cols].astype(F32)
        v = h * a[:, cols] + b[:, cols] + x[:, cols].astype(F32)
        up = jnp.concatenate([merged[0 : sh.main, cols]] * SIDE + [scr[:, cols]], axis=0)
        e = half * up * slope_twice(0.5 * v)
        e3[:, cols] = e.astype(BF)
        add_stats(st, rowsum(e), rowsum(e * h), cols)


def top_grad(sh, merged, h3, x, tot, inv, gb, mask):
    c = x.shape[1]
    return pl.pallas_call(
        functools.partial(top_grad_kernel, sh),
        grid=(SIDE,),
        in_specs=[
            pl.BlockSpec(memory_space=pltpu.SMEM),
            whole(merged.shape),
            tile(sh.rows, c),
            tile(sh.rows, c),
            whole((2, c)),
            whole((2, c)),
            tile(sh.rows, 1),
        ],
        out_specs=[tile(sh.rows, c), whole((2, c))],
        out_shape=[sds((sh.total, c), BF), sds((2, c), F32)],
        scratch_shapes=[pltpu.VMEM((sh.low, c), F32)],
        compiler_params=params(1),
        cost_estimate=cost(20 * sh.total * c, 6 * sh.total * c),
        name="top_grad",
    )(inv, merged, h3, x, tot, gb, mask)


def expand_back_kernel(inv, e3, h3, tot3, gb3, btot3, mask, w, h2, tot2, gb2, g3, e2, st):
    clear_at_first(st)
    mu, rstd, a, b = forward_consts(tot3, inv[0, 0], gb3)
    c1, c0 = backward_consts(mu, rstd, a, btot3, inv[0, 0])
    step = 512
    acc = None
    for c in range(0, e3.shape[1], step):
        cols = slice(c, c + step)
        g = a[:, cols] * e3[:, cols].astype(F32) + c1[:, cols] * h3[:, cols].astype(F32) + c0[:, cols]
        g = (mask[...] * g).astype(BF)
        g3[:, cols] = g
        part = nt(g, w[:, cols])
        acc = part if acc is None else acc + part
    mu, rstd, a, b = forward_consts(tot2, inv[0, 0], gb2)
    h = h2[...]
    e = acc * (0.5 * slope_twice(h * (0.5 * a) + 0.5 * b))
    e2[...] = e
    add_stats(st, rowsum(e), rowsum(e * h))


def expand_back(sh, e3, h3, tot3, gb3, btot3, inv, mask, w, h2, tot2, gb2):
    m, c = w.shape
    return pl.pallas_call(
        expand_back_kernel,
        grid=(sh.total // sh.half,),
        in_specs=[
            pl.BlockSpec(memory_space=pltpu.SMEM),
            tile(sh.half, c),
            tile(sh.half, c),
            whole((2, c)),
            whole((2, c)),
            whole((2, c)),
            tile(sh.half, 1),
            whole((m, c)),
            tile(sh.half, m),
            whole((2, m)),
            whole((2, m)),
        ],
        out_specs=[tile(sh.half, c), tile(sh.half, m), whole((2, m))],
        out_shape=[sds((sh.total, c), BF), sds((sh.total, m), F32), sds((2, m), F32)],
        compiler_params=params(1),
        cost_estimate=cost(2 * sh.total * c * m, 6 * sh.total * c + 8 * sh.total * m),
        name="expand_back",
    )(inv, e3, h3, tot3, gb3, btot3, mask, w, h2, tot2, gb2)


def spatial_back_kernel(
    sh, inv, e2, h2, tot2, gb2, btot2, mask, mask_out, w, h1, tot1, gb1, g2, e1, st, pat, scr
):
    j = pl.program_id(0)
    m = e2.shape[1]

    clear_at_first(pat, scr, st)

    def taps(k):
        at = pl.ds(pl.multiple_of((j + k) * sh.rows, sh.rows), sh.rows)
        total = None
        for l in range(TAPS):
            tap = TAPS * (2 - k) + (2 - l)
            part = nt(pat[at, l * m : (l + 1) * m], w[tap * m : (tap + 1) * m, :])
            total = part if total is None else total + part
        return total

    acc = taps(0) + taps(1)
    mu, rstd, a, b = forward_consts(tot2, inv[0, 0], gb2)
    c1, c0 = backward_consts(mu, rstd, a, btot2, inv[0, 0])
    g = mask[...] * (a * e2[...] + c1 * h2[...] + c0)
    g2[...] = g.astype(BF)
    put_shifted(sh, jnp.where(j < SIDE, g, 0.0), scr, pat, j + 2)
    acc = acc + taps(2)
    mu, rstd, a, b = forward_consts(tot1, inv[0, 0], gb1)
    h = h1[...]
    e = jnp.where(j > 0, 0.5 * mask_out[...], 0.0) * acc * slope_twice(h * (0.5 * a) + 0.5 * b)
    e1[...] = e
    add_stats(st, rowsum(e), rowsum(e * h))


def spatial_back(sh, e2, h2, tot2, gb2, btot2, inv, mask, w, h1, tot1, gb1):
    m = e2.shape[1]
    into = lambda j: (jnp.minimum(j, SIDE - 1), 0)
    outof = lambda j: (jnp.maximum(j - 1, 0), 0)
    return pl.pallas_call(
        functools.partial(spatial_back_kernel, sh),
        grid=(SIDE + 1,),
        in_specs=[
            pl.BlockSpec(memory_space=pltpu.SMEM),
            pl.BlockSpec((sh.rows, m), into),
            pl.BlockSpec((sh.rows, m), into),
            whole((2, m)),
            whole((2, m)),
            whole((2, m)),
            pl.BlockSpec((sh.rows, 1), into),
            pl.BlockSpec((sh.rows, 1), outof),
            whole(w.shape),
            pl.BlockSpec((sh.rows, m), outof),
            whole((2, m)),
            whole((2, m)),
        ],
        out_specs=[
            pl.BlockSpec((sh.rows, m), into),
            pl.BlockSpec((sh.rows, m), outof),
            whole((2, m)),
        ],
        out_shape=[sds((sh.total, m), BF), sds((sh.total, m), F32), sds((2, m), F32)],
        scratch_shapes=[
            pltpu.VMEM(((SIDE + 3) * sh.rows, TAPS * m), BF),
            pltpu.VMEM((sh.low + 16, m), F32),
        ],
        compiler_params=params(1),
        cost_estimate=cost(2 * sh.total * w.size, 2 * w.size + 18 * sh.total * m),
        name="spatial_back",
    )(inv, e2, h2, tot2, gb2, btot2, mask, mask, w, h1, tot1, gb1)


def reduce_back_kernel(
    inv, e1, h1, tot1, gb1, btot1, mask, w, e3, h3, x, tot3, gb3, g1, down, st
):
    clear_at_first(st)
    mu, rstd, a, b = forward_consts(tot1, inv[0, 0], gb1)
    c1, c0 = backward_consts(mu, rstd, a, btot1, inv[0, 0])
    g = (mask[...] * (a * e1[...] + c1 * h1[...] + c0)).astype(BF)
    g1[...] = g
    mu, rstd, a, b = forward_consts(tot3, inv[0, 0], gb3)
    step = 256
    for c in range(0, x.shape[1], step):
        cols = slice(c, c + step)
        up = nt(g, w[cols, :]) + e3[:, cols].astype(F32)
        h = h3[:, cols].astype(F32)
        v = h * a[:, cols] + b[:, cols] + x[:, cols].astype(F32)
        e = up * (0.5 * slope_twice(0.5 * v))
        down[:, cols] = e.astype(BF)
        add_stats(st, rowsum(e), rowsum(e * h), cols)


def reduce_back(sh, e1, h1, tot1, gb1, btot1, inv, mask, w, e3, h3, x, tot3, gb3):
    c, m = w.shape
    return pl.pallas_call(
        reduce_back_kernel,
        grid=(sh.total // sh.step,),
        in_specs=[
            pl.BlockSpec(memory_space=pltpu.SMEM),
            tile(sh.step, m),
            tile(sh.step, m),
            whole((2, m)),
            whole((2, m)),
            whole((2, m)),
            tile(sh.step, 1),
            whole((c, m)),
            tile(sh.step, c),
            tile(sh.step, c),
            tile(sh.step, c),
            whole((2, c)),
            whole((2, c)),
        ],
        out_specs=[tile(sh.step, m), tile(sh.step, c), whole((2, c))],
        out_shape=[sds((sh.total, m), BF), sds((sh.total, c), BF), sds((2, c), F32)],
        compiler_params=params(1),
        cost_estimate=cost(2 * sh.total * c * m, 8 * sh.total * c + 10 * sh.total * m),
        name="reduce_back",
    )(inv, e1, h1, tot1, gb1, btot1, mask, w, e3, h3, x, tot3, gb3)


def features_back_kernel(sh, inv, e1, h1, tot1, gb1, btot1, mask, w, e3, out, scr):
    mu, rstd, a, b = forward_consts(tot1, inv[0, 0], gb1)
    c1, c0 = backward_consts(mu, rstd, a, btot1, inv[0, 0])
    g = (mask[...] * (a * e1[...] + c1 * h1[...] + c0)).astype(BF)
    step = 512
    for c in range(0, w.shape[0], step):
        cols = slice(c, c + step)
        up = nt(g, w[cols, :]) + e3[:, cols].astype(F32)
        scr[:, cols] = up[sh.top :, :]
        for s in range(SIDE):
            out[s, 0 : sh.main, cols] = up[s * sh.main : (s + 1) * sh.main, :]
            out[s, sh.main : sh.images, cols] = scr[s * sh.rest : (s + 1) * sh.rest, cols]


def features_back(sh, e1, h1, tot1, gb1, btot1, inv, mask, w, e3):
    c, m = w.shape
    return pl.pallas_call(
        functools.partial(features_back_kernel, sh),
        grid=(SIDE,),
        in_specs=[
            pl.BlockSpec(memory_space=pltpu.SMEM),
            tile(sh.rows, m),
            tile(sh.rows, m),
            whole((2, m)),
            whole((2, m)),
            whole((2, m)),
            tile(sh.rows, 1),
            whole((c, m)),
            tile(sh.rows, c),
        ],
        out_specs=pl.BlockSpec((SIDE, sh.images, c), lambda j: (j, 0, 0)),
        out_shape=sds((SIDE * SIDE, sh.images, c), F32),
        scratch_shapes=[pltpu.VMEM((sh.low, c), F32)],
        compiler_params=params(1),
        cost_estimate=cost(2 * sh.total * c * m, 6 * sh.total * c + 10 * sh.total * m),
        name="features_back",
    )(inv, e1, h1, tot1, gb1, btot1, mask, w, e3)


def wgrad_kernel(left, right, out):
    out[...] = tn(left[...], right[...]).astype(BF)


def wgrad(left, right, step):
    rows, a = left.shape
    b = right.shape[1]
    by_left = a >= b
    if by_left:
        specs = [pl.BlockSpec((rows, step), lambda j: (0, j)), whole((rows, b))]
        out_spec = pl.BlockSpec((step, b), lambda j: (j, 0))
    else:
        specs = [whole((rows, a)), pl.BlockSpec((rows, step), lambda j: (0, j))]
        out_spec = pl.BlockSpec((a, step), lambda j: (0, j))
    return pl.pallas_call(
        wgrad_kernel,
        grid=(max(a, b) // step,),
        in_specs=specs,
        out_specs=out_spec,
        out_shape=sds((a, b), BF),
        compiler_params=params(1),
        cost_estimate=cost(2 * rows * a * b, 2 * (rows * (a + b) + a * b)),
        name="wgrad",
    )(left, right)


def reduce_wgrad_kernel(inv, e1, h1, tot1, gb1, btot1, mask, x, out, acc):
    clear_at_first(acc)
    mu, rstd, a, b = forward_consts(tot1, inv[0, 0], gb1)
    c1, c0 = backward_consts(mu, rstd, a, btot1, inv[0, 0])
    g = (mask[...] * (a * e1[...] + c1 * h1[...] + c0)).astype(BF)
    step = 512
    for c in range(0, x.shape[1], step):
        acc[c : c + step, :] += tn(x[:, c : c + step], g)

    @pl.when(pl.program_id(0) == pl.num_programs(0) - 1)
    def _():
        out[...] = acc[...].astype(BF)


def reduce_wgrad(sh, e1, h1, tot1, gb1, btot1, inv, mask, x):
    c, m = x.shape[1], e1.shape[1]
    return pl.pallas_call(
        reduce_wgrad_kernel,
        grid=(sh.total // sh.step,),
        in_specs=[
            pl.BlockSpec(memory_space=pltpu.SMEM),
            tile(sh.step, m),
            tile(sh.step, m),
            whole((2, m)),
            whole((2, m)),
            whole((2, m)),
            tile(sh.step, 1),
            tile(sh.step, c),
        ],
        out_specs=whole((c, m)),
        out_shape=sds((c, m), BF),
        scratch_shapes=[pltpu.VMEM((c, m), F32)],
        compiler_params=params(1),
        cost_estimate=cost(2 * sh.total * c * m, 2 * sh.total * c + 8 * sh.total * m),
        name="reduce_wgrad",
    )(inv, e1, h1, tot1, gb1, btot1, mask, x)


def put_owned(place, val, outs, first):
    dps, chips, rows, width = outs[0].shape
    last, at = first + val.shape[0], first
    while at < last:
        chip, start = at // (2 * rows), at % (2 * rows)
        stop = min(2 * rows, start + last - at)
        for side in range(2):
            low, high = max(start, side * rows), min(stop, (side + 1) * rows)
            if low >= high:
                continue
            source = pl.ds(at - first + low - start, high - low)
            for q in range(dps):
                piece = val[source, q * width : (q + 1) * width]
                for e, out in enumerate(outs):

                    @pl.when((place[0, 1] & 1) == (side ^ e))
                    def _(piece=piece, out=out, low=low, high=high, q=q):
                        out[q ^ place[0, 0], chip ^ (place[0, 1] >> 1), low - side * rows : high - side * rows, :] = piece
        at += stop - start


def spatial_wgrad_kernel(sh, owned, place, act, g, *rest):
    *outs, pat, scr, val = rest
    j = pl.program_id(0)
    m = act.shape[1]

    @pl.when(j == 0)
    def _():
        scr[...] = jnp.zeros_like(scr)
        pat[0 : sh.rows, :] = jnp.zeros((sh.rows, TAPS * m), BF)
        pat[(SIDE + 1) * sh.rows :, :] = jnp.zeros((sh.rows, TAPS * m), BF)
        for r in range(SIDE):
            put_shifted(sh, act[r * sh.rows : (r + 1) * sh.rows, :].astype(F32), scr, pat, r + 1)

    for k in range(TAPS):

        @pl.when(j == k)
        def _(k=k):
            rows = slice(k * sh.rows, (k + SIDE) * sh.rows)
            for l in range(TAPS):
                into = val if owned else outs[0]
                into[l * m : (l + 1) * m, :] = tn(pat[rows, l * m : (l + 1) * m], g[...]).astype(BF)
            if owned:
                put_owned(place, val, outs, k * TAPS * m)


def spatial_wgrad(sh, act, g, place, owners, dp, owned):
    m = act.shape[1]
    rows = TAPS * TAPS * m
    owned_shape = (dp, owners // 2, rows // owners, m // dp)
    return pl.pallas_call(
        functools.partial(spatial_wgrad_kernel, sh, owned),
        grid=(TAPS,),
        in_specs=[pl.BlockSpec(memory_space=pltpu.SMEM), whole(act.shape), whole(g.shape)],
        out_specs=[whole(owned_shape)] * 2 if owned else [pl.BlockSpec((TAPS * m, m), lambda j: (j, 0))],
        out_shape=[sds(owned_shape, BF)] * 2 if owned else [sds((rows, m), BF)],
        scratch_shapes=[
            pltpu.VMEM(((SIDE + 2) * sh.rows, TAPS * m), BF),
            pltpu.VMEM((sh.low + 16, m), F32),
            pltpu.VMEM((TAPS * m, m), BF),
        ],
        compiler_params=params(1),
        cost_estimate=cost(18 * sh.total * m * m, 4 * sh.total * m + 18 * m * m),
        name="spatial_wgrad",
    )(place, act, g)


def assemble_kernel(place, own, mate, out, sem):
    dps, chips, rows, width = own.shape
    copies = []
    for e, src in enumerate((own, mate)):
        for j in range(dps):
            for k in range(chips):
                owner = place[0, 1] ^ (2 * k + e)
                row = pl.multiple_of(owner * rows, rows)
                col = pl.multiple_of((place[0, 0] ^ j) * width, width)
                copies.append(
                    pltpu.make_async_copy(
                        src.at[j, k],
                        out.at[pl.ds(row, rows), pl.ds(col, width)],
                        sem.at[len(copies)],
                    )
                )
    for copy in copies:
        copy.start()
    for copy in copies:
        copy.wait()


def assemble(place, own, mate):
    dps, chips, rows, width = own.shape
    anywhere = pl.BlockSpec(memory_space=pl.ANY)
    return pl.pallas_call(
        assemble_kernel,
        in_specs=[pl.BlockSpec(memory_space=pltpu.SMEM), anywhere, anywhere],
        out_specs=pl.BlockSpec(memory_space=pltpu.VMEM),
        out_shape=sds((2 * chips * rows, dps * width), BF),
        scratch_shapes=[pltpu.SemaphoreType.DMA((2 * dps * chips,))],
        compiler_params=pltpu.CompilerParams(vmem_limit_bytes=VMEM_LIMIT),
        cost_estimate=cost(0, 8 * own.size),
        name="assemble",
    )(place, own, mate)


def flips(v, axis, size, unit):
    return [v] + [
        lax.ppermute(v, axis, [(i, i ^ (unit * k)) for i in range(size)]) for k in range(1, size // unit)
    ]


def others(v, axis, size, unit):
    turns = size // unit
    ways = [
        [(i, (i // unit + d) % turns * unit + i % unit) for i in range(size)]
        for d in range(1, turns)
    ]
    return sum([lax.ppermute(v, axis, way) for way in ways], v)


def total_of(v, sizes, beside=False):
    dp, fsdp = sizes
    flat = v.reshape(8, -1)
    if flat.size > 2048 and not beside:
        flat = flat + lax.ppermute(flat, "fsdp", [(i, i ^ 1) for i in range(fsdp)])
        flat = others(flat, "fsdp", fsdp, 2)
        return others(flat, "dp", dp, 1).reshape(v.shape)
    devices = dp * fsdp
    spread = jnp.broadcast_to(flat[None], (devices,) + flat.shape)
    got = lax.all_to_all(spread, AXES, 0, 0, tiled=True)
    return jnp.sum(got, axis=0).reshape(v.shape)


def added(*terms):
    return sum([v.astype(F32) for v in terms[1:]], terms[0].astype(F32)).astype(BF)


def copies_halves(arrays):
    flat = [v.reshape(-1, 512) for v in arrays]
    flat = jnp.concatenate(flat, axis=0) if len(flat) > 1 else flat[0]
    cut = flat.shape[0] // 32 * 16
    return [flat[:cut], flat[cut:]]


def copies_swap(halves, dp, turn):
    bits = [1 << k for k in range(dp.bit_length() - 1)]
    return [
        lax.ppermute(half, "dp", [(i, i ^ (bits, bits[::-1])[h][turn]) for i in range(dp)])
        for h, half in enumerate(halves)
    ]


def copies_add(halves, got):
    return [added(half, other) for half, other in zip(halves, got)]


def copies_sum(halves, dp, first=0):
    for turn in range(first, dp.bit_length() - 1):
        halves = copies_add(halves, copies_swap(halves, dp, turn))
    return halves


def swap_core(parts, owners):
    return lax.ppermute(parts[1], "fsdp", [(i, i ^ 1) for i in range(owners)])


def swap_rest(blocks, axis, size, unit):
    return [
        lax.ppermute(blocks[k], axis, [(i, i ^ (unit * k)) for i in range(size)])
        for k in range(1, len(blocks))
    ]


def copies_out(halves, arrays):
    flat = jnp.concatenate(halves, axis=0).astype(F32) / SCALE
    out, at = [], 0
    for v in arrays:
        rows = v.size // 512
        out.append(flat[at : at + rows].reshape(v.shape))
        at += rows
    return out


def on_device(
    dp,
    owners,
    features,
    grid_size,
    w_reduce,
    w_spatial,
    w_expand,
    gain_mid,
    bias_mid,
    gain_out,
    bias_out,
    head_a,
    head_b,
    head_c,
    label_a,
    label_b,
    label_c,
    drop_bits,
):
    images, _, channels = features.shape
    inner = w_reduce.shape[2]
    blocks = w_reduce.shape[0]
    sh = Shape(images)

    gather = functools.partial(lax.all_gather, axis_name="fsdp", axis=0, tiled=True)
    weights = [
        (
            gather(w_reduce[b]),
            None if b == 0 and owners == 8 and dp == 4 else gather(w_spatial[b]),
            gather(w_expand[b]),
        )
        for b in range(blocks)
    ]
    sizes = [head.shape[1] for head in (head_a, head_b, head_c)]
    spans = [-(-size // 16) * 16 for size in sizes]
    lanes = [-(-size // 128) * 128 for size in sizes]
    offsets = [0, lanes[0], lanes[0] + lanes[1]]
    head_t = jnp.concatenate(
        [
            jnp.pad(head.T, ((0, span - size), (0, 0)))
            for head, size, span in zip((head_a, head_b, head_c), sizes, spans)
        ],
        axis=0,
    )
    head_all = lax.all_gather(head_t, "fsdp", axis=1, tiled=True)

    steps = jnp.arange(SIDE + 1, dtype=jnp.int32)
    bound = grid_size
    row_ok = steps[:SIDE, None, None] < bound[None, None, :]
    col_ok = steps[None, :, None] < bound[None, None, :]
    alive = (row_ok & col_ok).astype(F32)
    mask = jnp.concatenate(
        [
            alive[:, :SIDE, : sh.main].reshape(SIDE, sh.top),
            alive[:, :, sh.main :].reshape(SIDE, sh.low),
        ],
        axis=1,
    ).reshape(sh.total, 1)
    pixel_area = (grid_size * grid_size).astype(F32)
    area = jnp.pad(pixel_area, (0, sh.padded - images), constant_values=1.0)[:, None]
    row = jnp.arange(sh.rows, dtype=jnp.int32)
    owner = jnp.where(row < sh.top, row % sh.main, sh.main + (row - sh.top) % sh.rest)
    pick = (owner[None, :] == jnp.arange(sh.padded, dtype=jnp.int32)[:, None]).astype(BF)
    labels = jnp.pad(jnp.stack([label_a, label_b, label_c], axis=1), ((0, sh.padded - images), (0, 0)))
    bits = jnp.pad(drop_bits, ((0, sh.padded - images), (0, 0)))
    gb_mid = jnp.stack([gain_mid, bias_mid], axis=2)
    gb_out = jnp.stack([gain_out, bias_out], axis=1)

    x = prep(sh, jnp.transpose(features, (1, 0, 2)), mask)
    saved = []

    def in_order(*values):
        return lax.optimization_barrier(values)

    place = jnp.stack([lax.axis_index("dp"), lax.axis_index("fsdp")]).astype(jnp.int32).reshape(1, 2)
    short = owners == 8 and dp == 4
    w1 = weights[0][0]
    if short:
        width = inner // dp
        quarter = lax.dynamic_slice_in_dim(w_spatial[0], place[0, 0] * width, width, 1)
        x, *column = in_order(x, *flips(quarter, "fsdp", owners, 2))
        column = jnp.stack(column)
        own = jnp.stack(flips(column, "dp", dp, 1))
        w1, own = in_order(w1, own)
        mate = lax.ppermute(own, "fsdp", [(i, i ^ 1) for i in range(owners)])
    h1, part = reduce_conv(sh, x, w1)
    if short:
        part, mate = in_order(part, mate)
    count = jnp.broadcast_to(jnp.sum(pixel_area), (2, inner))
    both = total_of(jnp.concatenate([part, count], axis=0), (dp, owners))
    if short:
        both, first_spatial = in_order(both, assemble(place, own, mate))
        weights[0] = (weights[0][0], first_spatial, weights[0][2])
    tot1, live_count = both[:2], both[2, 0]
    inv = (1.0 / live_count).reshape(1, 1)
    for b in range(blocks):
        w1, w2, w3 = weights[b]
        act1, h2, part = spatial_conv(sh, h1, tot1, inv, gb_mid[b, 0], mask, w2)
        tot2 = total_of(part, (dp, owners))
        act2, h3, part = expand_conv(sh, h2, tot2, inv, gb_mid[b, 1], mask, w3)
        tot3 = total_of(part, (dp, owners))
        saved.append((x, h1, tot1, act1, h2, tot2, act2, h3, tot3))
        if b + 1 < blocks:
            x, h1, part = join(sh, h3, x, tot3, inv, gb_out[b], mask, weights[b + 1][0])
            tot1 = total_of(part, (dp, owners))
    trunk, pooled = last_join(sh, h3, x, tot3, inv, gb_out[-1], mask, area, pick)
    merged, grad_logits = heads(
        pooled, labels, area, bits, head_all, sizes, offsets, sum(lanes)
    )

    mine = lax.all_to_all(
        pooled.reshape(sh.padded, owners, channels // owners).transpose(1, 0, 2),
        "fsdp",
        0,
        0,
        tiled=True,
    ).reshape(owners * sh.padded, channels // owners)
    all_logits = gather(grad_logits)

    def in_order(*values):
        return lax.optimization_barrier(values)

    e3, part = top_grad(sh, merged, h3, x, tot3, inv, gb_out[-1], mask)
    part, mine = in_order(part, mine)
    btot3 = total_of(part, (dp, owners))
    scatter = functools.partial(lax.psum_scatter, axis_name="fsdp", scatter_dimension=0, tiled=True)
    shards, swaps = {}, {}
    sums_mid, sums_out = [], []
    for b in reversed(range(blocks)):
        w1, w2, w3 = weights[b]
        x, h1, tot1, act1, h2, tot2, act2, h3, tot3 = saved[b]
        g3, e2, part = expand_back(
            sh, e3, h3, tot3, gb_out[b], btot3, inv, mask, w3, h2, tot2, gb_mid[b, 1]
        )
        grad = wgrad(act2, g3, inner)
        if short and b + 1 < blocks:
            terms = swaps[b + 1]
            part, *got = in_order(part, *swap_rest(terms, "dp", dp, 1))
            total = added(terms[0], *got)
            swaps[b + 1] = [total[k] for k in range(owners // 2)]
        btot2 = total_of(part, (dp, owners))
        btot2, grad = in_order(btot2, grad)
        shards["expand", b] = scatter(grad)
        if b + 1 == blocks:
            head_grad = tn(all_logits, mine).astype(BF)
        g2, e1, part = spatial_back(
            sh, e2, h2, tot2, gb_mid[b, 1], btot2, inv, mask, w2, h1, tot1, gb_mid[b, 0]
        )
        grad = spatial_wgrad(sh, act1, g2, place, owners, dp, short)
        if short and b + 1 < blocks:
            part, *chips = in_order(part, *swap_rest(swaps[b + 1], "fsdp", owners, 2))
        if b == 0:
            early = [head_grad] + [shards["reduce", k] for k in range(1, blocks)]
            early += [shards["expand", k] for k in range(1, blocks)]
            halves = copies_halves(early)
            part, *swapped = in_order(part, *copies_swap(halves, dp, 0))
            halves = copies_add(halves, swapped)
            swapped = copies_swap(halves, dp, 1)
        btot1 = total_of(part, (dp, owners))
        if b == 0:
            btot1, *swapped = in_order(btot1, *swapped)
        btot1, *grad = in_order(btot1, *grad)
        if short:
            other = swap_core(grad, owners)
        else:
            shards["spatial", b] = scatter(grad[0])
        sums_out.insert(0, (btot3, tot3))
        sums_mid.insert(0, ((btot1, tot1), (btot2, tot2)))
        if b > 0:
            xp, _, _, _, _, _, _, h3p, tot3p = saved[b - 1]
            g1, e3, part = reduce_back(
                sh, e1, h1, tot1, gb_mid[b, 0], btot1, inv, mask, w1, e3, h3p, xp, tot3p, gb_out[b - 1]
            )
            if short:
                part, other = in_order(part, other)
                swaps[b] = [added(grad[0][j], other[j]) for j in range(dp)]
            grad = wgrad(x, g1, inner)
            btot3 = total_of(part, (dp, owners), True)
            btot3, grad = in_order(btot3, grad)
            shards["reduce", b] = scatter(grad)
        else:
            if short:
                swaps[b] = [added(grad[0][j], other[j]) for j in range(dp)]
                e1, *swaps[b] = in_order(e1, *swaps[b])
                got = swap_rest(swaps[b], "dp", dp, 1)
            else:
                got = [shards["spatial", k] for k in range(blocks)]
            grad = reduce_wgrad(sh, e1, h1, tot1, gb_mid[b, 0], btot1, inv, mask, x)
            if short:
                grad, *got[:2] = in_order(grad, *got[:2])
            expand_halves = copies_halves([shards["expand", b]])
            grad, *other = in_order(grad, *copies_swap(expand_halves, dp, 0))
            expand_halves = copies_add(expand_halves, other)
            e3, grad = in_order(e3, grad)
            shards["reduce", b] = scatter(grad)
            grad_features = features_back(
                sh, e1, h1, tot1, gb_mid[b, 0], btot1, inv, mask, w1, e3
            )
            grad_features, *rest = in_order(
                grad_features, *swapped, *got, *(chips if short else [])
            )
            grad_features, shards["reduce", b] = in_order(grad_features, shards["reduce", b])
            swapped = rest[:2]
            got, chips = rest[2 : 2 + len(got)], rest[2 + len(got) :]

    if short:
        total = added(swaps[0][0], *got)
        total = [total[k] for k in range(owners // 2)]
        late_halves = copies_halves([shards["reduce", 0]])
        steps = in_order(*swap_rest(total, "fsdp", owners, 2), *copies_swap(late_halves, dp, 0), *swapped)
        shards["spatial", 0] = added(total[0], *steps[:-4])
        late_halves, swapped = copies_add(late_halves, steps[-4:-2]), steps[-2:]
        shards["spatial", 1] = added(swaps[1][0], *chips)
        flat = jnp.stack([shards["spatial", b] for b in range(blocks)])
        flat = jnp.broadcast_to(flat[None], (dp,) + flat.shape)
        flat = lax.all_to_all(flat, "dp", 0, 0, tiled=True)
        spatial = jnp.transpose(flat, (1, 2, 0, 3)).reshape(w_spatial.shape).astype(F32) / SCALE
    halves = copies_add(halves, swapped)
    sums = copies_out(halves, early)
    late = [shards["reduce", 0]] + ([] if short else got)
    if short:
        lates = copies_out(copies_sum(late_halves, dp, 1), late)
    else:
        lates = copies_out(copies_sum(copies_halves(late), dp), late)
    expand_sum = copies_out(copies_sum(expand_halves, dp, 1), [shards["expand", 0]])
    head_grad = sums[0]
    reduce_all = jnp.stack([lates[0]] + sums[1:blocks])
    expand_all = jnp.stack(expand_sum + sums[blocks:])
    if not short:
        spatial = jnp.stack(lates[1:])
    at = [(place, size) for place, size in zip(offsets, sizes)]

    def gains(pair):
        btot, tot = pair
        mu = tot[0] / live_count
        var = jnp.maximum(tot[1] / live_count - mu * mu, 0.0)
        return (btot[1] - mu * btot[0]) * lax.rsqrt(var + EPS) / SCALE

    return (
        jnp.transpose(trunk, (1, 0, 2)),
        jnp.transpose(grad_features, (1, 0, 2)),
        reduce_all,
        spatial,
        expand_all,
        jnp.stack([jnp.stack([gains(p) for p in pairs]) for pairs in sums_mid]),
        jnp.stack([jnp.stack([p[0][0] / SCALE for p in pairs]) for pairs in sums_mid]),
        jnp.stack([gains(p) for p in sums_out]),
        jnp.stack([p[0][0] / SCALE for p in sums_out]),
    ) + tuple(head_grad[place : place + size].T for place, size in at)


def solution(mesh):
    split = P(AXES)
    rows = P(None, "fsdp", None)
    head = P("fsdp", None)
    in_specs = (
        P(AXES, None, None), split, rows, rows, rows, P(), P(), P(), P(),
        head, head, head, split, split, split, P(AXES, None),
    )
    out_specs = (
        P(AXES, None, None), P(AXES, None, None), rows, rows, rows, P(), P(), P(), P(), head, head, head,
    )
    body = functools.partial(on_device, mesh.shape["dp"], mesh.shape["fsdp"])
    return jax.shard_map(body, mesh=mesh, in_specs=in_specs, out_specs=out_specs, check_vma=False)
```

```python
import functools

import jax
import jax.numpy as jnp
from jax import lax
from jax.experimental import pallas as pl
from jax.experimental.pallas import tpu as pltpu
from jax.sharding import PartitionSpec as P

SIDE = 7
TAPS = 3
EPS = 1e-05
FLOOR = 0.05
WIDTH = 0.1
SCALE = 256.0
BF = jnp.bfloat16
F32 = jnp.float32
VMEM_LIMIT = 56 * 1024 * 1024
AXES = ("dp", "fsdp")


def nn(left, right):
    return jnp.dot(left, right, preferred_element_type=F32)


def nt(left, right):
    return lax.dot_general(left, right, (((1,), (1,)), ((), ())), preferred_element_type=F32)


def tn(left, right):
    return lax.dot_general(left, right, (((0,), (0,)), ((), ())), preferred_element_type=F32)


def sigmoid(v):
    return 0.5 * jnp.tanh(0.5 * v) + 0.5


def silu_half(u):
    return u * jnp.tanh(u) + u


def slope_twice(u):
    t = jnp.tanh(u)
    return (1.0 + t) * (1.0 + u * (1.0 - t))


def rowsum(v):
    return jnp.sum(v, axis=0, keepdims=True)


def params(n_grid):
    return pltpu.CompilerParams(
        dimension_semantics=("arbitrary",) * n_grid, vmem_limit_bytes=VMEM_LIMIT
    )


def whole(shape):
    zeros = (0,) * len(shape)
    return pl.BlockSpec(shape, lambda *g: zeros)


def tile(rows, cols):
    return pl.BlockSpec((rows, cols), lambda j: (j, 0))


def sds(shape, dtype):
    return jax.ShapeDtypeStruct(shape, dtype)


def cost(flops, nbytes, trans=0):
    return pl.CostEstimate(flops=int(flops), bytes_accessed=int(nbytes), transcendentals=int(trans))


def forward_consts(tot, inv, gb):
    mu = tot[0:1, :] * inv
    var = jnp.maximum(tot[1:2, :] * inv - mu * mu, 0.0)
    rstd = lax.rsqrt(var + EPS)
    a = rstd * gb[0:1, :]
    return mu, rstd, a, gb[1:2, :] - mu * a


def backward_consts(mu, rstd, a, btot, inv):
    ex = (btot[1:2, :] - mu * btot[0:1, :]) * rstd * inv
    c1 = -a * rstd * ex
    c0 = -a * btot[0:1, :] * inv - c1 * mu
    return c1, c0


def clear_at_first(*refs):
    @pl.when(pl.program_id(0) == 0)
    def _():
        for ref in refs:
            ref[...] = jnp.zeros_like(ref)


def add_stats(st, top, low, cols=slice(None)):
    st[0:1, cols] += top
    st[1:2, cols] += low


def chunks(rows, columns, height, width=256):
    for c in range(0, columns, width):
        for r in range(0, rows, height):
            yield slice(r, r + height), slice(c, c + width)


class Shape:
    def __init__(self, images):
        self.images = images
        self.main = images // 16 * 16
        self.rest = images - self.main
        self.top = SIDE * self.main
        self.low = (SIDE + 1) * self.rest
        self.rows = self.top + self.low
        self.total = SIDE * self.rows
        self.step = self.total // 4
        self.half = self.total // 2
        self.padded = self.main + 16


def prep_kernel(sh, f, mask, x, scr):
    channels = x.shape[1]
    scr[...] = jnp.zeros_like(scr)
    for s in range(SIDE):
        x[s * sh.main : (s + 1) * sh.main, :] = (
            f[s, 0 : sh.main, :].astype(F32) * mask[s * sh.main : (s + 1) * sh.main, :]
        ).astype(BF)
        scr[s * sh.rest : (s + 1) * sh.rest, :] = f[s, sh.main : sh.images, :].astype(F32)
    x[sh.top : sh.rows, :] = jnp.where(mask[sh.top : sh.rows, :] > 0.0, scr[...], 0.0).astype(BF)


def prep(sh, features, mask):
    channels = features.shape[2]
    return pl.pallas_call(
        functools.partial(prep_kernel, sh),
        grid=(SIDE,),
        in_specs=[
            pl.BlockSpec((SIDE, sh.images, channels), lambda j: (j, 0, 0)),
            tile(sh.rows, 1),
        ],
        out_specs=tile(sh.rows, channels),
        out_shape=sds((sh.total, channels), BF),
        scratch_shapes=[pltpu.VMEM((sh.low, channels), F32)],
        compiler_params=params(1),
        name="prep",
    )(features, mask)


def reduce_kernel(x, w, h, st):
    clear_at_first(st)
    acc = nn(x[...], w[...])
    h[...] = acc
    add_stats(st, rowsum(acc), rowsum(acc * acc))


def reduce_conv(sh, x, w):
    c, m = w.shape
    return pl.pallas_call(
        reduce_kernel,
        grid=(sh.total // sh.step,),
        in_specs=[tile(sh.step, c), whole((c, m))],
        out_specs=[tile(sh.step, m), whole((2, m))],
        out_shape=[sds((sh.total, m), F32), sds((2, m), F32)],
        compiler_params=params(1),
        cost_estimate=cost(2 * sh.total * c * m, 2 * sh.total * c + 4 * sh.total * m),
        name="reduce_conv",
    )(x, w)


def shifted(sh, v, scr):
    m = v.shape[1]
    gap = jnp.zeros((sh.main, m), F32)
    scr[8 : 8 + sh.low, :] = v[sh.top :, :]
    before = jnp.concatenate([gap, v[: sh.top - sh.main, :], scr[8 - sh.rest : 8 - sh.rest + sh.low, :]], axis=0)
    after = jnp.concatenate([v[sh.main : sh.top, :], gap, scr[8 + sh.rest : 8 + sh.rest + sh.low, :]], axis=0)
    return before, v, after


def put_shifted(sh, v, scr, pat, row):
    m = v.shape[1]
    at = pl.ds(pl.multiple_of(row * sh.rows, sh.rows), sh.rows)
    for k, part in enumerate(shifted(sh, v, scr)):
        pat[at, k * m : (k + 1) * m] = part.astype(BF)


def spatial_kernel(sh, inv, h1, tot, gb, mask, mask_out, w, act, h2, st, pat, scr):
    j = pl.program_id(0)
    m = h1.shape[1]

    clear_at_first(pat, scr, st)
    mu, rstd, a, b = forward_consts(tot, inv[0, 0], gb)
    acc = None
    for k in range(2):
        at = pl.ds(pl.multiple_of((j + k) * sh.rows, sh.rows), sh.rows)
        part = nn(pat[at, :], w[k * TAPS * m : (k + 1) * TAPS * m, :])
        acc = part if acc is None else acc + part
    y = mask[...] * silu_half(h1[...] * (0.5 * a) + 0.5 * b)
    act[...] = y.astype(BF)
    put_shifted(sh, jnp.where(j < SIDE, y, 0.0), scr, pat, j + 2)
    at = pl.ds(pl.multiple_of((j + 2) * sh.rows, sh.rows), sh.rows)
    acc = acc + nn(pat[at, :], w[2 * TAPS * m :, :])
    h2[...] = acc
    got = jnp.where(j > 0, mask_out[...], 0.0) * acc
    add_stats(st, rowsum(got), rowsum(got * acc))


def spatial_conv(sh, h1, tot, inv, gb, mask, w):
    m = h1.shape[1]
    into = lambda j: (jnp.minimum(j, SIDE - 1), 0)
    outof = lambda j: (jnp.maximum(j - 1, 0), 0)
    return pl.pallas_call(
        functools.partial(spatial_kernel, sh),
        grid=(SIDE + 1,),
        in_specs=[
            pl.BlockSpec(memory_space=pltpu.SMEM),
            pl.BlockSpec((sh.rows, m), into),
            whole((2, m)),
            whole((2, m)),
            pl.BlockSpec((sh.rows, 1), into),
            pl.BlockSpec((sh.rows, 1), outof),
            whole(w.shape),
        ],
        out_specs=[
            pl.BlockSpec((sh.rows, m), into),
            pl.BlockSpec((sh.rows, m), outof),
            whole((2, m)),
        ],
        out_shape=[sds((sh.total, m), BF), sds((sh.total, m), F32), sds((2, m), F32)],
        scratch_shapes=[
            pltpu.VMEM(((SIDE + 3) * sh.rows, TAPS * m), BF),
            pltpu.VMEM((sh.low + 16, m), F32),
        ],
        compiler_params=params(1),
        cost_estimate=cost(2 * sh.total * w.size, 2 * w.size + 10 * sh.total * m),
        name="spatial_conv",
    )(inv, h1, tot, gb, mask, mask, w)


def expand_kernel(inv, h2, tot, gb, mask, w, act, h3, st):
    clear_at_first(st)
    mu, rstd, a, b = forward_consts(tot, inv[0, 0], gb)
    y = (mask[...] * silu_half(h2[...] * (0.5 * a) + 0.5 * b)).astype(BF)
    act[...] = y
    step = 512
    for c in range(0, w.shape[1], step):
        cols = slice(c, c + step)
        acc = nn(y, w[:, cols])
        h3[:, cols] = acc.astype(BF)
        add_stats(st, rowsum(acc), rowsum(acc * acc), cols)


def expand_conv(sh, h2, tot, inv, gb, mask, w):
    m, c = w.shape
    return pl.pallas_call(
        expand_kernel,
        grid=(sh.total // sh.step,),
        in_specs=[
            pl.BlockSpec(memory_space=pltpu.SMEM),
            tile(sh.step, m),
            whole((2, m)),
            whole((2, m)),
            tile(sh.step, 1),
            whole((m, c)),
        ],
        out_specs=[tile(sh.step, m), tile(sh.step, c), whole((2, c))],
        out_shape=[sds((sh.total, m), BF), sds((sh.total, c), BF), sds((2, c), F32)],
        compiler_params=params(1),
        cost_estimate=cost(2 * sh.total * c * m, 2 * sh.total * c + 6 * sh.total * m),
        name="expand_conv",
    )(inv, h2, tot, gb, mask, w)


def join_kernel(inv, h3, x, tot, gb, mask, w, y, h1, st):
    clear_at_first(st)
    mu, rstd, a, b = forward_consts(tot, inv[0, 0], gb)
    step = 512
    acc = None
    for c in range(0, x.shape[1], step):
        cols = slice(c, c + step)
        v = h3[:, cols].astype(F32) * a[:, cols] + b[:, cols] + x[:, cols].astype(F32)
        out = (mask[...] * silu_half(0.5 * v)).astype(BF)
        y[:, cols] = out
        part = nn(out, w[cols, :])
        acc = part if acc is None else acc + part
    h1[...] = acc
    add_stats(st, rowsum(acc), rowsum(acc * acc))


def join(sh, h3, x, tot, inv, gb, mask, w):
    c, m = w.shape
    return pl.pallas_call(
        join_kernel,
        grid=(sh.total // sh.step,),
        in_specs=[
            pl.BlockSpec(memory_space=pltpu.SMEM),
            tile(sh.step, c),
            tile(sh.step, c),
            whole((2, c)),
            whole((2, c)),
            tile(sh.step, 1),
            whole((c, m)),
        ],
        out_specs=[tile(sh.step, c), tile(sh.step, m), whole((2, m))],
        out_shape=[sds((sh.total, c), BF), sds((sh.total, m), F32), sds((2, m), F32)],
        compiler_params=params(1),
        cost_estimate=cost(2 * sh.total * c * m, 6 * sh.total * c + 4 * sh.total * m),
        name="join",
    )(inv, h3, x, tot, gb, mask, w)


def last_kernel(sh, inv, h3, x, tot, gb, mask, area, pick, trunk, pooled, sums, scr):
    j = pl.program_id(0)
    clear_at_first(sums)
    mu, rstd, a, b = forward_consts(tot, inv[0, 0], gb)
    step = 512
    for c in range(0, x.shape[1], step):
        cols = slice(c, c + step)
        v = h3[:, cols].astype(F32) * a[:, cols] + b[:, cols] + x[:, cols].astype(F32)
        out = mask[...] * silu_half(0.5 * v)
        low = out.astype(BF)
        scr[:, cols] = out[sh.top :, :]
        for s in range(SIDE):
            trunk[s, 0 : sh.main, cols] = low[s * sh.main : (s + 1) * sh.main, :]
            trunk[s, sh.main : sh.images, cols] = scr[s * sh.rest : (s + 1) * sh.rest, cols].astype(BF)
        sums[:, cols] += nn(pick[...], low)

    @pl.when(j == SIDE - 1)
    def _():
        pooled[...] = (sums[...] / area[...]).astype(BF)


def last_join(sh, h3, x, tot, inv, gb, mask, area, pick):
    c = x.shape[1]
    return pl.pallas_call(
        functools.partial(last_kernel, sh),
        grid=(SIDE,),
        in_specs=[
            pl.BlockSpec(memory_space=pltpu.SMEM),
            tile(sh.rows, c),
            tile(sh.rows, c),
            whole((2, c)),
            whole((2, c)),
            tile(sh.rows, 1),
            whole((sh.padded, 1)),
            whole((sh.padded, sh.rows)),
        ],
        out_specs=[
            pl.BlockSpec((SIDE, sh.images, c), lambda j: (j, 0, 0)),
            whole((sh.padded, c)),
        ],
        out_shape=[sds((SIDE * SIDE, sh.images, c), BF), sds((sh.padded, c), BF)],
        scratch_shapes=[pltpu.VMEM((sh.padded, c), F32), pltpu.VMEM((sh.low, c), F32)],
        compiler_params=params(1),
        cost_estimate=cost(2 * sh.padded * sh.total * c, 6 * sh.total * c),
        name="last_join",
    )(inv, h3, x, tot, gb, mask, area, pick)


def heads_kernel(sizes, offsets, pooled, labels, area, bits, w, merged, out):
    rows = pooled.shape[0]
    out[...] = jnp.zeros_like(out)
    summed = None
    at = 0
    for t, (classes, place) in enumerate(zip(sizes, offsets)):
        span = -(-classes // 16) * 16
        wt = w[at : at + span, :]
        at += span
        logits = nt(pooled[...], wt)
        index = lax.broadcasted_iota(jnp.int32, (rows, span), 1)
        inside = index < classes
        logits = jnp.where(inside, logits, -1e30)
        top = jnp.max(logits, axis=1, keepdims=True)
        ex = jnp.where(inside, jnp.exp(logits - top), 0.0)
        probs = ex / jnp.sum(ex, axis=1, keepdims=True)
        targets = jnp.where(index == labels[:, t : t + 1], 1.0, 0.0)
        grad = (SCALE * (probs - targets)).astype(BF)
        out[:, place : place + span] = grad
        single = nn(grad, wt) / area[...]
        size = jnp.sqrt(single * single + FLOOR * FLOOR)
        summed = single if summed is None else summed + single
        magnitude = size if t == 0 else magnitude + size
    purity = 0.5 * (1.0 + summed / magnitude)
    level = (bits[...].astype(F32) + 0.5) / 32768.0
    keep = sigmoid((purity - level) / WIDTH)
    merged[...] = 0.5 * summed + (keep - 0.5) * magnitude


def heads(pooled, labels, area, bits, w, sizes, offsets, span):
    rows, c = pooled.shape
    return pl.pallas_call(
        functools.partial(heads_kernel, sizes, offsets),
        out_shape=[sds((rows, c), F32), sds((rows, span), BF)],
        compiler_params=pltpu.CompilerParams(vmem_limit_bytes=VMEM_LIMIT),
        cost_estimate=cost(4 * rows * c * span, 2 * w.size),
        name="heads",
    )(pooled, labels, area, bits, w)


def top_grad_kernel(sh, inv, merged, h3, x, tot, gb, mask, e3, st, scr):
    j = pl.program_id(0)
    clear_at_first(st)

    @pl.when(j == 0)
    def _():
        for s in range(SIDE + 1):
            scr[s * sh.rest : (s + 1) * sh.rest, :] = merged[sh.main : sh.images, :]

    mu, rstd, a, b = forward_consts(tot, inv[0, 0], gb)
    for rows, cols in chunks(sh.rows, x.shape[1], sh.main):
        h = h3[rows, cols].astype(F32)
        v = h * a[:, cols] + b[:, cols] + x[rows, cols].astype(F32)
        up = scr[:, cols] if rows.start >= sh.top else merged[0 : sh.main, cols]
        e = (0.5 * mask[rows, :]) * up * slope_twice(0.5 * v)
        e3[rows, cols] = e.astype(BF)
        add_stats(st, rowsum(e), rowsum(e * h), cols)


def top_grad(sh, merged, h3, x, tot, inv, gb, mask):
    c = x.shape[1]
    return pl.pallas_call(
        functools.partial(top_grad_kernel, sh),
        grid=(SIDE,),
        in_specs=[
            pl.BlockSpec(memory_space=pltpu.SMEM),
            whole(merged.shape),
            tile(sh.rows, c),
            tile(sh.rows, c),
            whole((2, c)),
            whole((2, c)),
            tile(sh.rows, 1),
        ],
        out_specs=[tile(sh.rows, c), whole((2, c))],
        out_shape=[sds((sh.total, c), BF), sds((2, c), F32)],
        scratch_shapes=[pltpu.VMEM((sh.low, c), F32)],
        compiler_params=params(1),
        cost_estimate=cost(20 * sh.total * c, 6 * sh.total * c),
        name="top_grad",
    )(inv, merged, h3, x, tot, gb, mask)


def expand_back_kernel(inv, e3, h3, tot3, gb3, btot3, mask, w, h2, tot2, gb2, g3, e2, st):
    clear_at_first(st)
    mu, rstd, a, b = forward_consts(tot3, inv[0, 0], gb3)
    c1, c0 = backward_consts(mu, rstd, a, btot3, inv[0, 0])
    step = 512
    acc = None
    for c in range(0, e3.shape[1], step):
        cols = slice(c, c + step)
        g = a[:, cols] * e3[:, cols].astype(F32) + c1[:, cols] * h3[:, cols].astype(F32) + c0[:, cols]
        g = (mask[...] * g).astype(BF)
        g3[:, cols] = g
        part = nt(g, w[:, cols])
        acc = part if acc is None else acc + part
    mu, rstd, a, b = forward_consts(tot2, inv[0, 0], gb2)
    h = h2[...]
    e = acc * (0.5 * slope_twice(h * (0.5 * a) + 0.5 * b))
    e2[...] = e
    add_stats(st, rowsum(e), rowsum(e * h))


def expand_back(sh, e3, h3, tot3, gb3, btot3, inv, mask, w, h2, tot2, gb2):
    m, c = w.shape
    return pl.pallas_call(
        expand_back_kernel,
        grid=(sh.total // sh.half,),
        in_specs=[
            pl.BlockSpec(memory_space=pltpu.SMEM),
            tile(sh.half, c),
            tile(sh.half, c),
            whole((2, c)),
            whole((2, c)),
            whole((2, c)),
            tile(sh.half, 1),
            whole((m, c)),
            tile(sh.half, m),
            whole((2, m)),
            whole((2, m)),
        ],
        out_specs=[tile(sh.half, c), tile(sh.half, m), whole((2, m))],
        out_shape=[sds((sh.total, c), BF), sds((sh.total, m), F32), sds((2, m), F32)],
        compiler_params=params(1),
        cost_estimate=cost(2 * sh.total * c * m, 6 * sh.total * c + 8 * sh.total * m),
        name="expand_back",
    )(inv, e3, h3, tot3, gb3, btot3, mask, w, h2, tot2, gb2)


def spatial_back_kernel(
    sh, inv, e2, h2, tot2, gb2, btot2, mask, mask_out, w, h1, tot1, gb1, g2, e1, st, pat, scr
):
    j = pl.program_id(0)
    m = e2.shape[1]

    clear_at_first(pat, scr, st)

    def taps(k):
        at = pl.ds(pl.multiple_of((j + k) * sh.rows, sh.rows), sh.rows)
        total = None
        for l in range(TAPS):
            tap = TAPS * (2 - k) + (2 - l)
            part = nt(pat[at, l * m : (l + 1) * m], w[tap * m : (tap + 1) * m, :])
            total = part if total is None else total + part
        return total

    acc = taps(0) + taps(1)
    mu, rstd, a, b = forward_consts(tot2, inv[0, 0], gb2)
    c1, c0 = backward_consts(mu, rstd, a, btot2, inv[0, 0])
    g = mask[...] * (a * e2[...] + c1 * h2[...] + c0)
    g2[...] = g.astype(BF)
    put_shifted(sh, jnp.where(j < SIDE, g, 0.0), scr, pat, j + 2)
    acc = acc + taps(2)
    mu, rstd, a, b = forward_consts(tot1, inv[0, 0], gb1)
    h = h1[...]
    e = jnp.where(j > 0, 0.5 * mask_out[...], 0.0) * acc * slope_twice(h * (0.5 * a) + 0.5 * b)
    e1[...] = e
    add_stats(st, rowsum(e), rowsum(e * h))


def spatial_back(sh, e2, h2, tot2, gb2, btot2, inv, mask, w, h1, tot1, gb1):
    m = e2.shape[1]
    into = lambda j: (jnp.minimum(j, SIDE - 1), 0)
    outof = lambda j: (jnp.maximum(j - 1, 0), 0)
    return pl.pallas_call(
        functools.partial(spatial_back_kernel, sh),
        grid=(SIDE + 1,),
        in_specs=[
            pl.BlockSpec(memory_space=pltpu.SMEM),
            pl.BlockSpec((sh.rows, m), into),
            pl.BlockSpec((sh.rows, m), into),
            whole((2, m)),
            whole((2, m)),
            whole((2, m)),
            pl.BlockSpec((sh.rows, 1), into),
            pl.BlockSpec((sh.rows, 1), outof),
            whole(w.shape),
            pl.BlockSpec((sh.rows, m), outof),
            whole((2, m)),
            whole((2, m)),
        ],
        out_specs=[
            pl.BlockSpec((sh.rows, m), into),
            pl.BlockSpec((sh.rows, m), outof),
            whole((2, m)),
        ],
        out_shape=[sds((sh.total, m), BF), sds((sh.total, m), F32), sds((2, m), F32)],
        scratch_shapes=[
            pltpu.VMEM(((SIDE + 3) * sh.rows, TAPS * m), BF),
            pltpu.VMEM((sh.low + 16, m), F32),
        ],
        compiler_params=params(1),
        cost_estimate=cost(2 * sh.total * w.size, 2 * w.size + 18 * sh.total * m),
        name="spatial_back",
    )(inv, e2, h2, tot2, gb2, btot2, mask, mask, w, h1, tot1, gb1)


def reduce_back_kernel(
    inv, e1, h1, tot1, gb1, btot1, mask, w, e3, h3, x, tot3, gb3, g1, down, st
):
    clear_at_first(st)
    mu, rstd, a, b = forward_consts(tot1, inv[0, 0], gb1)
    c1, c0 = backward_consts(mu, rstd, a, btot1, inv[0, 0])
    g = (mask[...] * (a * e1[...] + c1 * h1[...] + c0)).astype(BF)
    g1[...] = g
    mu, rstd, a, b = forward_consts(tot3, inv[0, 0], gb3)
    step = 256
    for c in range(0, x.shape[1], step):
        cols = slice(c, c + step)
        up = nt(g, w[cols, :]) + e3[:, cols].astype(F32)
        h = h3[:, cols].astype(F32)
        v = h * a[:, cols] + b[:, cols] + x[:, cols].astype(F32)
        e = up * (0.5 * slope_twice(0.5 * v))
        down[:, cols] = e.astype(BF)
        add_stats(st, rowsum(e), rowsum(e * h), cols)


def reduce_back(sh, e1, h1, tot1, gb1, btot1, inv, mask, w, e3, h3, x, tot3, gb3):
    c, m = w.shape
    return pl.pallas_call(
        reduce_back_kernel,
        grid=(sh.total // sh.step,),
        in_specs=[
            pl.BlockSpec(memory_space=pltpu.SMEM),
            tile(sh.step, m),
            tile(sh.step, m),
            whole((2, m)),
            whole((2, m)),
            whole((2, m)),
            tile(sh.step, 1),
            whole((c, m)),
            tile(sh.step, c),
            tile(sh.step, c),
            tile(sh.step, c),
            whole((2, c)),
            whole((2, c)),
        ],
        out_specs=[tile(sh.step, m), tile(sh.step, c), whole((2, c))],
        out_shape=[sds((sh.total, m), BF), sds((sh.total, c), BF), sds((2, c), F32)],
        compiler_params=params(1),
        cost_estimate=cost(2 * sh.total * c * m, 8 * sh.total * c + 10 * sh.total * m),
        name="reduce_back",
    )(inv, e1, h1, tot1, gb1, btot1, mask, w, e3, h3, x, tot3, gb3)


def features_back_kernel(sh, inv, e1, h1, tot1, gb1, btot1, mask, w, e3, out, scr):
    mu, rstd, a, b = forward_consts(tot1, inv[0, 0], gb1)
    c1, c0 = backward_consts(mu, rstd, a, btot1, inv[0, 0])
    g = (mask[...] * (a * e1[...] + c1 * h1[...] + c0)).astype(BF)
    step = 512
    for c in range(0, w.shape[0], step):
        cols = slice(c, c + step)
        up = nt(g, w[cols, :]) + e3[:, cols].astype(F32)
        scr[:, cols] = up[sh.top :, :]
        for s in range(SIDE):
            out[s, 0 : sh.main, cols] = up[s * sh.main : (s + 1) * sh.main, :]
            out[s, sh.main : sh.images, cols] = scr[s * sh.rest : (s + 1) * sh.rest, cols]


def features_back(sh, e1, h1, tot1, gb1, btot1, inv, mask, w, e3):
    c, m = w.shape
    return pl.pallas_call(
        functools.partial(features_back_kernel, sh),
        grid=(SIDE,),
        in_specs=[
            pl.BlockSpec(memory_space=pltpu.SMEM),
            tile(sh.rows, m),
            tile(sh.rows, m),
            whole((2, m)),
            whole((2, m)),
            whole((2, m)),
            tile(sh.rows, 1),
            whole((c, m)),
            tile(sh.rows, c),
        ],
        out_specs=pl.BlockSpec((SIDE, sh.images, c), lambda j: (j, 0, 0)),
        out_shape=sds((SIDE * SIDE, sh.images, c), F32),
        scratch_shapes=[pltpu.VMEM((sh.low, c), F32)],
        compiler_params=params(1),
        cost_estimate=cost(2 * sh.total * c * m, 6 * sh.total * c + 10 * sh.total * m),
        name="features_back",
    )(inv, e1, h1, tot1, gb1, btot1, mask, w, e3)


def wgrad_kernel(left, right, out):
    out[...] = tn(left[...], right[...]).astype(BF)


def wgrad(left, right, step):
    rows, a = left.shape
    b = right.shape[1]
    by_left = a >= b
    if by_left:
        specs = [pl.BlockSpec((rows, step), lambda j: (0, j)), whole((rows, b))]
        out_spec = pl.BlockSpec((step, b), lambda j: (j, 0))
    else:
        specs = [whole((rows, a)), pl.BlockSpec((rows, step), lambda j: (0, j))]
        out_spec = pl.BlockSpec((a, step), lambda j: (0, j))
    return pl.pallas_call(
        wgrad_kernel,
        grid=(max(a, b) // step,),
        in_specs=specs,
        out_specs=out_spec,
        out_shape=sds((a, b), BF),
        compiler_params=params(1),
        cost_estimate=cost(2 * rows * a * b, 2 * (rows * (a + b) + a * b)),
        name="wgrad",
    )(left, right)


def reduce_wgrad_kernel(inv, e1, h1, tot1, gb1, btot1, mask, x, out, acc):
    clear_at_first(acc)
    mu, rstd, a, b = forward_consts(tot1, inv[0, 0], gb1)
    c1, c0 = backward_consts(mu, rstd, a, btot1, inv[0, 0])
    g = (mask[...] * (a * e1[...] + c1 * h1[...] + c0)).astype(BF)
    step = 512
    for c in range(0, x.shape[1], step):
        acc[c : c + step, :] += tn(x[:, c : c + step], g)

    @pl.when(pl.program_id(0) == pl.num_programs(0) - 1)
    def _():
        out[...] = acc[...].astype(BF)


def reduce_wgrad(sh, e1, h1, tot1, gb1, btot1, inv, mask, x):
    c, m = x.shape[1], e1.shape[1]
    return pl.pallas_call(
        reduce_wgrad_kernel,
        grid=(sh.total // sh.step,),
        in_specs=[
            pl.BlockSpec(memory_space=pltpu.SMEM),
            tile(sh.step, m),
            tile(sh.step, m),
            whole((2, m)),
            whole((2, m)),
            whole((2, m)),
            tile(sh.step, 1),
            tile(sh.step, c),
        ],
        out_specs=whole((c, m)),
        out_shape=sds((c, m), BF),
        scratch_shapes=[pltpu.VMEM((c, m), F32)],
        compiler_params=params(1),
        cost_estimate=cost(2 * sh.total * c * m, 2 * sh.total * c + 8 * sh.total * m),
        name="reduce_wgrad",
    )(inv, e1, h1, tot1, gb1, btot1, mask, x)


def put_owned(place, val, outs, first):
    dps, chips, rows, width = outs[0].shape
    last, at = first + val.shape[0], first
    while at < last:
        chip, start = at // (2 * rows), at % (2 * rows)
        stop = min(2 * rows, start + last - at)
        for side in range(2):
            low, high = max(start, side * rows), min(stop, (side + 1) * rows)
            if low >= high:
                continue
            source = pl.ds(at - first + low - start, high - low)
            for q in range(dps):
                piece = val[source, q * width : (q + 1) * width]
                for e, out in enumerate(outs):

                    @pl.when((place[0, 1] & 1) == (side ^ e))
                    def _(piece=piece, out=out, low=low, high=high, q=q):
                        out[q ^ place[0, 0], chip ^ (place[0, 1] >> 1), low - side * rows : high - side * rows, :] = piece
        at += stop - start


def spatial_wgrad_kernel(sh, owned, place, act, g, *rest):
    *outs, pat, scr, val = rest
    j = pl.program_id(0)
    m = act.shape[1]

    @pl.when(j == 0)
    def _():
        scr[...] = jnp.zeros_like(scr)
        pat[0 : sh.rows, :] = jnp.zeros((sh.rows, TAPS * m), BF)
        pat[(SIDE + 1) * sh.rows :, :] = jnp.zeros((sh.rows, TAPS * m), BF)
        for r in range(SIDE):
            put_shifted(sh, act[r * sh.rows : (r + 1) * sh.rows, :].astype(F32), scr, pat, r + 1)

    for k in range(TAPS):

        @pl.when(j == k)
        def _(k=k):
            rows = slice(k * sh.rows, (k + SIDE) * sh.rows)
            for l in range(TAPS):
                into = val if owned else outs[0]
                into[l * m : (l + 1) * m, :] = tn(pat[rows, l * m : (l + 1) * m], g[...]).astype(BF)
            if owned:
                put_owned(place, val, outs, k * TAPS * m)


def spatial_wgrad(sh, act, g, place, owners, dp, owned):
    m = act.shape[1]
    rows = TAPS * TAPS * m
    owned_shape = (dp, owners // 2, rows // owners, m // dp)
    return pl.pallas_call(
        functools.partial(spatial_wgrad_kernel, sh, owned),
        grid=(TAPS,),
        in_specs=[pl.BlockSpec(memory_space=pltpu.SMEM), whole(act.shape), whole(g.shape)],
        out_specs=[whole(owned_shape)] * 2 if owned else [pl.BlockSpec((TAPS * m, m), lambda j: (j, 0))],
        out_shape=[sds(owned_shape, BF)] * 2 if owned else [sds((rows, m), BF)],
        scratch_shapes=[
            pltpu.VMEM(((SIDE + 2) * sh.rows, TAPS * m), BF),
            pltpu.VMEM((sh.low + 16, m), F32),
            pltpu.VMEM((TAPS * m, m), BF),
        ],
        compiler_params=params(1),
        cost_estimate=cost(18 * sh.total * m * m, 4 * sh.total * m + 18 * m * m),
        name="spatial_wgrad",
    )(place, act, g)


def assemble_kernel(place, own, mate, out, sem):
    dps, chips, rows, width = own.shape
    copies = []
    for e, src in enumerate((own, mate)):
        for j in range(dps):
            for k in range(chips):
                owner = place[0, 1] ^ (2 * k + e)
                row = pl.multiple_of(owner * rows, rows)
                col = pl.multiple_of((place[0, 0] ^ j) * width, width)
                copies.append(
                    pltpu.make_async_copy(
                        src.at[j, k],
                        out.at[pl.ds(row, rows), pl.ds(col, width)],
                        sem.at[len(copies)],
                    )
                )
    for copy in copies:
        copy.start()
    for copy in copies:
        copy.wait()


def assemble(place, own, mate):
    dps, chips, rows, width = own.shape
    anywhere = pl.BlockSpec(memory_space=pl.ANY)
    return pl.pallas_call(
        assemble_kernel,
        in_specs=[pl.BlockSpec(memory_space=pltpu.SMEM), anywhere, anywhere],
        out_specs=pl.BlockSpec(memory_space=pltpu.VMEM),
        out_shape=sds((2 * chips * rows, dps * width), BF),
        scratch_shapes=[pltpu.SemaphoreType.DMA((2 * dps * chips,))],
        compiler_params=pltpu.CompilerParams(vmem_limit_bytes=VMEM_LIMIT),
        cost_estimate=cost(0, 8 * own.size),
        name="assemble",
    )(place, own, mate)


def flips(v, axis, size, unit):
    return [v] + [
        lax.ppermute(v, axis, [(i, i ^ (unit * k)) for i in range(size)]) for k in range(1, size // unit)
    ]


def others(v, axis, size, unit):
    turns = size // unit
    ways = [
        [(i, (i // unit + d) % turns * unit + i % unit) for i in range(size)]
        for d in range(1, turns)
    ]
    return sum([lax.ppermute(v, axis, way) for way in ways], v)


def total_of(v, sizes, beside=False):
    dp, fsdp = sizes
    flat = v.reshape(8, -1)
    if flat.size > 2048 and not beside:
        flat = flat + lax.ppermute(flat, "fsdp", [(i, i ^ 1) for i in range(fsdp)])
        flat = others(flat, "fsdp", fsdp, 2)
        return others(flat, "dp", dp, 1).reshape(v.shape)
    devices = dp * fsdp
    spread = jnp.broadcast_to(flat[None], (devices,) + flat.shape)
    got = lax.all_to_all(spread, AXES, 0, 0, tiled=True)
    return jnp.sum(got, axis=0).reshape(v.shape)


def added(*terms):
    return sum([v.astype(F32) for v in terms[1:]], terms[0].astype(F32)).astype(BF)


def copies_halves(arrays):
    flat = [v.reshape(-1, 512) for v in arrays]
    flat = jnp.concatenate(flat, axis=0) if len(flat) > 1 else flat[0]
    cut = flat.shape[0] // 32 * 16
    return [flat[:cut], flat[cut:]]


def copies_swap(halves, dp, turn):
    bits = [1 << k for k in range(dp.bit_length() - 1)]
    return [
        lax.ppermute(half, "dp", [(i, i ^ (bits, bits[::-1])[h][turn]) for i in range(dp)])
        for h, half in enumerate(halves)
    ]


def copies_add(halves, got):
    return [added(half, other) for half, other in zip(halves, got)]


def copies_sum(halves, dp, first=0):
    for turn in range(first, dp.bit_length() - 1):
        halves = copies_add(halves, copies_swap(halves, dp, turn))
    return halves


def swap_core(parts, owners):
    return lax.ppermute(parts[1], "fsdp", [(i, i ^ 1) for i in range(owners)])


def swap_rest(blocks, axis, size, unit):
    return [
        lax.ppermute(blocks[k], axis, [(i, i ^ (unit * k)) for i in range(size)])
        for k in range(1, len(blocks))
    ]


def copies_out(halves, arrays):
    flat = jnp.concatenate(halves, axis=0).astype(F32) / SCALE
    out, at = [], 0
    for v in arrays:
        rows = v.size // 512
        out.append(flat[at : at + rows].reshape(v.shape))
        at += rows
    return out


def on_device(
    dp,
    owners,
    features,
    grid_size,
    w_reduce,
    w_spatial,
    w_expand,
    gain_mid,
    bias_mid,
    gain_out,
    bias_out,
    head_a,
    head_b,
    head_c,
    label_a,
    label_b,
    label_c,
    drop_bits,
):
    images, _, channels = features.shape
    inner = w_reduce.shape[2]
    blocks = w_reduce.shape[0]
    sh = Shape(images)

    gather = functools.partial(lax.all_gather, axis_name="fsdp", axis=0, tiled=True)
    weights = [
        (
            gather(w_reduce[b]),
            None if b == 0 and owners == 8 and dp == 4 else gather(w_spatial[b]),
            gather(w_expand[b]),
        )
        for b in range(blocks)
    ]
    sizes = [head.shape[1] for head in (head_a, head_b, head_c)]
    spans = [-(-size // 16) * 16 for size in sizes]
    lanes = [-(-size // 128) * 128 for size in sizes]
    offsets = [0, lanes[0], lanes[0] + lanes[1]]
    head_t = jnp.concatenate(
        [
            jnp.pad(head.T, ((0, span - size), (0, 0)))
            for head, size, span in zip((head_a, head_b, head_c), sizes, spans)
        ],
        axis=0,
    )
    head_all = lax.all_gather(head_t, "fsdp", axis=1, tiled=True)

    steps = jnp.arange(SIDE + 1, dtype=jnp.int32)
    bound = grid_size
    row_ok = steps[:SIDE, None, None] < bound[None, None, :]
    col_ok = steps[None, :, None] < bound[None, None, :]
    alive = (row_ok & col_ok).astype(F32)
    mask = jnp.concatenate(
        [
            alive[:, :SIDE, : sh.main].reshape(SIDE, sh.top),
            alive[:, :, sh.main :].reshape(SIDE, sh.low),
        ],
        axis=1,
    ).reshape(sh.total, 1)
    pixel_area = (grid_size * grid_size).astype(F32)
    area = jnp.pad(pixel_area, (0, sh.padded - images), constant_values=1.0)[:, None]
    row = jnp.arange(sh.rows, dtype=jnp.int32)
    owner = jnp.where(row < sh.top, row % sh.main, sh.main + (row - sh.top) % sh.rest)
    pick = (owner[None, :] == jnp.arange(sh.padded, dtype=jnp.int32)[:, None]).astype(BF)
    labels = jnp.pad(jnp.stack([label_a, label_b, label_c], axis=1), ((0, sh.padded - images), (0, 0)))
    bits = jnp.pad(drop_bits, ((0, sh.padded - images), (0, 0)))
    gb_mid = jnp.stack([gain_mid, bias_mid], axis=2)
    gb_out = jnp.stack([gain_out, bias_out], axis=1)

    x = prep(sh, jnp.transpose(features, (1, 0, 2)), mask)
    saved = []

    def in_order(*values):
        return lax.optimization_barrier(values)

    place = jnp.stack([lax.axis_index("dp"), lax.axis_index("fsdp")]).astype(jnp.int32).reshape(1, 2)
    short = owners == 8 and dp == 4
    w1 = weights[0][0]
    if short:
        width = inner // dp
        quarter = lax.dynamic_slice_in_dim(w_spatial[0], place[0, 0] * width, width, 1)
        x, *column = in_order(x, *flips(quarter, "fsdp", owners, 2))
        column = jnp.stack(column)
        own = jnp.stack(flips(column, "dp", dp, 1))
        w1, own = in_order(w1, own)
        mate = lax.ppermute(own, "fsdp", [(i, i ^ 1) for i in range(owners)])
    h1, part = reduce_conv(sh, x, w1)
    if short:
        part, mate = in_order(part, mate)
    count = jnp.broadcast_to(jnp.sum(pixel_area), (2, inner))
    both = total_of(jnp.concatenate([part, count], axis=0), (dp, owners))
    if short:
        both, first_spatial = in_order(both, assemble(place, own, mate))
        weights[0] = (weights[0][0], first_spatial, weights[0][2])
    tot1, live_count = both[:2], both[2, 0]
    inv = (1.0 / live_count).reshape(1, 1)
    for b in range(blocks):
        w1, w2, w3 = weights[b]
        act1, h2, part = spatial_conv(sh, h1, tot1, inv, gb_mid[b, 0], mask, w2)
        tot2 = total_of(part, (dp, owners))
        act2, h3, part = expand_conv(sh, h2, tot2, inv, gb_mid[b, 1], mask, w3)
        tot3 = total_of(part, (dp, owners))
        saved.append((x, h1, tot1, act1, h2, tot2, act2, h3, tot3))
        if b + 1 < blocks:
            x, h1, part = join(sh, h3, x, tot3, inv, gb_out[b], mask, weights[b + 1][0])
            tot1 = total_of(part, (dp, owners))
    trunk, pooled = last_join(sh, h3, x, tot3, inv, gb_out[-1], mask, area, pick)
    merged, grad_logits = heads(
        pooled, labels, area, bits, head_all, sizes, offsets, sum(lanes)
    )

    mine = lax.all_to_all(
        pooled.reshape(sh.padded, owners, channels // owners).transpose(1, 0, 2),
        "fsdp",
        0,
        0,
        tiled=True,
    ).reshape(owners * sh.padded, channels // owners)
    all_logits = gather(grad_logits)

    def in_order(*values):
        return lax.optimization_barrier(values)

    e3, part = top_grad(sh, merged, h3, x, tot3, inv, gb_out[-1], mask)
    part, mine = in_order(part, mine)
    btot3 = total_of(part, (dp, owners))
    scatter = functools.partial(lax.psum_scatter, axis_name="fsdp", scatter_dimension=0, tiled=True)
    shards, swaps = {}, {}
    sums_mid, sums_out = [], []
    for b in reversed(range(blocks)):
        w1, w2, w3 = weights[b]
        x, h1, tot1, act1, h2, tot2, act2, h3, tot3 = saved[b]
        g3, e2, part = expand_back(
            sh, e3, h3, tot3, gb_out[b], btot3, inv, mask, w3, h2, tot2, gb_mid[b, 1]
        )
        grad = wgrad(act2, g3, inner)
        if short and b + 1 < blocks:
            terms = swaps[b + 1]
            part, *got = in_order(part, *swap_rest(terms, "dp", dp, 1))
            total = added(terms[0], *got)
            swaps[b + 1] = [total[k] for k in range(owners // 2)]
        btot2 = total_of(part, (dp, owners))
        btot2, grad = in_order(btot2, grad)
        shards["expand", b] = scatter(grad)
        if b + 1 == blocks:
            head_grad = tn(all_logits, mine).astype(BF)
        g2, e1, part = spatial_back(
            sh, e2, h2, tot2, gb_mid[b, 1], btot2, inv, mask, w2, h1, tot1, gb_mid[b, 0]
        )
        grad = spatial_wgrad(sh, act1, g2, place, owners, dp, short)
        if short and b + 1 < blocks:
            part, *chips = in_order(part, *swap_rest(swaps[b + 1], "fsdp", owners, 2))
        if b == 0:
            early = [head_grad] + [shards["reduce", k] for k in range(1, blocks)]
            early += [shards["expand", k] for k in range(1, blocks)]
            halves = copies_halves(early)
            part, *swapped = in_order(part, *copies_swap(halves, dp, 0))
            halves = copies_add(halves, swapped)
            swapped = copies_swap(halves, dp, 1)
        btot1 = total_of(part, (dp, owners))
        if b == 0:
            btot1, *swapped = in_order(btot1, *swapped)
        btot1, *grad = in_order(btot1, *grad)
        if short:
            other = swap_core(grad, owners)
        else:
            shards["spatial", b] = scatter(grad[0])
        sums_out.insert(0, (btot3, tot3))
        sums_mid.insert(0, ((btot1, tot1), (btot2, tot2)))
        if b > 0:
            xp, _, _, _, _, _, _, h3p, tot3p = saved[b - 1]
            g1, e3, part = reduce_back(
                sh, e1, h1, tot1, gb_mid[b, 0], btot1, inv, mask, w1, e3, h3p, xp, tot3p, gb_out[b - 1]
            )
            if short:
                part, other = in_order(part, other)
                swaps[b] = [added(grad[0][j], other[j]) for j in range(dp)]
            grad = wgrad(x, g1, inner)
            btot3 = total_of(part, (dp, owners), True)
            btot3, grad = in_order(btot3, grad)
            shards["reduce", b] = scatter(grad)
        else:
            if short:
                swaps[b] = [added(grad[0][j], other[j]) for j in range(dp)]
                e1, *swaps[b] = in_order(e1, *swaps[b])
                got = swap_rest(swaps[b], "dp", dp, 1)
            else:
                got = [shards["spatial", k] for k in range(blocks)]
            grad = reduce_wgrad(sh, e1, h1, tot1, gb_mid[b, 0], btot1, inv, mask, x)
            if short:
                grad, *got[:2] = in_order(grad, *got[:2])
            expand_halves = copies_halves([shards["expand", b]])
            grad, *other = in_order(grad, *copies_swap(expand_halves, dp, 0))
            expand_halves = copies_add(expand_halves, other)
            e3, grad = in_order(e3, grad)
            shards["reduce", b] = scatter(grad)
            grad_features = features_back(
                sh, e1, h1, tot1, gb_mid[b, 0], btot1, inv, mask, w1, e3
            )
            grad_features, *rest = in_order(
                grad_features, *swapped, *got, *(chips if short else [])
            )
            grad_features, shards["reduce", b] = in_order(grad_features, shards["reduce", b])
            swapped = rest[:2]
            got, chips = rest[2 : 2 + len(got)], rest[2 + len(got) :]

    if short:
        total = added(swaps[0][0], *got)
        total = [total[k] for k in range(owners // 2)]
        late_halves = copies_halves([shards["reduce", 0]])
        steps = in_order(*swap_rest(total, "fsdp", owners, 2), *copies_swap(late_halves, dp, 0), *swapped)
        shards["spatial", 0] = added(total[0], *steps[:-4])
        late_halves, swapped = copies_add(late_halves, steps[-4:-2]), steps[-2:]
        shards["spatial", 1] = added(swaps[1][0], *chips)
        flat = jnp.stack([shards["spatial", b] for b in range(blocks)])
        flat = jnp.broadcast_to(flat[None], (dp,) + flat.shape)
        flat = lax.all_to_all(flat, "dp", 0, 0, tiled=True)
        spatial = jnp.transpose(flat, (1, 2, 0, 3)).reshape(w_spatial.shape).astype(F32) / SCALE
    halves = copies_add(halves, swapped)
    sums = copies_out(halves, early)
    late = [shards["reduce", 0]] + ([] if short else got)
    if short:
        lates = copies_out(copies_sum(late_halves, dp, 1), late)
    else:
        lates = copies_out(copies_sum(copies_halves(late), dp), late)
    expand_sum = copies_out(copies_sum(expand_halves, dp, 1), [shards["expand", 0]])
    head_grad = sums[0]
    reduce_all = jnp.stack([lates[0]] + sums[1:blocks])
    expand_all = jnp.stack(expand_sum + sums[blocks:])
    if not short:
        spatial = jnp.stack(lates[1:])
    at = [(place, size) for place, size in zip(offsets, sizes)]

    def gains(pair):
        btot, tot = pair
        mu = tot[0] / live_count
        var = jnp.maximum(tot[1] / live_count - mu * mu, 0.0)
        return (btot[1] - mu * btot[0]) * lax.rsqrt(var + EPS) / SCALE

    return (
        jnp.transpose(trunk, (1, 0, 2)),
        jnp.transpose(grad_features, (1, 0, 2)),
        reduce_all,
        spatial,
        expand_all,
        jnp.stack([jnp.stack([gains(p) for p in pairs]) for pairs in sums_mid]),
        jnp.stack([jnp.stack([p[0][0] / SCALE for p in pairs]) for pairs in sums_mid]),
        jnp.stack([gains(p) for p in sums_out]),
        jnp.stack([p[0][0] / SCALE for p in sums_out]),
    ) + tuple(head_grad[place : place + size].T for place, size in at)


def solution(mesh):
    split = P(AXES)
    rows = P(None, "fsdp", None)
    head = P("fsdp", None)
    in_specs = (
        P(AXES, None, None), split, rows, rows, rows, P(), P(), P(), P(),
        head, head, head, split, split, split, P(AXES, None),
    )
    out_specs = (
        P(AXES, None, None), P(AXES, None, None), rows, rows, rows, P(), P(), P(), P(), head, head, head,
    )
    body = functools.partial(on_device, mesh.shape["dp"], mesh.shape["fsdp"])
    return jax.shard_map(body, mesh=mesh, in_specs=in_specs, out_specs=out_specs, check_vma=False)
```
